256 devices in a mesh: section: 8 (over y, z_lo), replica: 32 (over z_hi, x, core).
Axes of the slice: x: 4, y: 4, z: 8 (z_hi: 4, z_lo: 2; z = z_hi * 2 + z_lo), core: 2. Of those that a mesh axis runs over, the one named last changes fastest.
Arguments:
- section_inputs: bfloat16 [8, 11264, 1280], P('section', 'replica'), may hold values from -6 to 6
- in_weight: bfloat16 [8, 1280, 2560], P('section', 'replica'), may hold values from -0.15625 to 0.15625
- out_weight: bfloat16 [8, 2560, 1280], P('section', 'replica'), may hold values from -0.125 to 0.125
- projection: bfloat16 [1280, 512], replicated, may hold values from -0.15625 to 0.15625
- text_embed: bfloat16 [256, 512], P('replica'), may hold values from -6 to 6
- pair_label: int32 [128, 2], P('replica'), may hold values from 0 to 1, each once within a row
- pool_group: int32 [32], replicated, may hold values from 0 to 7
Outputs:
- input_grad: bfloat16 [8, 11264, 1280], P('section', 'replica')
- in_weight_grad: float32 [8, 1280, 2560], P('section', 'replica')
- out_weight_grad: float32 [8, 2560, 1280], P('section', 'replica')
The draws below stay inside these ranges and needn't reach their ends.
Inputs may be any that keep to these rules, and one draw needn't show every extreme that they name: Each row of pair_label is a permutation of the 2 slots.
All inputs are finite; a program needn't handle non-finite values.
Results may differ from the reference program's by a relative error of at most 0.04.
Values may be sent and summed in bfloat16 or wider, within the bound.
No kernel may reach another device: no remote copies, remote signals or barrier semaphores. Data moves between devices by JAX's collectives and lax.ppermute only.
A program may use at most 128 MiB of HBM per device.

```python
import jax
import jax.numpy as jnp
from jax import lax

D = 1280
F = 2560
E = 512
MICRO = 4
CLIPS = 2
FRAMES = 44
GROUPS = 8
SECTIONS = 8
REPLICAS = 32
ROWS = 11264


def touch_ends(values, key, least, largest):
    place = [jax.random.randint(jax.random.fold_in(key, axis), (), 0, length) for axis, length in enumerate(values.shape)]
    main_axis = values.shape.index(max(values.shape))
    next_to = place[:main_axis] + [(place[main_axis] + 1) % values.shape[main_axis]] + place[main_axis + 1:]
    return values.at[tuple(place)].set(least).at[tuple(next_to)].set(largest)


def spiked(values, key, source, target, parts, factor):
    owner, partner = [(jnp.arange(values.shape[axis_at]) // (values.shape[axis_at] // parts)).reshape([-1 if axis == axis_at else 1 for axis in range(values.ndim)]) for axis_at in (source, target)]
    chosen = jax.random.permutation(key, parts)[partner]
    strong = (owner == chosen) | (owner == (partner + parts // 2) % parts)
    return jnp.where(strong, factor * values, values)


def level_of(own_key, shape, split, smallest, largest):
    level, own = 1.0, jax.random.fold_in(own_key, 6)
    for dim, parts in split:
        draws = jnp.exp(jax.random.uniform(jax.random.fold_in(own, dim), (parts,), jnp.float32, smallest / len(split), largest / len(split)))
        level = level * jnp.repeat(draws, shape[dim] // parts).reshape([-1 if axis == dim else 1 for axis in range(len(shape))])
    return level


def scatter_about(stream_key, shape, scale, most, shards=(), held_as=jnp.bfloat16):
    array = jax.random.normal(stream_key, shape, jnp.float32) * scale
    if len(shards) > 0:
        array = level_of(stream_key, shape, shards, -0.22, 0.18) * array
    return jnp.clip(array, min=-most, max=most).astype(held_as)


def bell_draw_with(rng, dims, scale, most, cuts, heavy, kind=jnp.bfloat16):
    values = scale * jax.random.normal(rng, dims, jnp.float32)
    if cuts:
        values = values * level_of(rng, dims, cuts, -0.22, 0.18)
    return jnp.clip(spiked(values, jax.random.fold_in(rng, 3), *heavy), -most, most).astype(kind)


def setup_inputs(seed: int = 0) -> dict:
    keys = jax.random.split(jax.random.key(seed), 8)
    section_inputs = bell_draw_with(keys[0], (SECTIONS, ROWS, D), 1.0, 6.0, ((0, 8), (1, 32)), (1, 2, 32, 2.75))
    in_weight = scatter_about(keys[1], (SECTIONS, D, F), D ** -0.5, 0.15625, ((0, 8), (1, 32)))
    out_weight = scatter_about(keys[2], (SECTIONS, F, D), F ** -0.5, 0.125, ((0, 8), (1, 32)))
    projection = scatter_about(keys[3], (D, E), D ** -0.5, 0.15625)
    text_embed = scatter_about(keys[4], (REPLICAS * MICRO * CLIPS, E), 1.0, 6.0, ((0, 32),))
    pair_label = jax.vmap(lambda own: jax.random.permutation(own, CLIPS))(jax.random.split(keys[5], (REPLICAS * MICRO))).reshape((REPLICAS * MICRO, CLIPS)).astype(jnp.int32)
    pool_group = touch_ends(jax.random.randint(keys[6], (REPLICAS,), 0, GROUPS), jax.random.fold_in(keys[6], 1), 0, GROUPS - 1).astype(jnp.int32)
    return dict(section_inputs=section_inputs, in_weight=in_weight, out_weight=out_weight, projection=projection, text_embed=text_embed, pair_label=pair_label, pool_group=pool_group)


eps_norm = 1e-05
eps_unit = 1e-06
inv_temp = 1.0 / 0.07
grad_scale = 256.0
sqrt_half = 0.7071067811865476
inv_sqrt_two_pi = 0.3989422804014327

def layer_norm(values):
    average = lax.optimization_barrier(jnp.mean(values, axis=-1, keepdims=True))
    centred = values - average
    inv_std = lax.rsqrt(lax.optimization_barrier(jnp.mean(centred * centred, axis=-1, keepdims=True)) + eps_norm)
    return (centred * inv_std, inv_std)

def norm_backward(upstream, centred, inv_std):
    first = lax.optimization_barrier(jnp.mean(upstream, axis=-1, keepdims=True))
    second = lax.optimization_barrier(jnp.mean(upstream * centred, axis=-1, keepdims=True))
    return inv_std * (upstream - first - centred * second)

def gelu_exact(values):
    return 0.5 * values * (1.0 + lax.erf(values * sqrt_half))

def gelu_slope(values):
    return 0.5 * (1.0 + lax.erf(values * sqrt_half)) + values * jnp.exp(-0.5 * values * values) * inv_sqrt_two_pi

def block_front(inputs, first_weight):
    centred, inv_std = layer_norm(inputs.astype(jnp.float32))
    normed = centred.astype(jnp.bfloat16)
    preact = jnp.dot(normed, first_weight, preferred_element_type=jnp.float32)
    hidden = gelu_exact(preact).astype(jnp.bfloat16)
    return (normed, preact, hidden)

def block_output(inputs, hidden, second_weight):
    return inputs.astype(jnp.float32) + jnp.dot(hidden, second_weight, preferred_element_type=jnp.float32)

def block_backward(out_grad, inputs, preact, first_weight, second_weight):
    act_grad = lax.dot_general(out_grad, second_weight, (((1,), (1,)), ((), ())), preferred_element_type=jnp.float32)
    pre_grad = (act_grad * gelu_slope(preact)).astype(jnp.bfloat16)
    normed_grad = lax.dot_general(pre_grad, first_weight, (((1,), (1,)), ((), ())), preferred_element_type=jnp.float32)
    centred, inv_std = layer_norm(inputs.astype(jnp.float32))
    in_grad = (out_grad.astype(jnp.float32) + norm_backward(normed_grad, centred, inv_std)).astype(jnp.bfloat16)
    return (in_grad, pre_grad)

def audio_embed(block_out, projection, frames):
    centred, inv_std = layer_norm(block_out)
    width = centred.shape[1]
    pooled = lax.optimization_barrier(jnp.mean(centred.reshape(-1, frames, width), axis=1)).astype(jnp.bfloat16)
    embedded = jnp.dot(pooled, projection, preferred_element_type=jnp.float32)
    inv_norm = lax.rsqrt(lax.optimization_barrier(jnp.sum(embedded * embedded, axis=-1, keepdims=True)) + eps_unit)
    return (embedded * inv_norm, inv_norm, centred, inv_std)

def embed_backward(audio_grad, audio_unit, inv_norm, projection, centred, inv_std, frames):
    emb_grad = (audio_grad - audio_unit * lax.optimization_barrier(jnp.sum(audio_unit * audio_grad, axis=-1, keepdims=True))) * inv_norm
    pooled_grad = jnp.dot(emb_grad, projection.astype(jnp.float32).T, precision=lax.Precision.HIGHEST)
    row_grad = jnp.repeat(pooled_grad / frames, frames, axis=0)
    return norm_backward(row_grad, centred, inv_std).astype(jnp.bfloat16)

def paired_texts(text_embed, pair_label):
    texts = text_embed.astype(jnp.float32)
    unit_text = texts * lax.rsqrt(lax.optimization_barrier(jnp.sum(texts * texts, axis=-1, keepdims=True)) + eps_unit)
    slots = pair_label.shape[1]
    unit_text = unit_text.reshape(-1, slots, unit_text.shape[1])
    chooser = (pair_label[:, :, None] == jnp.arange(slots, dtype=jnp.int32)[None, None, :]).astype(jnp.float32)
    chosen = jnp.einsum('mcj,mje->mce', chooser, unit_text, precision=lax.Precision.HIGHEST)
    return chosen.reshape(-1, chosen.shape[2])

def pair_weights(audio_all, text_all, groups):
    scores = jnp.dot(audio_all, text_all.T, precision=lax.Precision.HIGHEST) * inv_temp
    same_group = (groups[:, None] == groups[None, :]).astype(jnp.float32)
    weighted = same_group * jnp.exp(scores)
    by_rows = weighted / lax.optimization_barrier(jnp.sum(weighted, axis=1, keepdims=True))
    by_cols = weighted / lax.optimization_barrier(jnp.sum(weighted, axis=0, keepdims=True))
    return by_rows + by_cols

def replica_sum(left_rows, right_rows):
    left_all = left_rows.astype(jnp.float32).reshape(REPLICAS, -1, left_rows.shape[1])
    right_all = right_rows.astype(jnp.float32).reshape(REPLICAS, -1, right_rows.shape[1])
    terms = jnp.einsum('rkd,rkf->rdf', left_all, right_all, precision=lax.Precision.HIGHEST)
    rounded = lax.optimization_barrier(terms.astype(jnp.bfloat16))
    return lax.optimization_barrier(jnp.sum(rounded.astype(jnp.float32), axis=0)) / REPLICAS

def reference(section_inputs, in_weight, out_weight, projection, text_embed, pair_label, pool_group):
    in_grads = []
    first_grads = []
    second_grads = []
    out_grad = None
    for section_idx in reversed(range(SECTIONS)):
        inputs = section_inputs[section_idx]
        normed, preact, hidden = block_front(inputs, in_weight[section_idx])
        if section_idx == SECTIONS - 1:
            block_out = block_output(inputs, hidden, out_weight[section_idx])
            audio_unit, inv_norm, centred, inv_std = audio_embed(block_out, projection, FRAMES)
            text_all = paired_texts(text_embed, pair_label)
            groups = jnp.repeat(pool_group, MICRO * CLIPS)
            weights = pair_weights(audio_unit, text_all, groups)
            clip_total = audio_unit.shape[0]
            coeffs = grad_scale * (weights - 2.0 * jnp.eye(clip_total, dtype=jnp.float32))
            audio_grad = jnp.dot(coeffs, text_all, precision=lax.Precision.HIGHEST) * inv_temp
            out_grad = embed_backward(audio_grad, audio_unit, inv_norm, projection, centred, inv_std, FRAMES)
        in_grad, pre_grad = block_backward(out_grad, inputs, preact, in_weight[section_idx], out_weight[section_idx])
        in_grads.append(in_grad)
        first_grads.append(replica_sum(normed, pre_grad))
        second_grads.append(replica_sum(hidden, out_grad))
        out_grad = in_grad
    return (jnp.stack(in_grads[::-1]), jnp.stack(first_grads[::-1]), jnp.stack(second_grads[::-1]))
```

```python
import jax
import jax.numpy as jnp
from jax import lax
from jax.sharding import PartitionSpec as P

MICRO = 4
FRAMES = 44

HI = 4
COL = 4
CORE = 2

eps_norm = 1e-05
eps_unit = 1e-06
inv_temp = 1.0 / 0.07
grad_scale = 256.0
sqrt_half = 0.7071067811865476
inv_sqrt_two_pi = 0.3989422804014327


def replica_of(hi, col, core):
    return ((hi % HI) * COL + col % COL) * CORE + core % CORE


def move(block, hi=0, col=0, core=0):
    route = [
        (replica_of(h, c, k), replica_of(h + hi, c + col, k + core))
        for h in range(HI)
        for c in range(COL)
        for k in range(CORE)
    ]
    return lax.ppermute(block, "replica", route)


def place():
    replica = lax.axis_index("replica")
    return replica // (COL * CORE), (replica // CORE) % COL, replica % CORE


def in_order(own, from_back, axis_size, position):
    ring = [from_back[2], from_back[1], from_back[0], own]
    ring = jnp.stack(ring + ring[:3])
    return lax.dynamic_slice_in_dim(ring, axis_size - 1 - position, axis_size, 0)


def gather_hi(shard):
    hi, _, _ = place()
    return in_order(shard, [move(shard, hi=d) for d in (1, 2, 3)], HI, hi)


def gather_weight(shard):
    _, col, core = place()
    stack = gather_hi(shard)
    left = move(stack, col=1)
    right = move(stack, col=-1)
    far_low = move(left[:2], col=1)
    far_high = move(right[2:], col=-1)
    far = jnp.concatenate([far_low, far_high])
    whole = jnp.zeros((HI, COL, CORE) + shard.shape, shard.dtype)
    for blocks, where in (
        (stack, col),
        (left, (col + COL - 1) % COL),
        (right, (col + 1) % COL),
        (far, (col + 2) % COL),
    ):
        other = move(blocks, core=1)
        for held, side in ((blocks, core), (other, 1 - core)):
            whole = lax.dynamic_update_slice(
                whole, held[:, None, None], (0, where, side, 0, 0)
            )
    return whole.reshape(HI * COL * CORE * shard.shape[0], shard.shape[1])


def gather_small(shard):
    hi, col, core = place()
    other = move(shard, core=1)
    pair = jnp.where(core == 0, jnp.stack([shard, other]), jnp.stack([other, shard]))
    line = in_order(pair, [move(pair, col=d) for d in (1, 2, 3)], COL, col)
    plane = in_order(line, [move(line, hi=d) for d in (1, 2, 3)], HI, hi)
    return plane.reshape(-1, shard.shape[1])


def half_columns(values):
    _, col, _ = place()
    rows, width = values.shape
    part = width // (HI * COL * CORE)
    turned = values.T.reshape(HI, COL, CORE, part, rows)
    turned = turned.transpose(2, 1, 0, 3, 4)
    return lax.dynamic_slice_in_dim(
        jnp.concatenate([turned, turned[:, : COL - 1]], axis=1), col, COL, 1
    )


def chip_columns(values):
    _, _, core = place()
    halves = half_columns(values)
    own = lax.dynamic_index_in_dim(halves, core, 0, keepdims=False)
    given = lax.dynamic_index_in_dim(halves, 1 - core, 0, keepdims=False)
    other = move(given, core=1)
    return jnp.concatenate([own, other], axis=-1)


def chip_rows(values):
    return jnp.concatenate([values, move(values, core=1)], axis=0)


def scatter_sum(left, right):
    hi, _, _ = place()
    part, rows = left.shape[2:]
    width = right.shape[1]

    def term(distance, halves=slice(None)):
        chosen = left[distance, halves]
        product = jnp.dot(
            chosen.reshape(-1, rows), right, preferred_element_type=jnp.float32
        )
        return product.reshape(-1, part, width)

    low, high = slice(0, 2), slice(2, 4)
    far = term(2).astype(jnp.bfloat16)
    far_low = move(far[:2], col=1)
    far_high = move(far[2:], col=-1)
    next_term = term(1)
    back_term = term(3)
    next_high = move(next_term[2:].astype(jnp.bfloat16), col=1)
    back_low = move(back_term[:2].astype(jnp.bfloat16), col=-1)
    next_low = move(
        (next_term[:2] + far_low.astype(jnp.float32)).astype(jnp.bfloat16), col=1
    )
    back_high = move(
        (back_term[2:] + far_high.astype(jnp.float32)).astype(jnp.bfloat16), col=-1
    )
    own = term(0)
    total = jnp.concatenate(
        [
            own[:2] + next_low.astype(jnp.float32) + back_low.astype(jnp.float32),
            own[2:] + next_high.astype(jnp.float32) + back_high.astype(jnp.float32),
        ]
    )
    result = lax.dynamic_index_in_dim(total, hi, 0, keepdims=False)
    rounded = total.astype(jnp.bfloat16)
    for distance in (1, 2, 3):
        given = lax.dynamic_index_in_dim(rounded, (hi + distance) % HI, 0, keepdims=False)
        result = result + move(given, hi=distance).astype(jnp.float32)
    return result / (HI * COL * CORE)


def shifted(block, axis, distance):
    devices = range(lax.axis_size(axis))
    route = [(i - distance, i) for i in devices if i - distance in devices]
    return lax.ppermute(block, axis, route)


def layer_norm(values):
    average = jnp.mean(values, axis=-1, keepdims=True)
    centred = values - average
    inv_std = lax.rsqrt(jnp.mean(centred * centred, axis=-1, keepdims=True) + eps_norm)
    return (centred * inv_std, inv_std)


def norm_backward(upstream, centred, inv_std):
    first = jnp.mean(upstream, axis=-1, keepdims=True)
    second = jnp.mean(upstream * centred, axis=-1, keepdims=True)
    return inv_std * (upstream - first - centred * second)


def gelu_exact(values):
    return 0.5 * values * (1.0 + lax.erf(values * sqrt_half))


def gelu_slope(values):
    return (
        0.5 * (1.0 + lax.erf(values * sqrt_half))
        + values * jnp.exp(-0.5 * values * values) * inv_sqrt_two_pi
    )


def block_front(inputs, first_weight):
    centred, inv_std = layer_norm(inputs.astype(jnp.float32))
    normed = centred.astype(jnp.bfloat16)
    preact = jnp.dot(normed, first_weight, preferred_element_type=jnp.float32)
    hidden = gelu_exact(preact).astype(jnp.bfloat16)
    return (normed, preact, hidden)


def block_output(inputs, hidden, second_weight):
    return inputs.astype(jnp.float32) + jnp.dot(
        hidden, second_weight, preferred_element_type=jnp.float32
    )


def block_backward(out_grad, inputs, preact, first_weight, second_weight):
    act_grad = lax.dot_general(
        out_grad, second_weight, (((1,), (1,)), ((), ())), preferred_element_type=jnp.float32
    )
    pre_grad = (act_grad * gelu_slope(preact)).astype(jnp.bfloat16)
    normed_grad = lax.dot_general(
        pre_grad, first_weight, (((1,), (1,)), ((), ())), preferred_element_type=jnp.float32
    )
    centred, inv_std = layer_norm(inputs.astype(jnp.float32))
    in_grad = (out_grad.astype(jnp.float32) + norm_backward(normed_grad, centred, inv_std)).astype(
        jnp.bfloat16
    )
    return (in_grad, pre_grad)


def audio_embed(block_out, projection, frames):
    centred, inv_std = layer_norm(block_out)
    width = centred.shape[1]
    pooled = jnp.mean(centred.reshape(-1, frames, width), axis=1).astype(jnp.bfloat16)
    embedded = jnp.dot(pooled, projection, preferred_element_type=jnp.float32)
    inv_norm = lax.rsqrt(jnp.sum(embedded * embedded, axis=-1, keepdims=True) + eps_unit)
    return (embedded * inv_norm, inv_norm, centred, inv_std)


def embed_backward(audio_grad, audio_unit, inv_norm, projection, centred, inv_std, frames):
    emb_grad = (
        audio_grad - audio_unit * jnp.sum(audio_unit * audio_grad, axis=-1, keepdims=True)
    ) * inv_norm
    pooled_grad = jnp.dot(
        emb_grad, projection.astype(jnp.float32).T, precision=lax.Precision.HIGHEST
    )
    row_grad = jnp.repeat(pooled_grad / frames, frames, axis=0)
    return norm_backward(row_grad, centred, inv_std).astype(jnp.bfloat16)


def paired_texts(text_embed, pair_label):
    texts = text_embed.astype(jnp.float32)
    unit_text = texts * lax.rsqrt(jnp.sum(texts * texts, axis=-1, keepdims=True) + eps_unit)
    slots = pair_label.shape[1]
    unit_text = unit_text.reshape(-1, slots, unit_text.shape[1])
    chooser = (pair_label[:, :, None] == jnp.arange(slots, dtype=jnp.int32)[None, None, :]).astype(
        jnp.float32
    )
    chosen = jnp.einsum("mcj,mje->mce", chooser, unit_text, precision=lax.Precision.HIGHEST)
    return chosen.reshape(-1, chosen.shape[2])


def pair_weights(audio_all, text_all, groups):
    scores = jnp.dot(audio_all, text_all.T, precision=lax.Precision.HIGHEST) * inv_temp
    same_group = (groups[:, None] == groups[None, :]).astype(jnp.float32)
    weighted = same_group * jnp.exp(scores)
    by_rows = weighted / jnp.sum(weighted, axis=1, keepdims=True)
    by_cols = weighted / jnp.sum(weighted, axis=0, keepdims=True)
    return by_rows + by_cols


def take_micro(stacked, which_micro):
    return lax.dynamic_index_in_dim(stacked, which_micro, 0, keepdims=False)


def store_micro(stacked, update, which_micro):
    return lax.dynamic_update_index_in_dim(stacked, update, which_micro, 0)


def local(section_inputs, in_weight, out_weight, projection, text_embed, pair_label, pool_group):
    inputs = section_inputs[0]
    row_count = inputs.shape[0]
    per_micro = row_count // MICRO
    first_weight = gather_weight(in_weight[0])
    second_weight = gather_weight(out_weight[0])
    local_text = paired_texts(text_embed, pair_label)
    text_all = gather_small(local_text.astype(jnp.bfloat16)).astype(jnp.float32)
    normed, preact, hidden = block_front(inputs, first_weight)
    block_out = block_output(inputs, hidden, second_weight)
    audio_unit, inv_norm, centred, inv_std = audio_embed(block_out, projection, FRAMES)
    audio_all = gather_small(audio_unit.astype(jnp.bfloat16)).astype(jnp.float32)
    clip_count = audio_unit.shape[0]
    first_clip = lax.axis_index("replica") * clip_count
    groups = jnp.repeat(pool_group, clip_count)
    weights = pair_weights(audio_all, text_all, groups)
    own_weights = lax.dynamic_slice_in_dim(weights, first_clip, clip_count, 0)
    targets = (
        jnp.arange(audio_all.shape[0], dtype=jnp.int32)[None, :]
        == first_clip + jnp.arange(clip_count, dtype=jnp.int32)[:, None]
    ).astype(jnp.float32)
    coeffs = grad_scale * (own_weights - 2.0 * targets)
    audio_grad = jnp.dot(coeffs, text_all, precision=lax.Precision.HIGHEST) * inv_temp
    last_grad = embed_backward(
        audio_grad, audio_unit, inv_norm, projection, centred, inv_std, FRAMES
    )
    normed_columns = chip_columns(normed)
    hidden_columns = chip_columns(hidden)
    section_count = lax.axis_size("section")
    section_id = lax.axis_index("section")
    is_last = section_id == section_count - 1
    width = inputs.shape[1]
    inputs_micro = inputs.reshape(MICRO, per_micro, width)
    preact_micro = preact.reshape(MICRO, per_micro, preact.shape[1])
    last_micro = last_grad.reshape(MICRO, per_micro, width)

    def tick(tick_id, state_tuple):
        incoming, grads_out, grads_pre, grads_in = state_tuple
        micro_id = tick_id - (section_count - 1 - section_id)
        active = jnp.logical_and(micro_id >= 0, micro_id < MICRO)
        which_micro = jnp.clip(micro_id, 0, MICRO - 1)

        def run_block(stores):
            upstream = jnp.where(is_last, take_micro(last_micro, which_micro), incoming)
            in_grad, pre_grad = block_backward(
                upstream,
                take_micro(inputs_micro, which_micro),
                take_micro(preact_micro, which_micro),
                first_weight,
                second_weight,
            )
            updated = (
                store_micro(stores[0], upstream, which_micro),
                store_micro(stores[1], pre_grad, which_micro),
                store_micro(stores[2], in_grad, which_micro),
            )
            return (updated, in_grad)

        def skip_block(stores):
            return (stores, jnp.zeros_like(incoming))

        stores, passed = lax.cond(active, run_block, skip_block, (grads_out, grads_pre, grads_in))
        received = shifted(passed, "section", -1)
        return (received, stores[0], stores[1], stores[2])

    initial = (
        jnp.zeros((per_micro, width), jnp.bfloat16),
        jnp.zeros((MICRO, per_micro, width), jnp.bfloat16),
        jnp.zeros((MICRO, per_micro, preact.shape[1]), jnp.bfloat16),
        jnp.zeros((MICRO, per_micro, width), jnp.bfloat16),
    )
    final_state = lax.fori_loop(0, MICRO + section_count - 1, tick, initial)
    out_grads = final_state[1].reshape(row_count, width)
    pre_grads = final_state[2].reshape(row_count, preact.shape[1])
    in_grads = final_state[3].reshape(row_count, width)
    second_sum = scatter_sum(hidden_columns, chip_rows(out_grads))
    first_sum = scatter_sum(normed_columns, chip_rows(pre_grads))
    return (in_grads[None], first_sum[None], second_sum[None])


def solution(mesh):
    return jax.shard_map(
        local,
        mesh=mesh,
        in_specs=(
            P("section", "replica", None),
            P("section", "replica", None),
            P("section", "replica", None),
            P(),
            P("replica", None),
            P("replica", None),
            P(),
        ),
        out_specs=(
            P("section", "replica", None),
            P("section", "replica", None),
            P("section", "replica", None),
        ),
        check_vma=False,
    )
```

```python
import functools

import jax
import jax.numpy as jnp
from jax import lax
from jax.experimental import pallas as pl
from jax.experimental.pallas import tpu as pltpu
from jax.sharding import PartitionSpec as P

MICRO = 4
FRAMES = 44

HI = 4
COL = 4
CORE = 2

eps_norm = 1e-05
eps_unit = 1e-06
inv_temp = 1.0 / 0.07
grad_scale = 256.0
sqrt_half = 0.7071067811865476
inv_sqrt_two_pi = 0.3989422804014327


def replica_of(hi, col, core):
    return ((hi % HI) * COL + col % COL) * CORE + core % CORE


def move(block, hi=0, col=0, core=0):
    route = [
        (replica_of(h, c, k), replica_of(h + hi, c + col, k + core))
        for h in range(HI)
        for c in range(COL)
        for k in range(CORE)
    ]
    return lax.ppermute(block, "replica", route)


def place():
    replica = lax.axis_index("replica")
    return replica // (COL * CORE), (replica // CORE) % COL, replica % CORE


def in_order(own, from_back, axis_size, position):
    ring = [from_back[2], from_back[1], from_back[0], own]
    ring = jnp.stack(ring + ring[:3])
    return lax.dynamic_slice_in_dim(ring, axis_size - 1 - position, axis_size, 0)


def gather_hi(shard):
    hi, _, _ = place()
    return in_order(shard, [move(shard, hi=d) for d in (1, 2, 3)], HI, hi)


def gather_weight(shard):
    _, col, core = place()
    stack = gather_hi(shard)
    left = move(stack, col=1)
    right = move(stack, col=-1)
    far_low = move(left[:2], col=1)
    far_high = move(right[2:], col=-1)
    far = jnp.concatenate([far_low, far_high])
    whole = jnp.zeros((HI, COL, CORE) + shard.shape, shard.dtype)
    for blocks, where in (
        (stack, col),
        (left, (col + COL - 1) % COL),
        (right, (col + 1) % COL),
        (far, (col + 2) % COL),
    ):
        other = move(blocks, core=1)
        for held, side in ((blocks, core), (other, 1 - core)):
            whole = lax.dynamic_update_slice(
                whole, held[:, None, None], (0, where, side, 0, 0)
            )
    return whole.reshape(HI * COL * CORE * shard.shape[0], shard.shape[1])


def gather_small(shard):
    hi, col, core = place()
    other = move(shard, core=1)
    pair = jnp.where(core == 0, jnp.stack([shard, other]), jnp.stack([other, shard]))
    line = in_order(pair, [move(pair, col=d) for d in (1, 2, 3)], COL, col)
    plane = in_order(line, [move(line, hi=d) for d in (1, 2, 3)], HI, hi)
    return plane.reshape(-1, shard.shape[1])


def half_columns(values):
    _, col, _ = place()
    rows, width = values.shape
    part = width // (HI * COL * CORE)
    turned = values.T.reshape(HI, COL, CORE, part, rows)
    turned = turned.transpose(2, 1, 0, 3, 4)
    return lax.dynamic_slice_in_dim(
        jnp.concatenate([turned, turned[:, : COL - 1]], axis=1), col, COL, 1
    )


def chip_columns(values):
    _, _, core = place()
    halves = half_columns(values)
    own = lax.dynamic_index_in_dim(halves, core, 0, keepdims=False)
    given = lax.dynamic_index_in_dim(halves, 1 - core, 0, keepdims=False)
    other = move(given, core=1)
    return jnp.concatenate([own, other], axis=-1)


def chip_rows(values):
    return jnp.concatenate([values, move(values, core=1)], axis=0)


def scatter_sum(left, right):
    hi, _, _ = place()
    part, rows = left.shape[2:]
    width = right.shape[1]

    def term(distance, halves=slice(None)):
        chosen = left[distance, halves]
        product = jnp.dot(
            chosen.reshape(-1, rows), right, preferred_element_type=jnp.float32
        )
        return product.reshape(-1, part, width)

    low, high = slice(0, 2), slice(2, 4)
    far = term(2).astype(jnp.bfloat16)
    far_low = move(far[:2], col=1)
    far_high = move(far[2:], col=-1)
    next_term = term(1)
    back_term = term(3)
    next_high = move(next_term[2:].astype(jnp.bfloat16), col=1)
    back_low = move(back_term[:2].astype(jnp.bfloat16), col=-1)
    next_low = move(
        (next_term[:2] + far_low.astype(jnp.float32)).astype(jnp.bfloat16), col=1
    )
    back_high = move(
        (back_term[2:] + far_high.astype(jnp.float32)).astype(jnp.bfloat16), col=-1
    )
    own = term(0)
    total = jnp.concatenate(
        [
            own[:2] + next_low.astype(jnp.float32) + back_low.astype(jnp.float32),
            own[2:] + next_high.astype(jnp.float32) + back_high.astype(jnp.float32),
        ]
    )
    result = lax.dynamic_index_in_dim(total, hi, 0, keepdims=False)
    rounded = total.astype(jnp.bfloat16)
    for distance in (1, 2, 3):
        given = lax.dynamic_index_in_dim(rounded, (hi + distance) % HI, 0, keepdims=False)
        result = result + move(given, hi=distance).astype(jnp.float32)
    return result / (HI * COL * CORE)


def layer_norm(values):
    average = jnp.mean(values, axis=-1, keepdims=True)
    centred = values - average
    inv_std = lax.rsqrt(jnp.mean(centred * centred, axis=-1, keepdims=True) + eps_norm)
    return (centred * inv_std, inv_std)


def norm_backward(upstream, centred, inv_std):
    first = jnp.mean(upstream, axis=-1, keepdims=True)
    second = jnp.mean(upstream * centred, axis=-1, keepdims=True)
    return inv_std * (upstream - first - centred * second)


def gelu_exact(values):
    return 0.5 * values * (1.0 + lax.erf(values * sqrt_half))


def gelu_slope(values):
    return (
        0.5 * (1.0 + lax.erf(values * sqrt_half))
        + values * jnp.exp(-0.5 * values * values) * inv_sqrt_two_pi
    )


def block_front(inputs, first_weight):
    centred, inv_std = layer_norm(inputs.astype(jnp.float32))
    normed = centred.astype(jnp.bfloat16)
    preact = jnp.dot(normed, first_weight, preferred_element_type=jnp.float32)
    hidden = gelu_exact(preact).astype(jnp.bfloat16)
    return (normed, inv_std, gelu_slope(preact), hidden)


def block_output(inputs, hidden, second_weight):
    return inputs.astype(jnp.float32) + jnp.dot(
        hidden, second_weight, preferred_element_type=jnp.float32
    )


LAST_DIMS = (((1,), (1,)), ((), ()))


def step_kernel(
    from_last,
    info,
    second_ref,
    first_ref,
    slope_ref,
    normed_ref,
    inv_ref,
    *rest,
):
    given, (passed_ref, out_ref, pre_ref, in_ref) = rest[:-7], rest[-4:]

    @pl.when(info[2] == 1)
    def _():
        if from_last == 0:
            upstream = given[0][0]
        elif from_last == 1:
            upstream = jnp.where(info[3] == 1, given[0][0], given[1][...])
        else:
            upstream = given[0][...]
        act_grad = lax.dot_general(
            upstream, second_ref[...], LAST_DIMS, preferred_element_type=jnp.float32
        )
        pre_grad = (act_grad * slope_ref[0]).astype(jnp.bfloat16)
        pre_ref[0] = pre_grad
        out_ref[0] = upstream
        normed_grad = lax.dot_general(
            pre_grad, first_ref[...], LAST_DIMS, preferred_element_type=jnp.float32
        )
        normed = normed_ref[0].astype(jnp.float32)
        mean = jnp.mean(normed_grad, axis=-1, keepdims=True)
        along = jnp.mean(normed_grad * normed, axis=-1, keepdims=True)
        in_grad = upstream.astype(jnp.float32) + inv_ref[0] * (
            normed_grad - mean - normed * along
        )
        in_grad = in_grad.astype(jnp.bfloat16)
        passed_ref[...] = in_grad
        in_ref[0] = in_grad


def chain_step(info, weights, fixed, last_micro, received, stores):
    rows, width = fixed[1].shape[1:]
    wide = fixed[0].shape[2]

    def at_read(n):
        return pl.BlockSpec((1, rows, n), lambda g, i: (i[0], 0, 0))

    def at_store(n):
        return pl.BlockSpec((1, rows, n), lambda g, i: (i[1], 0, 0))

    whole = pl.BlockSpec(memory_space=pltpu.VMEM)
    given, specs = [], []
    if last_micro is not None:
        given.append(last_micro)
        specs.append(at_read(width))
    if received is not None:
        given.append(received)
        specs.append(pl.BlockSpec((rows, width), lambda g, i: (0, 0)))
    from_last = 0 if received is None else (2 if last_micro is None else 1)
    first_store = 1 + 5 + len(given)
    return pl.pallas_call(
        functools.partial(step_kernel, from_last),
        grid_spec=pltpu.PrefetchScalarGridSpec(
            num_scalar_prefetch=1,
            grid=(1,),
            in_specs=[whole, whole, at_read(wide), at_read(width), at_read(1)]
            + specs
            + [pl.BlockSpec(memory_space=pl.ANY)] * 3,
            out_specs=[
                pl.BlockSpec((rows, width), lambda g, i: (0, 0)),
                at_store(width),
                at_store(wide),
                at_store(width),
            ],
        ),
        out_shape=[jax.ShapeDtypeStruct((rows, width), jnp.bfloat16)]
        + [jax.ShapeDtypeStruct(a.shape, a.dtype) for a in stores],
        input_output_aliases={first_store + i: 1 + i for i in range(3)},
        compiler_params=pltpu.CompilerParams(vmem_limit_bytes=20 * 2**20),
        cost_estimate=pl.CostEstimate(
            flops=4 * rows * width * wide, bytes_accessed=4 * width * wide, transcendentals=0
        ),
        name="chain_step",
    )(
        info,
        *[pltpu.with_memory_space_constraint(w, pltpu.VMEM) for w in weights],
        *fixed,
        *given,
        *stores,
    )


def audio_embed(block_out, projection, frames):
    centred, inv_std = layer_norm(block_out)
    width = centred.shape[1]
    pooled = jnp.mean(centred.reshape(-1, frames, width), axis=1).astype(jnp.bfloat16)
    embedded = jnp.dot(pooled, projection, preferred_element_type=jnp.float32)
    inv_norm = lax.rsqrt(jnp.sum(embedded * embedded, axis=-1, keepdims=True) + eps_unit)
    return (embedded * inv_norm, inv_norm, centred, inv_std)


def embed_backward(audio_grad, audio_unit, inv_norm, projection, centred, inv_std, frames):
    emb_grad = (
        audio_grad - audio_unit * jnp.sum(audio_unit * audio_grad, axis=-1, keepdims=True)
    ) * inv_norm
    pooled_grad = jnp.dot(
        emb_grad, projection.astype(jnp.float32).T, precision=lax.Precision.HIGHEST
    )
    row_grad = jnp.repeat(pooled_grad / frames, frames, axis=0)
    return norm_backward(row_grad, centred, inv_std).astype(jnp.bfloat16)


def paired_texts(text_embed, pair_label):
    texts = text_embed.astype(jnp.float32)
    unit_text = texts * lax.rsqrt(jnp.sum(texts * texts, axis=-1, keepdims=True) + eps_unit)
    slots = pair_label.shape[1]
    unit_text = unit_text.reshape(-1, slots, unit_text.shape[1])
    chooser = (pair_label[:, :, None] == jnp.arange(slots, dtype=jnp.int32)[None, None, :]).astype(
        jnp.float32
    )
    chosen = jnp.einsum("mcj,mje->mce", chooser, unit_text, precision=lax.Precision.HIGHEST)
    return chosen.reshape(-1, chosen.shape[2])


def pair_weights(audio_all, text_all, groups):
    scores = jnp.dot(audio_all, text_all.T, precision=lax.Precision.HIGHEST) * inv_temp
    same_group = (groups[:, None] == groups[None, :]).astype(jnp.float32)
    weighted = same_group * jnp.exp(scores)
    by_rows = weighted / jnp.sum(weighted, axis=1, keepdims=True)
    by_cols = weighted / jnp.sum(weighted, axis=0, keepdims=True)
    return by_rows + by_cols


def local(section_inputs, in_weight, out_weight, projection, text_embed, pair_label, pool_group):
    inputs = section_inputs[0]
    row_count = inputs.shape[0]
    per_micro = row_count // MICRO
    first_weight = gather_weight(in_weight[0])
    second_weight = gather_weight(out_weight[0])
    local_text = paired_texts(text_embed, pair_label)
    text_all = gather_small(local_text.astype(jnp.bfloat16)).astype(jnp.float32)
    normed, inv_std_in, slope, hidden = block_front(inputs, first_weight)
    block_out = block_output(inputs, hidden, second_weight)
    audio_unit, inv_norm, centred, inv_std = audio_embed(block_out, projection, FRAMES)
    audio_all = gather_small(audio_unit.astype(jnp.bfloat16)).astype(jnp.float32)
    clip_count = audio_unit.shape[0]
    first_clip = lax.axis_index("replica") * clip_count
    groups = jnp.repeat(pool_group, clip_count)
    weights = pair_weights(audio_all, text_all, groups)
    own_weights = lax.dynamic_slice_in_dim(weights, first_clip, clip_count, 0)
    targets = (
        jnp.arange(audio_all.shape[0], dtype=jnp.int32)[None, :]
        == first_clip + jnp.arange(clip_count, dtype=jnp.int32)[:, None]
    ).astype(jnp.float32)
    coeffs = grad_scale * (own_weights - 2.0 * targets)
    audio_grad = jnp.dot(coeffs, text_all, precision=lax.Precision.HIGHEST) * inv_temp
    last_grad = embed_backward(
        audio_grad, audio_unit, inv_norm, projection, centred, inv_std, FRAMES
    )
    normed_columns = chip_columns(normed)
    hidden_columns = chip_columns(hidden)
    section_count = lax.axis_size("section")
    section_id = lax.axis_index("section")
    is_last = section_id == section_count - 1
    width = inputs.shape[1]
    wide = slope.shape[1]
    fixed = (
        slope.reshape(MICRO, per_micro, wide),
        normed.reshape(MICRO, per_micro, width),
        inv_std_in.reshape(MICRO, per_micro, 1),
    )
    last_micro = last_grad.reshape(MICRO, per_micro, width)
    weights = (second_weight, first_weight)
    stores = [
        jnp.zeros((MICRO + 1, per_micro, n), jnp.bfloat16) for n in (width, wide, width)
    ]
    arrived = [None, None]
    for slot in range(2 * (section_count - 1) + MICRO):
        micro_id = slot - 2 * (section_count - 1 - section_id)
        active = jnp.logical_and(micro_id >= 0, micro_id < MICRO)
        info = jnp.stack(
            [
                jnp.clip(micro_id, 0, MICRO - 1),
                jnp.where(active, micro_id, MICRO),
                active.astype(jnp.int32),
                is_last.astype(jnp.int32),
            ]
        ).astype(jnp.int32)
        received = arrived[slot]
        passed, *stores = chain_step(
            info, weights, fixed, last_micro if slot < MICRO else None, received, stores
        )
        route = [
            (s, s - 1)
            for s in range(1, section_count)
            if 0 <= slot - 2 * (section_count - 1 - s) < MICRO
        ]
        arrived.append(lax.ppermute(passed, "section", route) if route else None)
    out_grads, pre_grads, in_grads = (
        a[:MICRO].reshape(row_count, a.shape[2]) for a in stores
    )
    second_sum = scatter_sum(hidden_columns, chip_rows(out_grads))
    first_sum = scatter_sum(normed_columns, chip_rows(pre_grads))
    return (in_grads[None], first_sum[None], second_sum[None])


def solution(mesh):
    return jax.shard_map(
        local,
        mesh=mesh,
        in_specs=(
            P("section", "replica", None),
            P("section", "replica", None),
            P("section", "replica", None),
            P(),
            P("replica", None),
            P("replica", None),
            P(),
        ),
        out_specs=(
            P("section", "replica", None),
            P("section", "replica", None),
            P("section", "replica", None),
        ),
        check_vma=False,
    )
```

```python
import functools

import jax
import jax.numpy as jnp
from jax import lax
from jax.experimental import pallas as pl
from jax.experimental.pallas import tpu as pltpu
from jax.sharding import PartitionSpec as P

MICRO = 4
FRAMES = 44

HI = 4
COL = 4
CORE = 2

MIB = 2**20
LAST_DIMS = (((1,), (1,)), ((), ()))
EXACT = lax.Precision.HIGHEST

eps_norm = 1e-05
eps_unit = 1e-06
inv_temp = 1.0 / 0.07
grad_scale = 256.0
sqrt_half = 0.7071067811865476
inv_sqrt_two_pi = 0.3989422804014327

bf16 = jnp.bfloat16
f32 = jnp.float32


def replica_of(hi, col, core):
    return ((hi % HI) * COL + col % COL) * CORE + core % CORE


def move(block, hi=0, col=0, core=0):
    route = [
        (replica_of(h, c, k), replica_of(h + hi, c + col, k + core))
        for h in range(HI)
        for c in range(COL)
        for k in range(CORE)
    ]
    return lax.ppermute(block, "replica", route)


def place():
    replica = lax.axis_index("replica")
    return replica // (COL * CORE), (replica // CORE) % COL, replica % CORE


def after(value, *others):
    return lax.optimization_barrier((value, *others))[0]


def in_order(own, from_back, axis_size, position):
    ring = [from_back[2], from_back[1], from_back[0], own]
    ring = jnp.stack(ring + ring[:3])
    return lax.dynamic_slice_in_dim(ring, axis_size - 1 - position, axis_size, 0)


def in_vmem(value):
    return pltpu.with_memory_space_constraint(value, pltpu.VMEM)


VMEM_SPEC = pl.BlockSpec(memory_space=pltpu.VMEM)
ANY_SPEC = pl.BlockSpec(memory_space=pl.ANY)
SMEM_SPEC = pl.BlockSpec(memory_space=pltpu.SMEM)


def place_kernel(plan, by_columns, info, *refs):
    pieces = refs[: len(plan)]
    whole, sems = refs[-2], refs[-1]
    col, core = info[0], info[1]
    copies = []
    for (first_hi, distance, other), piece in zip(plan, pieces):
        count, rows, width = piece.shape
        at_col = lax.rem(col + distance, COL)
        side = 1 - core if other else core
        for k in range(count):
            chip = (first_hi + k) * COL + at_col
            if by_columns:
                row = chip * rows
                column = pl.ds(pl.multiple_of(side * width, 128), width)
            else:
                row = (chip * CORE + side) * rows
                column = slice(None)
            copy = pltpu.make_async_copy(
                piece.at[k],
                whole.at[pl.ds(pl.multiple_of(row, 16), rows), column],
                sems.at[len(copies)],
            )
            copy.start()
            copies.append(copy)
    for copy in copies:
        copy.wait()


def place_blocks(info, plan, pieces, shape, by_columns, whole=None):
    count = sum(p.shape[0] for p in pieces)
    return pl.pallas_call(
        functools.partial(place_kernel, plan, by_columns),
        in_specs=[SMEM_SPEC]
        + [ANY_SPEC] * len(pieces)
        + ([] if whole is None else [VMEM_SPEC]),
        out_specs=VMEM_SPEC,
        out_shape=pltpu.VMEM(shape, bf16),
        scratch_shapes=[pltpu.SemaphoreType.DMA((count,))],
        input_output_aliases={} if whole is None else {1 + len(pieces): 0},
        compiler_params=pltpu.CompilerParams(vmem_limit_bytes=8 * MIB),
        name="place_blocks",
    )(info, *pieces, *([] if whole is None else [in_vmem(whole)]))


def start_columns(stack):
    return move(stack, col=1), move(stack, col=-1)


def front_kernel(
    inputs_ref, first_ref, normed_ref, inv_ref, normed_t_ref, hidden_ref, hidden_t_ref, slope_ref
):
    micro, rows = normed_ref.shape[:2]
    values = inputs_ref[...].astype(f32)
    centred = values - jnp.mean(values, axis=-1, keepdims=True)
    inv_std = lax.rsqrt(jnp.mean(centred * centred, axis=-1, keepdims=True) + eps_norm)
    scaled = centred * inv_std
    normed = scaled.astype(bf16)
    for m in range(micro):
        normed_ref[m] = normed[m * rows : (m + 1) * rows]
        inv_ref[m] = inv_std[m * rows : (m + 1) * rows]
    normed_t_ref[...] = scaled.T.astype(bf16)
    step = 256

    @pl.loop(0, first_ref.shape[1] // step)
    def _(j):
        part = pl.ds(pl.multiple_of(j * step, step), step)
        preact = jnp.dot(normed, first_ref[:, part], preferred_element_type=f32)
        cdf = 0.5 * (1.0 + lax.erf(preact * sqrt_half))
        hidden = preact * cdf
        hidden_ref[:, part] = hidden.astype(bf16)
        hidden_t_ref[part, :] = hidden.T.astype(bf16)
        slope = cdf + preact * jnp.exp(-0.5 * preact * preact) * inv_sqrt_two_pi
        for m in range(micro):
            slope_ref[m, :, part] = slope[m * rows : (m + 1) * rows]


def front(inputs, first_weight):
    rows, width = inputs.shape
    wide = first_weight.shape[1]
    per_micro = rows // MICRO
    return pl.pallas_call(
        front_kernel,
        in_specs=[VMEM_SPEC] * 2,
        out_specs=[VMEM_SPEC] * 6,
        out_shape=[
            pltpu.VMEM((MICRO, per_micro, width), bf16),
            pltpu.VMEM((MICRO, per_micro, 1), f32),
            jax.ShapeDtypeStruct((width, rows), bf16),
            jax.ShapeDtypeStruct((rows, wide), bf16),
            jax.ShapeDtypeStruct((wide, rows), bf16),
            pltpu.VMEM((MICRO, per_micro, wide), f32),
        ],
        compiler_params=pltpu.CompilerParams(vmem_limit_bytes=24 * MIB),
        cost_estimate=pl.CostEstimate(
            flops=2 * rows * width * wide, bytes_accessed=4 * MIB, transcendentals=0
        ),
        name="front",
    )(inputs, in_vmem(first_weight))


def clip_rows(rows, clips):
    first = lax.broadcasted_iota(jnp.int32, (clips, rows), 0) * (rows // clips)
    row = lax.broadcasted_iota(jnp.int32, (clips, rows), 1)
    return jnp.where((row >= first) & (row < first + rows // clips), 1.0, 0.0).astype(f32)


def embed_kernel(
    inputs_ref,
    hidden_ref,
    second_ref,
    projection_ref,
    normed_ref,
    inv_ref,
    unit_ref,
    inv_norm_ref,
    sent_ref,
):
    rows = inputs_ref.shape[0]
    clips = unit_ref.shape[0]
    block_out = inputs_ref[...].astype(f32) + jnp.dot(
        hidden_ref[...], second_ref[...], preferred_element_type=f32
    )
    centred = block_out - jnp.mean(block_out, axis=-1, keepdims=True)
    inv_std = lax.rsqrt(jnp.mean(centred * centred, axis=-1, keepdims=True) + eps_norm)
    normed = centred * inv_std
    normed_ref[...] = normed
    inv_ref[...] = inv_std
    sums = jnp.dot(
        clip_rows(rows, clips), normed, precision=EXACT, preferred_element_type=f32
    )
    pooled = (sums * (1.0 / (rows // clips))).astype(bf16)
    embedded = jnp.dot(pooled, projection_ref[...], preferred_element_type=f32)
    inv_norm = lax.rsqrt(jnp.sum(embedded * embedded, axis=-1, keepdims=True) + eps_unit)
    unit = embedded * inv_norm
    unit_ref[...] = unit
    inv_norm_ref[...] = inv_norm
    sent_ref[...] = unit.astype(bf16)


def embed(inputs, hidden, second_weight, projection):
    rows, width = inputs.shape
    clips = rows // FRAMES
    joint = projection.shape[1]
    return pl.pallas_call(
        embed_kernel,
        in_specs=[VMEM_SPEC] * 4,
        out_specs=[VMEM_SPEC] * 5,
        out_shape=[
            pltpu.VMEM((rows, width), f32),
            pltpu.VMEM((rows, 1), f32),
            pltpu.VMEM((clips, joint), f32),
            pltpu.VMEM((clips, 1), f32),
            jax.ShapeDtypeStruct((clips, joint), bf16),
        ],
        compiler_params=pltpu.CompilerParams(vmem_limit_bytes=24 * MIB),
        cost_estimate=pl.CostEstimate(
            flops=2 * rows * width * hidden.shape[1], bytes_accessed=4 * MIB, transcendentals=0
        ),
        name="embed",
    )(inputs, hidden, in_vmem(second_weight), projection)


def gather_line(shard):
    pair = jnp.concatenate([shard, move(shard, core=1)])
    return jnp.concatenate([pair] + [move(pair, col=d) for d in (1, 2, 3)])


def gather_planes(line):
    return [line] + [move(line, hi=d) for d in (1, 2, 3)]


def groups_by_distance(pool_group, clips):
    hi, col, core = place()
    order = jnp.stack(
        [
            replica_of(hi + HI - h, col + COL - c, core + k)
            for h in range(HI)
            for c in range(COL)
            for k in range(CORE)
        ]
    )
    return jnp.repeat(pool_group[order], clips)


def loss_kernel(
    row_group_ref,
    col_group_ref,
    *refs,
):
    audio_refs, text_refs = refs[:HI], refs[HI : 2 * HI]
    projection_ref, normed_ref, inv_ref, unit_ref, inv_norm_ref, out_ref = refs[2 * HI :]
    clips = unit_ref.shape[0]
    rows = normed_ref.shape[0]
    audio = jnp.concatenate([r[...] for r in audio_refs], axis=0)
    text = jnp.concatenate([r[...] for r in text_refs], axis=0)
    scores = lax.dot_general(audio, text, LAST_DIMS, preferred_element_type=f32) * inv_temp
    weighted = jnp.where(row_group_ref[...] == col_group_ref[...], jnp.exp(scores), 0.0)
    by_cols = weighted[:clips] / jnp.sum(weighted, axis=0, keepdims=True)
    by_rows = weighted[:clips] / jnp.sum(weighted[:clips], axis=1, keepdims=True)
    shape = by_rows.shape
    own = lax.broadcasted_iota(jnp.int32, shape, 0) == lax.broadcasted_iota(jnp.int32, shape, 1)
    coeffs = grad_scale * (by_rows + by_cols - jnp.where(own, 2.0, 0.0))
    audio_grad = (
        jnp.dot(coeffs, text.astype(f32), precision=EXACT, preferred_element_type=f32) * inv_temp
    )
    unit = unit_ref[...]
    emb_grad = (
        audio_grad - unit * jnp.sum(unit * audio_grad, axis=-1, keepdims=True)
    ) * inv_norm_ref[...]
    pooled_grad = lax.dot_general(
        emb_grad,
        projection_ref[...].astype(f32),
        LAST_DIMS,
        precision=EXACT,
        preferred_element_type=f32,
    ) * (1.0 / (rows // clips))
    upstream = lax.dot_general(
        clip_rows(rows, clips),
        pooled_grad,
        (((0,), (0,)), ((), ())),
        precision=EXACT,
        preferred_element_type=f32,
    )
    normed = normed_ref[...]
    mean = jnp.mean(upstream, axis=-1, keepdims=True)
    along = jnp.mean(upstream * normed, axis=-1, keepdims=True)
    grad = (inv_ref[...] * (upstream - mean - normed * along)).astype(bf16)
    per_micro = out_ref.shape[1]
    for m in range(out_ref.shape[0]):
        out_ref[m] = grad[m * per_micro : (m + 1) * per_micro]


def loss_grad(groups, audio, text, projection, normed, inv_std, unit, inv_norm):
    rows, width = normed.shape
    operands = [groups[:, None], groups[None, :], *audio, *text, projection]
    return pl.pallas_call(
        loss_kernel,
        in_specs=[VMEM_SPEC] * (len(operands) + 4),
        out_specs=VMEM_SPEC,
        out_shape=pltpu.VMEM((MICRO, rows // MICRO, width), bf16),
        compiler_params=pltpu.CompilerParams(vmem_limit_bytes=24 * MIB),
        name="loss_grad",
    )(*operands, *[in_vmem(a) for a in (normed, inv_std, unit, inv_norm)])


def step_kernel(inputs_given, keeps, info, second_ref, first_ref, slope_ref, normed_ref, inv_ref, *rest):
    count = len(inputs_given)
    given, stores = rest[:count], rest[count : count + 3]
    if keeps:
        passed_ref, out_ref, pre_ref, in_ref = rest[count + 3 :]
    else:
        out_ref, pre_ref, in_ref = rest[count + 3 :]
    micro = info[0]

    @pl.when(info[1] == 1)
    def _():
        if count == 2:
            upstream = jnp.where(info[2] == 1, given[0][micro], given[1][...])
        elif inputs_given[0] == "last":
            upstream = given[0][micro]
        else:
            upstream = given[0][...]
        act_grad = lax.dot_general(
            upstream, second_ref[...], LAST_DIMS, preferred_element_type=f32
        )
        pre_grad = (act_grad * slope_ref[micro]).astype(bf16)
        normed_grad = lax.dot_general(
            pre_grad, first_ref[...], LAST_DIMS, preferred_element_type=f32
        )
        normed = normed_ref[micro].astype(f32)
        mean = jnp.mean(normed_grad, axis=-1, keepdims=True)
        along = jnp.mean(normed_grad * normed, axis=-1, keepdims=True)
        in_grad = upstream.astype(f32) + inv_ref[micro] * (normed_grad - mean - normed * along)
        in_grad = in_grad.astype(bf16)
        if keeps:
            passed_ref[...] = in_grad
            pre_ref[micro] = pre_grad
            out_ref[micro] = upstream
            in_ref[micro] = in_grad
        else:
            pre_ref[...] = pre_grad
            out_ref[...] = upstream
            in_ref[...] = in_grad

    if not keeps:

        @pl.when(info[1] == 0)
        def _():
            for store, last in zip(stores, (out_ref, pre_ref, in_ref)):
                last[...] = store[MICRO - 1]


def chain_step(info, weights, fixed, given, stores, keeps):
    rows, width = fixed[1].shape[1:]
    wide = fixed[0].shape[2]
    names = tuple(given)
    values = [in_vmem(given[n]) if n == "last" else given[n] for n in names]
    first_store = 1 + 5 + len(names)
    if keeps:
        shapes = [jax.ShapeDtypeStruct((rows, width), bf16)]
        shapes += [pltpu.VMEM(a.shape, a.dtype) for a in stores]
        aliases = {first_store + i: 1 + i for i in range(3)}
    else:
        shapes = [jax.ShapeDtypeStruct((rows, n), bf16) for n in (width, wide, width)]
        aliases = {}
    return pl.pallas_call(
        functools.partial(step_kernel, names, keeps),
        in_specs=[SMEM_SPEC] + [VMEM_SPEC] * (5 + len(names) + 3),
        out_specs=[VMEM_SPEC] * len(shapes),
        out_shape=shapes,
        input_output_aliases=aliases,
        compiler_params=pltpu.CompilerParams(vmem_limit_bytes=16 * MIB),
        cost_estimate=pl.CostEstimate(
            flops=4 * rows * width * wide, bytes_accessed=8 * MIB, transcendentals=0
        ),
        name="chain_step",
    )(
        info,
        *[in_vmem(w) for w in weights],
        *[in_vmem(a) for a in fixed],
        *values,
        *[in_vmem(a) for a in stores],
    )


def empty_stores(shapes):
    return pl.pallas_call(
        lambda *refs: None,
        out_specs=[VMEM_SPEC] * len(shapes),
        out_shape=[pltpu.VMEM(s, bf16) for s in shapes],
        compiler_params=pltpu.CompilerParams(vmem_limit_bytes=MIB),
        name="empty_stores",
    )()


def chip_columns(turned):
    _, col, core = place()
    width, rows = turned.shape
    part = width // (HI * COL * CORE)
    blocks = turned.reshape(HI, COL, CORE, part, rows)

    def half(side):
        chosen = lax.dynamic_index_in_dim(blocks, side, 2, keepdims=False)
        chosen = chosen.transpose(1, 0, 2, 3)
        return lax.dynamic_slice_in_dim(
            jnp.concatenate([chosen, chosen[: COL - 1]]), col, COL, 0
        )

    return jnp.concatenate([half(core), move(half(1 - core), core=1)], axis=-1)


def term_of(left, right, distance):
    chosen = left[distance]
    part, rows = chosen.shape[1:]
    product = jnp.dot(chosen.reshape(-1, rows), right, preferred_element_type=f32)
    return product.reshape(-1, part, right.shape[1])


def scatter_begin(left, right):
    far = term_of(left, right, 2).astype(bf16)
    far_low = move(far[:2], col=1)
    far_high = move(far[2:], col=-1)
    ahead = term_of(left, right, 1)
    back = term_of(left, right, 3)
    ahead_high = move(ahead[2:].astype(bf16), col=1)
    back_low = move(back[:2].astype(bf16), col=-1)
    return ahead[:2], back[2:], far_low, far_high, ahead_high, back_low


def scatter_rest(begun):
    ahead, back, far_low, far_high, ahead_high, back_low = begun
    ahead_low = move((ahead + far_low.astype(f32)).astype(bf16), col=1)
    back_high = move((back + far_high.astype(f32)).astype(bf16), col=-1)
    return ahead_low, ahead_high, back_low, back_high


def scatter_end(own, rest):
    ahead_low, ahead_high, back_low, back_high = (a.astype(f32) for a in rest)
    hi, _, _ = place()
    total = jnp.concatenate(
        [own[:2] + ahead_low + back_low, own[2:] + ahead_high + back_high]
    )
    result = lax.dynamic_index_in_dim(total, hi, 0, keepdims=False)
    rounded = total.astype(bf16)
    for distance in (1, 2, 3):
        given = lax.dynamic_index_in_dim(rounded, (hi + distance) % HI, 0, keepdims=False)
        result = result + move(given, hi=distance).astype(f32)
    return result / (HI * COL * CORE)


def paired_texts(text_embed, pair_label):
    texts = text_embed.astype(f32)
    unit_text = texts * lax.rsqrt(jnp.sum(texts * texts, axis=-1, keepdims=True) + eps_unit)
    slots = pair_label.shape[1]
    unit_text = unit_text.reshape(-1, slots, unit_text.shape[1])
    chooser = (pair_label[:, :, None] == jnp.arange(slots, dtype=jnp.int32)[None, None, :]).astype(f32)
    chosen = jnp.einsum("mcj,mje->mce", chooser, unit_text, precision=EXACT)
    return chosen.reshape(-1, chosen.shape[2])


def local(section_inputs, in_weight, out_weight, projection, text_embed, pair_label, pool_group):
    inputs = section_inputs[0]
    row_count, width = inputs.shape
    per_micro = row_count // MICRO
    clips = row_count // FRAMES
    wide = in_weight.shape[2]
    hi, col, core = place()
    info = jnp.stack([col, core]).astype(jnp.int32)

    shard = in_weight[0]
    half = wide // CORE
    kept = lax.dynamic_slice_in_dim(shard, core * half, half, 1)
    got = move(lax.dynamic_slice_in_dim(shard, (1 - core) * half, half, 1), core=1)
    first_shard = jnp.where(
        core == 0, jnp.concatenate([kept, got]), jnp.concatenate([got, kept])
    )
    second_shard = out_weight[0]
    first_moved = [move(first_shard, hi=d) for d in (1, 2, 3)]
    second_moved = [move(after(second_shard, first_shard), hi=d) for d in (1, 2, 3)]
    local_text = paired_texts(text_embed, pair_label).astype(bf16)

    first_stack = in_order(first_shard, first_moved, HI, hi)
    first_left, first_right = start_columns(first_stack)
    second_stack = in_order(second_shard, second_moved, HI, hi)
    second_left, second_right = start_columns(after(second_stack, first_stack))

    def spread(stack, left, right):
        far_low = move(left[:2], col=1)
        far_high = move(right[2:], col=-1)
        near = [stack, left, right]
        far = [far_low, far_high]
        return near + [move(a, core=1) for a in near], far + [move(a, core=1) for a in far]

    near_plan = [(0, d, o) for o in (False, True) for d in (0, COL - 1, 1)]
    far_plan = [(h, 2, o) for o in (False, True) for h in (0, 2)]
    first_near, first_far = spread(first_stack, first_left, first_right)
    second_near, second_far = spread(second_stack, second_left, second_right)
    first_weight = place_blocks(info, near_plan, first_near, (width, wide), True)
    first_weight = place_blocks(info, far_plan, first_far, (width, wide), True, first_weight)
    second_weight = place_blocks(info, near_plan, second_near, (wide, width), False)
    second_weight = place_blocks(
        info, far_plan, second_far, (wide, width), False, second_weight
    )
    text_line = gather_line(after(local_text, first_left, first_right))
    text_all = gather_planes(text_line)

    normed, inv_in, normed_t, hidden, hidden_t, slope = front(inputs, first_weight)
    out_normed, out_inv, unit, inv_norm, sent = embed(
        inputs, hidden, second_weight, projection
    )
    audio_line = gather_line(sent)
    audio_all = gather_planes(audio_line)
    normed_columns = chip_columns(after(normed_t, sent))
    hidden_columns = chip_columns(after(hidden_t, sent))
    groups = groups_by_distance(pool_group, clips)
    last_micro = loss_grad(
        groups, audio_all, text_all, projection, out_normed, out_inv, unit, inv_norm
    )

    section_count = lax.axis_size("section")
    section_id = lax.axis_index("section")
    is_last = section_id == section_count - 1
    fixed = (slope, normed, inv_in)
    weights = (second_weight, first_weight)
    stores = empty_stores([(MICRO, per_micro, n) for n in (width, wide, width)])
    arrived = [None, None]
    slots = 2 * (section_count - 1) + MICRO
    for slot in range(slots):
        micro_id = slot - 2 * (section_count - 1 - section_id)
        active = jnp.logical_and(micro_id >= 0, micro_id < MICRO)
        step_info = jnp.stack(
            [jnp.clip(micro_id, 0, MICRO - 1), active, is_last]
        ).astype(jnp.int32)
        given = {}
        if slot < MICRO:
            given["last"] = last_micro
        if arrived[slot] is not None:
            given["next"] = arrived[slot]
        keeps = slot < slots - 1
        results = chain_step(step_info, weights, fixed, given, stores, keeps)
        if not keeps:
            last_out, last_pre, last_in = results
            break
        passed, *stores = results
        route = [
            (s, s - 1)
            for s in range(1, section_count)
            if 0 <= slot - 2 * (section_count - 1 - s) < MICRO
        ]
        arrived.append(lax.ppermute(passed, "section", route) if route else None)

    def rows_of(store, last):
        early = store[: MICRO - 1].reshape(-1, store.shape[2])
        return jnp.concatenate(
            [early, last, move(early, core=1), move(last, core=1)], axis=0
        )

    out_rows = rows_of(stores[0], last_out)
    pre_rows = rows_of(stores[1], last_pre)
    second_begun = scatter_begin(hidden_columns, out_rows)
    first_begun = scatter_begin(normed_columns, pre_rows)
    second_rest = scatter_rest(second_begun)
    first_rest = scatter_rest(first_begun)
    second_own = term_of(hidden_columns, out_rows, 0)
    first_own = term_of(normed_columns, pre_rows, 0)
    second_sum = scatter_end(second_own, second_rest)
    first_sum = scatter_end(first_own, first_rest)
    in_grads = jnp.concatenate([stores[2][: MICRO - 1].reshape(-1, width), last_in])
    return (in_grads[None], first_sum[None], second_sum[None])


def solution(mesh):
    return jax.shard_map(
        local,
        mesh=mesh,
        in_specs=(
            P("section", "replica", None),
            P("section", "replica", None),
            P("section", "replica", None),
            P(),
            P("replica", None),
            P("replica", None),
            P(),
        ),
        out_specs=(
            P("section", "replica", None),
            P("section", "replica", None),
            P("section", "replica", None),
        ),
        check_vma=False,
    )
```

```python
import functools

import jax
import jax.numpy as jnp
from jax import lax
from jax.experimental import pallas as pl
from jax.experimental.pallas import tpu as pltpu
from jax.sharding import PartitionSpec as P

MICRO = 4
FRAMES = 44

HI = 4
COL = 4
CORE = 2

MIB = 2**20
LAST_DIMS = (((1,), (1,)), ((), ()))
EXACT = lax.Precision.HIGHEST

eps_norm = 1e-05
eps_unit = 1e-06
inv_temp = 1.0 / 0.07
grad_scale = 256.0
sqrt_half = 0.7071067811865476
inv_sqrt_two_pi = 0.3989422804014327

bf16 = jnp.bfloat16
f32 = jnp.float32


def replica_of(hi, col, core):
    return ((hi % HI) * COL + col % COL) * CORE + core % CORE


def move(block, hi=0, col=0, core=0):
    route = [
        (replica_of(h, c, k), replica_of(h + hi, c + col, k + core))
        for h in range(HI)
        for c in range(COL)
        for k in range(CORE)
    ]
    return lax.ppermute(block, "replica", route)


def place():
    replica = lax.axis_index("replica")
    return replica // (COL * CORE), (replica // CORE) % COL, replica % CORE


def after(value, *others):
    return lax.optimization_barrier((value, *others))[0]


def move_across(block, mask):
    count = HI * COL * CORE
    return lax.ppermute(block, "replica", [(r, r ^ mask) for r in range(count)])


def slice_at(values, start, size, axis):
    return lax.dynamic_slice_in_dim(values, start, size, axis, allow_negative_indices=False)


def item_at(values, index, axis=0):
    return lax.dynamic_index_in_dim(
        values, index, axis, keepdims=False, allow_negative_indices=False
    )


def in_order(own, from_back, axis_size, first):
    ring = [from_back[2], from_back[1], from_back[0], own]
    ring = jnp.stack(ring + ring[:3])
    return slice_at(ring, first, axis_size, 0)


def in_vmem(value):
    return pltpu.with_memory_space_constraint(value, pltpu.VMEM)


VMEM_SPEC = pl.BlockSpec(memory_space=pltpu.VMEM)
ANY_SPEC = pl.BlockSpec(memory_space=pl.ANY)
SMEM_SPEC = pl.BlockSpec(memory_space=pltpu.SMEM)


def place_kernel(plan, by_columns, info, *refs):
    pieces = refs[: len(plan)]
    whole, sems = refs[-2], refs[-1]
    col, core = info[0], info[1]
    copies = []
    for (first_hi, distance, other), piece in zip(plan, pieces):
        count, rows, width = piece.shape
        at_col = lax.rem(col + distance, COL)
        side = 1 - core if other else core
        for k in range(count):
            chip = (first_hi + k) * COL + at_col
            if by_columns:
                row = chip * rows
                column = pl.ds(pl.multiple_of(side * width, 128), width)
            else:
                row = (chip * CORE + side) * rows
                column = slice(None)
            copy = pltpu.make_async_copy(
                piece.at[k],
                whole.at[pl.ds(pl.multiple_of(row, 16), rows), column],
                sems.at[len(copies)],
            )
            copy.start()
            copies.append(copy)
    for copy in copies:
        copy.wait()


def place_blocks(info, plan, pieces, shape, by_columns, whole=None):
    count = sum(p.shape[0] for p in pieces)
    return pl.pallas_call(
        functools.partial(place_kernel, plan, by_columns),
        in_specs=[SMEM_SPEC]
        + [ANY_SPEC] * len(pieces)
        + ([] if whole is None else [VMEM_SPEC]),
        out_specs=VMEM_SPEC,
        out_shape=pltpu.VMEM(shape, bf16),
        scratch_shapes=[pltpu.SemaphoreType.DMA((count,))],
        input_output_aliases={} if whole is None else {1 + len(pieces): 0},
        compiler_params=pltpu.CompilerParams(vmem_limit_bytes=8 * MIB),
        cost_estimate=pl.CostEstimate(
            flops=0, bytes_accessed=2 * sum(2 * p.size for p in pieces), transcendentals=0
        ),
        name="place_blocks",
    )(info, *pieces, *([] if whole is None else [in_vmem(whole)]))


def front_kernel(
    inputs_ref, first_ref, normed_ref, inv_ref, normed_t_ref, hidden_ref, hidden_t_ref, slope_ref
):
    micro, rows = normed_ref.shape[:2]
    values = inputs_ref[...].astype(f32)
    centred = values - jnp.mean(values, axis=-1, keepdims=True)
    inv_std = lax.rsqrt(jnp.mean(centred * centred, axis=-1, keepdims=True) + eps_norm)
    scaled = centred * inv_std
    normed = scaled.astype(bf16)
    for m in range(micro):
        normed_ref[m] = normed[m * rows : (m + 1) * rows]
        inv_ref[m] = inv_std[m * rows : (m + 1) * rows]
    normed_t_ref[...] = scaled.T.astype(bf16)
    step = 256

    @pl.loop(0, first_ref.shape[1] // step)
    def _(j):
        part = pl.ds(pl.multiple_of(j * step, step), step)
        preact = jnp.dot(normed, first_ref[:, part], preferred_element_type=f32)
        cdf = 0.5 * (1.0 + lax.erf(preact * sqrt_half))
        hidden = preact * cdf
        hidden_ref[:, part] = hidden.astype(bf16)
        hidden_t_ref[part, :] = hidden.T.astype(bf16)
        slope = cdf + preact * jnp.exp(-0.5 * preact * preact) * inv_sqrt_two_pi
        for m in range(micro):
            slope_ref[m, :, part] = slope[m * rows : (m + 1) * rows]


def front(inputs, first_weight):
    rows, width = inputs.shape
    wide = first_weight.shape[1]
    per_micro = rows // MICRO
    return pl.pallas_call(
        front_kernel,
        in_specs=[VMEM_SPEC] * 2,
        out_specs=[VMEM_SPEC] * 6,
        out_shape=[
            pltpu.VMEM((MICRO, per_micro, width), bf16),
            pltpu.VMEM((MICRO, per_micro, 1), f32),
            jax.ShapeDtypeStruct((width, rows), bf16),
            jax.ShapeDtypeStruct((rows, wide), bf16),
            jax.ShapeDtypeStruct((wide, rows), bf16),
            pltpu.VMEM((MICRO, per_micro, wide), f32),
        ],
        compiler_params=pltpu.CompilerParams(vmem_limit_bytes=24 * MIB),
        cost_estimate=pl.CostEstimate(
            flops=2 * rows * width * wide, bytes_accessed=4 * MIB, transcendentals=0
        ),
        name="front",
    )(inputs, in_vmem(first_weight))


def clip_rows(rows, clips):
    first = lax.broadcasted_iota(jnp.int32, (clips, rows), 0) * (rows // clips)
    row = lax.broadcasted_iota(jnp.int32, (clips, rows), 1)
    return jnp.where((row >= first) & (row < first + rows // clips), 1.0, 0.0).astype(f32)


def embed_kernel(
    inputs_ref,
    hidden_ref,
    second_ref,
    projection_ref,
    normed_ref,
    inv_ref,
    unit_ref,
    inv_norm_ref,
    sent_ref,
):
    rows = inputs_ref.shape[0]
    clips = unit_ref.shape[0]
    block_out = inputs_ref[...].astype(f32) + jnp.dot(
        hidden_ref[...], second_ref[...], preferred_element_type=f32
    )
    centred = block_out - jnp.mean(block_out, axis=-1, keepdims=True)
    inv_std = lax.rsqrt(jnp.mean(centred * centred, axis=-1, keepdims=True) + eps_norm)
    normed = centred * inv_std
    normed_ref[...] = normed
    inv_ref[...] = inv_std
    sums = jnp.dot(
        clip_rows(rows, clips), normed, precision=EXACT, preferred_element_type=f32
    )
    pooled = (sums * (1.0 / (rows // clips))).astype(bf16)
    embedded = jnp.dot(pooled, projection_ref[...], preferred_element_type=f32)
    inv_norm = lax.rsqrt(jnp.sum(embedded * embedded, axis=-1, keepdims=True) + eps_unit)
    unit = embedded * inv_norm
    unit_ref[...] = unit
    inv_norm_ref[...] = inv_norm
    sent_ref[...] = unit.astype(bf16)


def embed(inputs, hidden, second_weight, projection):
    rows, width = inputs.shape
    clips = rows // FRAMES
    joint = projection.shape[1]
    return pl.pallas_call(
        embed_kernel,
        in_specs=[VMEM_SPEC] * 4,
        out_specs=[VMEM_SPEC] * 5,
        out_shape=[
            pltpu.VMEM((rows, width), f32),
            pltpu.VMEM((rows, 1), f32),
            pltpu.VMEM((clips, joint), f32),
            pltpu.VMEM((clips, 1), f32),
            jax.ShapeDtypeStruct((clips, joint), bf16),
        ],
        compiler_params=pltpu.CompilerParams(vmem_limit_bytes=24 * MIB),
        cost_estimate=pl.CostEstimate(
            flops=2 * rows * width * hidden.shape[1], bytes_accessed=4 * MIB, transcendentals=0
        ),
        name="embed",
    )(inputs, hidden, in_vmem(second_weight), projection)


MASKS = (1, 2, 4, 8, 16)


def gather_step(held, mask):
    return jnp.concatenate([held, move_across(held, mask)])


def gather_clips(shard):
    for mask in MASKS[:-1]:
        shard = gather_step(shard, mask)
    return [shard, move_across(shard, MASKS[-1])]


def groups_by_distance(pool_group, clips):
    order = [0]
    for mask in MASKS:
        order = order + [o ^ mask for o in order]
    replica = lax.axis_index("replica")
    groups = pool_group[jnp.bitwise_xor(replica, jnp.array(order, jnp.int32))]
    return jnp.broadcast_to(groups[:, None], (len(order), clips)).reshape(1, -1).astype(f32)


def loss_kernel(group_ref, *refs):
    audio_refs, text_refs = refs[:2], refs[2:4]
    projection_ref, normed_ref, inv_ref, unit_ref, inv_norm_ref, out_ref = refs[4:]
    clips = unit_ref.shape[0]
    rows = normed_ref.shape[0]
    audio = jnp.concatenate([r[...] for r in audio_refs], axis=0)
    text = jnp.concatenate([r[...] for r in text_refs], axis=0)
    scores = lax.dot_general(audio, text, LAST_DIMS, preferred_element_type=f32) * inv_temp
    groups = jnp.broadcast_to(group_ref[...], scores.shape)
    weighted = jnp.where(groups == groups.T, jnp.exp(scores), 0.0)
    by_cols = weighted[:clips] / jnp.sum(weighted, axis=0, keepdims=True)
    by_rows = weighted[:clips] / jnp.sum(weighted[:clips], axis=1, keepdims=True)
    shape = by_rows.shape
    own = lax.broadcasted_iota(jnp.int32, shape, 0) == lax.broadcasted_iota(jnp.int32, shape, 1)
    coeffs = grad_scale * (by_rows + by_cols - jnp.where(own, 2.0, 0.0))
    audio_grad = (
        jnp.dot(coeffs, text.astype(f32), precision=EXACT, preferred_element_type=f32) * inv_temp
    )
    unit = unit_ref[...]
    emb_grad = (
        audio_grad - unit * jnp.sum(unit * audio_grad, axis=-1, keepdims=True)
    ) * inv_norm_ref[...]
    pooled_grad = lax.dot_general(
        emb_grad,
        projection_ref[...].astype(f32),
        LAST_DIMS,
        precision=EXACT,
        preferred_element_type=f32,
    ) * (1.0 / (rows // clips))
    upstream = lax.dot_general(
        clip_rows(rows, clips),
        pooled_grad,
        (((0,), (0,)), ((), ())),
        precision=EXACT,
        preferred_element_type=f32,
    )
    normed = normed_ref[...]
    mean = jnp.mean(upstream, axis=-1, keepdims=True)
    along = jnp.mean(upstream * normed, axis=-1, keepdims=True)
    grad = (inv_ref[...] * (upstream - mean - normed * along)).astype(bf16)
    per_micro = out_ref.shape[1]
    for m in range(out_ref.shape[0]):
        out_ref[m] = grad[m * per_micro : (m + 1) * per_micro]


def loss_grad(groups, audio, text, projection, normed, inv_std, unit, inv_norm):
    rows, width = normed.shape
    operands = [groups, *audio, *text, projection]
    return pl.pallas_call(
        loss_kernel,
        in_specs=[VMEM_SPEC] * (len(operands) + 4),
        out_specs=VMEM_SPEC,
        out_shape=pltpu.VMEM((MICRO, rows // MICRO, width), bf16),
        compiler_params=pltpu.CompilerParams(vmem_limit_bytes=24 * MIB),
        name="loss_grad",
    )(*operands, *[in_vmem(a) for a in (normed, inv_std, unit, inv_norm)])


def step_kernel(inputs_given, keeps, slot, last_section, section_ref, second_ref, first_ref, slope_ref, normed_ref, inv_ref, *rest):
    count = len(inputs_given)
    given, stores = rest[:count], rest[count : count + 3]
    if keeps:
        passed_ref, out_ref, pre_ref, in_ref = rest[count + 3 :]
    else:
        out_ref, pre_ref, in_ref = rest[count + 3 :]
    section = section_ref[0]
    micro_id = slot - 2 * (last_section - section)
    active = (micro_id >= 0) & (micro_id < MICRO)
    micro = jnp.clip(micro_id, 0, MICRO - 1)

    @pl.when(active)
    def _():
        if count == 2:
            upstream = jnp.where(section == last_section, given[0][micro], given[1][...])
        elif inputs_given[0] == "last":
            upstream = given[0][micro]
        else:
            upstream = given[0][...]
        act_grad = lax.dot_general(
            upstream, second_ref[...], LAST_DIMS, preferred_element_type=f32
        )
        pre_grad = (act_grad * slope_ref[micro]).astype(bf16)
        normed_grad = lax.dot_general(
            pre_grad, first_ref[...], LAST_DIMS, preferred_element_type=f32
        )
        normed = normed_ref[micro].astype(f32)
        mean = jnp.mean(normed_grad, axis=-1, keepdims=True)
        along = jnp.mean(normed_grad * normed, axis=-1, keepdims=True)
        in_grad = upstream.astype(f32) + inv_ref[micro] * (normed_grad - mean - normed * along)
        in_grad = in_grad.astype(bf16)
        if keeps:
            passed_ref[...] = in_grad
            pre_ref[micro] = pre_grad
            out_ref[micro] = upstream
            in_ref[micro] = in_grad
        else:
            pre_ref[...] = pre_grad
            out_ref[...] = upstream
            in_ref[...] = in_grad

    if not keeps:

        @pl.when(jnp.logical_not(active))
        def _():
            for store, last in zip(stores, (out_ref, pre_ref, in_ref)):
                last[...] = store[MICRO - 1]


def chain_step(slot, last_section, section, weights, fixed, given, stores, keeps):
    rows, width = fixed[1].shape[1:]
    wide = fixed[0].shape[2]
    names = tuple(given)
    values = [in_vmem(given[n]) if n == "last" else given[n] for n in names]
    first_store = 1 + 5 + len(names)
    if keeps:
        shapes = [jax.ShapeDtypeStruct((rows, width), bf16)]
        shapes += [pltpu.VMEM(a.shape, a.dtype) for a in stores]
        aliases = {first_store + i: 1 + i for i in range(3)}
    else:
        shapes = [jax.ShapeDtypeStruct((rows, n), bf16) for n in (width, wide, width)]
        aliases = {}
    return pl.pallas_call(
        functools.partial(step_kernel, names, keeps, slot, last_section),
        in_specs=[SMEM_SPEC] + [VMEM_SPEC] * (5 + len(names) + 3),
        out_specs=[VMEM_SPEC] * len(shapes),
        out_shape=shapes,
        input_output_aliases=aliases,
        compiler_params=pltpu.CompilerParams(vmem_limit_bytes=16 * MIB),
        cost_estimate=pl.CostEstimate(
            flops=4 * rows * width * wide, bytes_accessed=8 * MIB, transcendentals=0
        ),
        name="chain_step",
    )(
        section,
        *[in_vmem(w) for w in weights],
        *[in_vmem(a) for a in fixed],
        *values,
        *[in_vmem(a) for a in stores],
    )


def empty_stores(shapes):
    return pl.pallas_call(
        lambda *refs: None,
        out_specs=[VMEM_SPEC] * len(shapes),
        out_shape=[pltpu.VMEM(s, bf16) for s in shapes],
        compiler_params=pltpu.CompilerParams(vmem_limit_bytes=MIB),
        name="empty_stores",
    )()


def column_halves(turned, at):
    width, rows = turned.shape
    blocks = turned.reshape(HI, COL, CORE, width // (HI * COL * CORE), rows)
    return item_at(blocks, at["core"], 2), item_at(blocks, at["other"], 2)


LOW, HIGH = slice(0, HI // 2), slice(HI // 2, HI)


def term_of(left, right, at, distance, part=slice(None)):
    chosen = item_at(left[part], at["columns"][distance], 1)
    height, rows = chosen.shape[1:]
    product = jnp.dot(chosen.reshape(-1, rows), right, preferred_element_type=f32)
    return product.reshape(-1, height, right.shape[1])


def scatter_end(own, ahead, back, at):
    total = jnp.concatenate(
        [
            own[part] + a.astype(f32) + b.astype(f32)
            for part, a, b in zip((LOW, HIGH), ahead, back)
        ]
    )
    result = item_at(total, at["hi"][0])
    rounded = total.astype(bf16)
    for distance in (1, 2, 3):
        given = item_at(rounded, at["hi"][distance])
        result = result + move(given, hi=distance).astype(f32)
    return result / (HI * COL * CORE)


def paired_texts(text_embed, pair_label):
    texts = text_embed.astype(f32)
    unit_text = texts * lax.rsqrt(jnp.sum(texts * texts, axis=-1, keepdims=True) + eps_unit)
    slots = pair_label.shape[1]
    unit_text = unit_text.reshape(-1, slots, unit_text.shape[1])
    chooser = (pair_label[:, :, None] == jnp.arange(slots, dtype=jnp.int32)[None, None, :]).astype(f32)
    chosen = jnp.einsum("mcj,mje->mce", chooser, unit_text, precision=EXACT)
    return chosen.reshape(-1, chosen.shape[2])


def local(section_inputs, in_weight, out_weight, projection, text_embed, pair_label, pool_group):
    inputs = section_inputs[0]
    row_count, width = inputs.shape
    per_micro = row_count // MICRO
    clips = row_count // FRAMES
    wide = in_weight.shape[2]
    half = wide // CORE
    section_count = lax.axis_size("section")
    hi, col, core = place()
    groups = groups_by_distance(pool_group, clips)
    at = dict(
        hi=[(hi + d) % HI for d in range(HI)],
        first_hi=HI - 1 - hi,
        col=col,
        core=core,
        other=1 - core,
        chip=jnp.stack([col, core]).astype(jnp.int32),
        section=jnp.full((1,), lax.axis_index("section"), jnp.int32),
        groups=groups,
        text=paired_texts(text_embed, pair_label).astype(bf16),
        columns=[(col + d) % COL for d in range(COL)],
        kept=core * half,
        given=(1 - core) * half,
    )
    at = lax.optimization_barrier(at)

    shard = in_weight[0]
    kept = slice_at(shard, at["kept"], half, 1)
    got = move(slice_at(shard, at["given"], half, 1), core=1)
    first_shard = jnp.where(
        at["core"] == 0, jnp.concatenate([kept, got]), jnp.concatenate([got, kept])
    )
    first_moved = [move(first_shard, hi=d) for d in (1, 2, 3)]
    first_stack = in_order(first_shard, first_moved, HI, at["first_hi"])
    texts = at["text"]
    for mask in MASKS[:3]:
        texts = gather_step(texts, mask)
    first_stack, texts = lax.optimization_barrier((first_stack, texts))
    first_left, first_right = move(first_stack, col=1), move(first_stack, col=-1)
    texts = gather_step(texts, MASKS[3])
    second_shard, texts = lax.optimization_barrier((out_weight[0], texts))
    second_moved = [move(second_shard, hi=d) for d in (1, 2, 3)]
    second_stack = in_order(second_shard, second_moved, HI, at["first_hi"])
    second_stack, texts = lax.optimization_barrier((second_stack, texts))
    text_all = [texts, move_across(texts, MASKS[4])]
    first_far = move(first_left, col=1)
    second_right = move(after(second_stack, first_right), col=-1)
    second_left = move(after(second_stack, first_far), col=1)
    second_far = move(second_right, col=-1)

    near_plan = [(0, d, o) for d in (0, COL - 1, 1) for o in (False, True)]
    far_plan = [(0, 2, o) for o in (False, True)]

    def both(*blocks):
        return [piece for b in blocks for piece in (b, move(b, core=1))]

    first_weight = place_blocks(
        at["chip"], near_plan, both(first_stack, first_left, first_right), (width, wide), True
    )
    first_weight = place_blocks(
        at["chip"], far_plan, both(first_far), (width, wide), True, first_weight
    )
    normed, inv_in, normed_t, hidden, hidden_t, slope = front(
        after(inputs, *text_all), first_weight
    )
    normed_halves = column_halves(normed_t, at)
    hidden_halves = column_halves(hidden_t, at)
    second_weight = place_blocks(
        at["chip"],
        [near_plan[i] for i in (0, 1, 4, 5)],
        both(second_stack, second_right),
        (wide, width),
        False,
    )
    second_weight = place_blocks(
        at["chip"],
        [near_plan[2], near_plan[3]] + far_plan,
        both(after(second_left, *normed_halves, *hidden_halves), second_far),
        (wide, width),
        False,
        second_weight,
    )
    out_normed, out_inv, unit, inv_norm, sent = embed(
        inputs, hidden, second_weight, projection
    )
    audio_all = gather_clips(sent)
    last_micro = loss_grad(
        at["groups"], audio_all, text_all, projection, out_normed, out_inv, unit, inv_norm
    )

    normed_columns, hidden_columns = (
        jnp.concatenate([own, move(other, core=1)], axis=-1)
        for own, other in (normed_halves, hidden_halves)
    )
    fixed = (slope, normed, inv_in)
    weights = (second_weight, first_weight)
    stores = empty_stores([(MICRO, per_micro, n) for n in (width, wide, width)])
    arrived = [None, None]
    slots = 2 * (section_count - 1) + MICRO
    for slot in range(slots):
        given = {}
        if slot == slots - 6:
            arrived[slot] = after(arrived[slot], normed_columns, hidden_columns)
        if slot == slots - 1:
            early = [a[: MICRO - 1].reshape(-1, a.shape[2]) for a in stores]
            crossed = [move(a, core=1) for a in early[:2]]
            arrived[slot], *crossed = lax.optimization_barrier((arrived[slot], *crossed))
        if slot < MICRO:
            given["last"] = last_micro
        if arrived[slot] is not None:
            given["next"] = arrived[slot]
        keeps = slot < slots - 1
        results = chain_step(
            slot, section_count - 1, at["section"], weights, fixed, given, stores, keeps
        )
        if not keeps:
            last_out, last_pre, last_in = results
            break
        passed, *stores = results
        route = [
            (s, s - 1)
            for s in range(1, section_count)
            if 0 <= slot - 2 * (section_count - 1 - s) < MICRO
        ]
        arrived.append(lax.ppermute(passed, "section", route) if route else None)

    out_rows, pre_rows = (
        jnp.concatenate([own, last, other, move(last, core=1)])
        for own, last, other in zip(early, (last_out, last_pre), crossed)
    )

    def term(second, distance, part=slice(None)):
        left, right = (hidden_columns, out_rows) if second else (normed_columns, pre_rows)
        return term_of(left, right, at, distance, part)

    def far(second, *gates):
        low, high = term(second, 2, LOW).astype(bf16), term(second, 2, HIGH).astype(bf16)
        if gates:
            low, high = after(low, *gates), after(high, *gates)
        return low, high, move(low, col=1), move(high, col=-1)

    def near_free(second, *gates):
        ahead = after(term(second, 1, HIGH).astype(bf16), *gates)
        back = after(term(second, 3, LOW).astype(bf16), *gates)
        return ahead, back, move(ahead, col=1), move(back, col=-1)

    def near_summed(second, low, high):
        ahead = (term(second, 1, LOW) + low.astype(f32)).astype(bf16)
        back = (term(second, 3, HIGH) + high.astype(f32)).astype(bf16)
        return ahead, back, move(ahead, col=1), move(back, col=-1)

    *sent, low2, high2 = far(True)
    *sent, ahead_high2, back_low2 = near_free(True, *sent)
    *sent, low1, high1 = far(False, *sent)
    *sent, ahead_low2, back_high2 = near_summed(True, low2, high2)
    *sent, ahead_high1, back_low1 = near_free(False, *sent)
    *sent, ahead_low1, back_high1 = near_summed(False, low1, high1)
    second_sum = scatter_end(
        term(True, 0), (ahead_low2, ahead_high2), (back_low2, back_high2), at
    )
    first_sum = scatter_end(
        term(False, 0), (ahead_low1, ahead_high1), (back_low1, back_high1), at
    )
    in_grads = jnp.concatenate([early[2], last_in])
    return (in_grads[None], first_sum[None], second_sum[None])


def solution(mesh):
    return jax.shard_map(
        local,
        mesh=mesh,
        in_specs=(
            P("section", "replica", None),
            P("section", "replica", None),
            P("section", "replica", None),
            P(),
            P("replica", None),
            P("replica", None),
            P(),
        ),
        out_specs=(
            P("section", "replica", None),
            P("section", "replica", None),
            P("section", "replica", None),
        ),
        check_vma=False,
    )
```

```python
import functools

import jax
import jax.numpy as jnp
from jax import lax
from jax.experimental import pallas as pl
from jax.experimental.pallas import tpu as pltpu
from jax.sharding import PartitionSpec as P

MICRO = 4
FRAMES = 44

HI = 4
COL = 4
CORE = 2

MIB = 2**20
LAST_DIMS = (((1,), (1,)), ((), ()))
EXACT = lax.Precision.HIGHEST

eps_norm = 1e-05
eps_unit = 1e-06
inv_temp = 1.0 / 0.07
grad_scale = 256.0
sqrt_half = 0.7071067811865476
inv_sqrt_two_pi = 0.3989422804014327

bf16 = jnp.bfloat16
f32 = jnp.float32


def replica_of(hi, col, core):
    return ((hi % HI) * COL + col % COL) * CORE + core % CORE


def move(block, hi=0, col=0, core=0):
    route = [
        (replica_of(h, c, k), replica_of(h + hi, c + col, k + core))
        for h in range(HI)
        for c in range(COL)
        for k in range(CORE)
    ]
    return lax.ppermute(block, "replica", route)


def place():
    replica = lax.axis_index("replica")
    return replica >> 3, (replica >> 1) & (COL - 1), replica & (CORE - 1)


def together(*values):
    return lax.optimization_barrier(values)


def move_across(block, mask):
    count = HI * COL * CORE
    return lax.ppermute(block, "replica", [(r, r ^ mask) for r in range(count)])


def slice_at(values, start, size, axis):
    return lax.dynamic_slice_in_dim(values, start, size, axis, allow_negative_indices=False)


def item_at(values, index, axis=0):
    return lax.dynamic_index_in_dim(
        values, index, axis, keepdims=False, allow_negative_indices=False
    )


def in_order(own, from_back, axis_size, first):
    ring = [from_back[2], from_back[1], from_back[0], own]
    ring = jnp.stack(ring + ring[:3])
    return slice_at(ring, first, axis_size, 0)


def in_vmem(value):
    return pltpu.with_memory_space_constraint(value, pltpu.VMEM)


VMEM_SPEC = pl.BlockSpec(memory_space=pltpu.VMEM)
ANY_SPEC = pl.BlockSpec(memory_space=pl.ANY)
SMEM_SPEC = pl.BlockSpec(memory_space=pltpu.SMEM)


def place_kernel(plan, by_columns, info, *refs):
    pieces, whole = refs[: len(plan)], refs[-1]
    col, core = info[0], info[1]
    for (first_hi, distance, other), piece in zip(plan, pieces):
        count, rows, width = piece.shape
        at_col = lax.rem(col + distance, COL)
        side = 1 - core if other else core
        for k in range(count):
            chip = (first_hi + k) * COL + at_col
            if by_columns:
                row = chip * rows
                column = pl.ds(pl.multiple_of(side * width, width), width)
            else:
                row = (chip * CORE + side) * rows
                column = slice(None)
            whole[pl.ds(pl.multiple_of(row, 16), rows), column] = piece[k]


def place_blocks(info, plan, pieces, shape, by_columns, whole=None):
    return pl.pallas_call(
        functools.partial(place_kernel, plan, by_columns),
        in_specs=[SMEM_SPEC]
        + [VMEM_SPEC] * len(pieces)
        + ([] if whole is None else [VMEM_SPEC]),
        out_specs=VMEM_SPEC,
        out_shape=pltpu.VMEM(shape, bf16),
        input_output_aliases={} if whole is None else {1 + len(pieces): 0},
        compiler_params=pltpu.CompilerParams(vmem_limit_bytes=12 * MIB),
        cost_estimate=pl.CostEstimate(
            flops=0, bytes_accessed=2 * sum(p.size for p in pieces), transcendentals=0
        ),
        name="place_blocks",
    )(info, *pieces, *([] if whole is None else [in_vmem(whole)]))


def front_kernel(
    inputs_ref, first_ref, waits_ref, normed_ref, inv_ref, normed_t_ref, hidden_ref, hidden_t_ref, slope_ref
):
    micro, rows = normed_ref.shape[:2]
    values = inputs_ref[...].astype(f32)
    centred = values - jnp.mean(values, axis=-1, keepdims=True)
    inv_std = lax.rsqrt(jnp.mean(centred * centred, axis=-1, keepdims=True) + eps_norm)
    scaled = centred * inv_std
    normed = scaled.astype(bf16)
    for m in range(micro):
        normed_ref[m] = normed[m * rows : (m + 1) * rows]
        inv_ref[m] = inv_std[m * rows : (m + 1) * rows]
    normed_t_ref[...] = scaled.T.astype(bf16)
    step = 256

    @pl.loop(0, first_ref.shape[1] // step)
    def _(j):
        part = pl.ds(pl.multiple_of(j * step, step), step)
        preact = jnp.dot(normed, first_ref[:, part], preferred_element_type=f32)
        cdf = 0.5 * (1.0 + lax.erf(preact * sqrt_half))
        hidden = preact * cdf
        hidden_ref[:, part] = hidden.astype(bf16)
        hidden_t_ref[part, :] = hidden.T.astype(bf16)
        slope = cdf + preact * jnp.exp(-0.5 * preact * preact) * inv_sqrt_two_pi
        for m in range(micro):
            slope_ref[m, :, part] = slope[m * rows : (m + 1) * rows]


def front(inputs, first_weight, waits):
    rows, width = inputs.shape
    wide = first_weight.shape[1]
    per_micro = rows // MICRO
    return pl.pallas_call(
        front_kernel,
        in_specs=[VMEM_SPEC] * 3,
        out_specs=[VMEM_SPEC] * 6,
        out_shape=[
            pltpu.VMEM((MICRO, per_micro, width), bf16),
            pltpu.VMEM((MICRO, per_micro, 1), f32),
            jax.ShapeDtypeStruct((width, rows), bf16),
            jax.ShapeDtypeStruct((rows, wide), bf16),
            jax.ShapeDtypeStruct((wide, rows), bf16),
            pltpu.VMEM((MICRO, per_micro, wide), f32),
        ],
        compiler_params=pltpu.CompilerParams(vmem_limit_bytes=24 * MIB),
        cost_estimate=pl.CostEstimate(
            flops=2 * rows * width * wide, bytes_accessed=4 * MIB, transcendentals=0
        ),
        name="front",
    )(inputs, in_vmem(first_weight), in_vmem(waits))


def clip_rows(rows, clips):
    first = lax.broadcasted_iota(jnp.int32, (clips, rows), 0) * (rows // clips)
    row = lax.broadcasted_iota(jnp.int32, (clips, rows), 1)
    return jnp.where((row >= first) & (row < first + rows // clips), 1.0, 0.0).astype(f32)


def embed_kernel(
    inputs_ref,
    hidden_ref,
    second_ref,
    projection_ref,
    normed_ref,
    inv_ref,
    unit_ref,
    inv_norm_ref,
    sent_ref,
):
    rows = inputs_ref.shape[0]
    clips = unit_ref.shape[0]
    block_out = inputs_ref[...].astype(f32) + jnp.dot(
        hidden_ref[...], second_ref[...], preferred_element_type=f32
    )
    centred = block_out - jnp.mean(block_out, axis=-1, keepdims=True)
    inv_std = lax.rsqrt(jnp.mean(centred * centred, axis=-1, keepdims=True) + eps_norm)
    normed = centred * inv_std
    normed_ref[...] = normed
    inv_ref[...] = inv_std
    sums = jnp.dot(
        clip_rows(rows, clips), normed, precision=EXACT, preferred_element_type=f32
    )
    pooled = (sums * (1.0 / (rows // clips))).astype(bf16)
    embedded = jnp.dot(pooled, projection_ref[...], preferred_element_type=f32)
    inv_norm = lax.rsqrt(jnp.sum(embedded * embedded, axis=-1, keepdims=True) + eps_unit)
    unit = embedded * inv_norm
    unit_ref[...] = unit
    inv_norm_ref[...] = inv_norm
    sent_ref[...] = unit.astype(bf16)


def embed(inputs, hidden, second_weight, projection):
    rows, width = inputs.shape
    clips = rows // FRAMES
    joint = projection.shape[1]
    return pl.pallas_call(
        embed_kernel,
        in_specs=[VMEM_SPEC] * 4,
        out_specs=[VMEM_SPEC] * 5,
        out_shape=[
            pltpu.VMEM((rows, width), f32),
            pltpu.VMEM((rows, 1), f32),
            pltpu.VMEM((clips, joint), f32),
            pltpu.VMEM((clips, 1), f32),
            jax.ShapeDtypeStruct((clips, joint), bf16),
        ],
        compiler_params=pltpu.CompilerParams(vmem_limit_bytes=24 * MIB),
        cost_estimate=pl.CostEstimate(
            flops=2 * rows * width * hidden.shape[1], bytes_accessed=4 * MIB, transcendentals=0
        ),
        name="embed",
    )(inputs, hidden, in_vmem(second_weight), projection)


MASKS = (1, 8, 16, 2, 4)


def gather_step(held, mask):
    return jnp.concatenate([held, move_across(held, mask)])


def gather_clips(shard):
    for mask in MASKS[:-1]:
        shard = gather_step(shard, mask)
    return [shard, move_across(shard, MASKS[-1])]


def groups_by_distance(pool_group, clips):
    order = [0]
    for mask in MASKS:
        order = order + [o ^ mask for o in order]
    replica = lax.axis_index("replica")
    groups = pool_group[jnp.bitwise_xor(replica, jnp.array(order, jnp.int32))]
    return jnp.broadcast_to(groups[:, None], (len(order), clips)).reshape(1, -1).astype(f32)


def loss_kernel(group_ref, *refs):
    audio_refs, text_refs = refs[:2], refs[2:4]
    projection_ref, normed_ref, inv_ref, unit_ref, inv_norm_ref, out_ref = refs[4:]
    clips = unit_ref.shape[0]
    rows = normed_ref.shape[0]
    audio = jnp.concatenate([r[...] for r in audio_refs], axis=0)
    text = jnp.concatenate([r[...] for r in text_refs], axis=0)
    scores = lax.dot_general(audio, text, LAST_DIMS, preferred_element_type=f32) * inv_temp
    groups = jnp.broadcast_to(group_ref[...], scores.shape)
    weighted = jnp.where(groups == groups.T, jnp.exp(scores), 0.0)
    by_cols = weighted[:clips] / jnp.sum(weighted, axis=0, keepdims=True)
    by_rows = weighted[:clips] / jnp.sum(weighted[:clips], axis=1, keepdims=True)
    shape = by_rows.shape
    own = lax.broadcasted_iota(jnp.int32, shape, 0) == lax.broadcasted_iota(jnp.int32, shape, 1)
    coeffs = grad_scale * (by_rows + by_cols - jnp.where(own, 2.0, 0.0))
    audio_grad = (
        jnp.dot(coeffs, text.astype(f32), precision=EXACT, preferred_element_type=f32) * inv_temp
    )
    unit = unit_ref[...]
    emb_grad = (
        audio_grad - unit * jnp.sum(unit * audio_grad, axis=-1, keepdims=True)
    ) * inv_norm_ref[...]
    pooled_grad = lax.dot_general(
        emb_grad,
        projection_ref[...].astype(f32),
        LAST_DIMS,
        precision=EXACT,
        preferred_element_type=f32,
    ) * (1.0 / (rows // clips))
    upstream = lax.dot_general(
        clip_rows(rows, clips),
        pooled_grad,
        (((0,), (0,)), ((), ())),
        precision=EXACT,
        preferred_element_type=f32,
    )
    normed = normed_ref[...]
    mean = jnp.mean(upstream, axis=-1, keepdims=True)
    along = jnp.mean(upstream * normed, axis=-1, keepdims=True)
    grad = (inv_ref[...] * (upstream - mean - normed * along)).astype(bf16)
    per_micro = out_ref.shape[1]
    for m in range(out_ref.shape[0]):
        out_ref[m] = grad[m * per_micro : (m + 1) * per_micro]


def loss_grad(groups, audio, text, projection, normed, inv_std, unit, inv_norm):
    rows, width = normed.shape
    operands = [groups, *audio, *text, projection]
    return pl.pallas_call(
        loss_kernel,
        in_specs=[VMEM_SPEC] * (len(operands) + 4),
        out_specs=VMEM_SPEC,
        out_shape=pltpu.VMEM((MICRO, rows // MICRO, width), bf16),
        compiler_params=pltpu.CompilerParams(vmem_limit_bytes=24 * MIB),
        name="loss_grad",
    )(*operands, *[in_vmem(a) for a in (normed, inv_std, unit, inv_norm)])


def step_kernel(inputs_given, keeps, slot, last_section, section_ref, second_ref, first_ref, slope_ref, normed_ref, inv_ref, *rest):
    count = len(inputs_given)
    given, stores = rest[:count], rest[count : count + 3]
    if keeps:
        passed_ref, out_ref, pre_ref, in_ref = rest[count + 3 :]
    else:
        out_ref, pre_ref, in_ref = rest[count + 3 :]
    section = section_ref[0]
    micro_id = slot - 2 * (last_section - section)
    active = (micro_id >= 0) & (micro_id < MICRO)
    micro = jnp.clip(micro_id, 0, MICRO - 1)

    @pl.when(active)
    def _():
        if count == 2:
            upstream = jnp.where(section == last_section, given[0][micro], given[1][...])
        elif inputs_given[0] == "last":
            upstream = given[0][micro]
        else:
            upstream = given[0][...]
        act_grad = lax.dot_general(
            upstream, second_ref[...], LAST_DIMS, preferred_element_type=f32
        )
        pre_grad = (act_grad * slope_ref[micro]).astype(bf16)
        normed_grad = lax.dot_general(
            pre_grad, first_ref[...], LAST_DIMS, preferred_element_type=f32
        )
        normed = normed_ref[micro].astype(f32)
        mean = jnp.mean(normed_grad, axis=-1, keepdims=True)
        along = jnp.mean(normed_grad * normed, axis=-1, keepdims=True)
        in_grad = upstream.astype(f32) + inv_ref[micro] * (normed_grad - mean - normed * along)
        in_grad = in_grad.astype(bf16)
        if keeps:
            passed_ref[...] = in_grad
            pre_ref[micro] = pre_grad
            out_ref[micro] = upstream
            in_ref[micro] = in_grad
        else:
            pre_ref[...] = pre_grad
            out_ref[...] = upstream
            in_ref[...] = in_grad

    if not keeps:

        @pl.when(jnp.logical_not(active))
        def _():
            for store, last in zip(stores, (out_ref, pre_ref, in_ref)):
                last[...] = store[MICRO - 1]


def chain_step(slot, last_section, section, weights, fixed, given, stores, keeps):
    rows, width = fixed[1].shape[1:]
    wide = fixed[0].shape[2]
    names = tuple(given)
    values = [in_vmem(given[n]) if n == "last" else given[n] for n in names]
    first_store = 1 + 5 + len(names)
    if keeps:
        shapes = [jax.ShapeDtypeStruct((rows, width), bf16)]
        shapes += [pltpu.VMEM(a.shape, a.dtype) for a in stores]
        aliases = {first_store + i: 1 + i for i in range(3)}
    else:
        shapes = [jax.ShapeDtypeStruct((rows, n), bf16) for n in (width, wide, width)]
        aliases = {}
    return pl.pallas_call(
        functools.partial(step_kernel, names, keeps, slot, last_section),
        in_specs=[SMEM_SPEC] + [VMEM_SPEC] * (5 + len(names) + 3),
        out_specs=[VMEM_SPEC] * len(shapes),
        out_shape=shapes,
        input_output_aliases=aliases,
        compiler_params=pltpu.CompilerParams(vmem_limit_bytes=16 * MIB),
        cost_estimate=pl.CostEstimate(
            flops=4 * rows * width * wide, bytes_accessed=8 * MIB, transcendentals=0
        ),
        name="chain_step",
    )(
        section,
        *[in_vmem(w) for w in weights],
        *[in_vmem(a) for a in fixed],
        *values,
        *[in_vmem(a) for a in stores],
    )


def empty_stores(shapes):
    return pl.pallas_call(
        lambda *refs: None,
        out_specs=[VMEM_SPEC] * len(shapes),
        out_shape=[pltpu.VMEM(s, bf16) for s in shapes],
        compiler_params=pltpu.CompilerParams(vmem_limit_bytes=MIB),
        name="empty_stores",
    )()


def column_halves(turned, at):
    width, rows = turned.shape
    blocks = turned.reshape(HI, COL, CORE, width // (HI * COL * CORE), rows)
    return item_at(blocks, at["core"], 2), item_at(blocks, at["other"], 2)


LOW, HIGH = slice(0, HI // 2), slice(HI // 2, HI)


def term_of(left, right, at, distance, part=slice(None)):
    chosen = item_at(left[part], at["columns"][distance], 1)
    height, rows = chosen.shape[1:]
    product = jnp.dot(chosen.reshape(-1, rows), right, preferred_element_type=f32)
    return product.reshape(-1, height, right.shape[1])


def scatter_total(own, ahead, back):
    return jnp.concatenate(
        [
            own[part] + a.astype(f32) + b.astype(f32)
            for part, a, b in zip((LOW, HIGH), ahead, back)
        ]
    )


def scatter_planes(total, at):
    rounded = total.astype(bf16)
    return [move(item_at(rounded, at["hi"][d]), hi=d) for d in (1, 2, 3)]


def scatter_end(total, got, at):
    result = item_at(total, at["hi"][0])
    for block in got:
        result = result + block.astype(f32)
    return result / (HI * COL * CORE)


def paired_texts(text_embed, pair_label):
    texts = text_embed.astype(f32)
    unit_text = texts * lax.rsqrt(jnp.sum(texts * texts, axis=-1, keepdims=True) + eps_unit)
    slots = pair_label.shape[1]
    unit_text = unit_text.reshape(-1, slots, unit_text.shape[1])
    chooser = (pair_label[:, :, None] == jnp.arange(slots, dtype=jnp.int32)[None, None, :]).astype(f32)
    chosen = jnp.einsum("mcj,mje->mce", chooser, unit_text, precision=EXACT)
    return chosen.reshape(-1, chosen.shape[2])


def local(section_inputs, in_weight, out_weight, projection, text_embed, pair_label, pool_group):
    inputs = section_inputs[0]
    row_count, width = inputs.shape
    per_micro = row_count // MICRO
    clips = row_count // FRAMES
    wide = in_weight.shape[2]
    half = wide // CORE
    section_count = lax.axis_size("section")
    hi, col, core = place()
    at = dict(
        hi=[(hi + d) & (HI - 1) for d in range(HI)],
        first_hi=HI - 1 - hi,
        col=col,
        core=core,
        other=1 - core,
        chip=jnp.stack([col, core]).astype(jnp.int32),
        section=jnp.full((1,), lax.axis_index("section"), jnp.int32),
        columns=[(col + d) & (COL - 1) for d in range(COL)],
        kept=core * half,
        given=(1 - core) * half,
    )
    at = lax.optimization_barrier(at)

    shard = in_weight[0]
    kept = slice_at(shard, at["kept"], half, 1)
    got = move(slice_at(shard, at["given"], half, 1), core=1)
    first_shard = jnp.where(
        at["core"] == 0, jnp.concatenate([kept, got]), jnp.concatenate([got, kept])
    )
    first_moved = [move(first_shard, hi=d) for d in (1, 2, 3)]
    texts = paired_texts(text_embed, pair_label).astype(bf16)
    groups = groups_by_distance(pool_group, clips)
    *first_moved, texts, groups = together(*first_moved, texts, groups)
    first_stack = in_order(first_shard, first_moved, HI, at["first_hi"])
    first_stack, second_shard = together(first_stack, out_weight[0])
    first_left, first_right = move(first_stack, col=1), move(first_stack, col=-1)
    second_moved = [move(second_shard, hi=d) for d in (1, 2, 3)]
    for mask in MASKS[:2]:
        texts = gather_step(texts, mask)
    first_left, first_right, texts = together(first_left, first_right, texts)
    first_far = move(first_left, col=1)
    *second_moved, first_right = together(*second_moved, first_right)
    second_stack = in_order(second_shard, second_moved, HI, at["first_hi"])
    second_right = move(second_stack, col=-1)
    texts = gather_step(texts, MASKS[2])
    first_far, texts, second_sent = together(first_far, texts, second_stack)
    second_left = move(second_sent, col=1)
    second_far = move(second_right, col=-1)
    texts = gather_step(texts, MASKS[3])

    near_plan = [(0, d, o) for d in (0, COL - 1, 1) for o in (False, True)]
    far_plan = [(0, 2, o) for o in (False, True)]

    def both(*blocks):
        return [piece for b in blocks for piece in (b, move(b, core=1))]

    first_weight = place_blocks(
        at["chip"], near_plan, both(first_stack, first_left, first_right), (width, wide), True
    )
    first_weight = place_blocks(
        at["chip"], far_plan, both(first_far), (width, wide), True, first_weight
    )
    second_weight = place_blocks(
        at["chip"],
        [near_plan[i] for i in (0, 1, 4, 5)],
        both(second_stack, second_right),
        (wide, width),
        False,
    )
    normed, inv_in, normed_t, hidden, hidden_t, slope = front(
        inputs, first_weight, second_weight
    )
    normed_halves = column_halves(normed_t, at)
    hidden_halves = column_halves(hidden_t, at)
    second_weight = place_blocks(
        at["chip"],
        [near_plan[2], near_plan[3]] + far_plan,
        both(second_left, second_far),
        (wide, width),
        False,
        second_weight,
    )
    text_all = [texts, move_across(texts, MASKS[4])]
    out_normed, out_inv, unit, inv_norm, sent = embed(
        inputs, hidden, second_weight, projection
    )
    audio_all = gather_clips(sent)
    last_micro = loss_grad(
        groups, audio_all, text_all, projection, out_normed, out_inv, unit, inv_norm
    )

    normed_columns, hidden_columns = (
        jnp.concatenate([own, move(other, core=1)], axis=-1)
        for own, other in (normed_halves, hidden_halves)
    )
    fixed = (slope, normed, inv_in)
    weights = (second_weight, first_weight)
    stores = empty_stores([(MICRO, per_micro, n) for n in (width, wide, width)])
    arrived = [None, None]
    slots = 2 * (section_count - 1) + MICRO
    for slot in range(slots):
        given = {}
        if slot == slots - 6:
            arrived[slot], normed_columns, hidden_columns = together(
                arrived[slot], normed_columns, hidden_columns
            )
        if slot == slots - 1:
            early = [a[: MICRO - 1].reshape(-1, a.shape[2]) for a in stores]
            arrived[slot], *early = together(arrived[slot], *early)
            crossed = [move(a, core=1) for a in early[:2]]
        if slot < MICRO:
            given["last"] = last_micro
        if arrived[slot] is not None:
            given["next"] = arrived[slot]
        keeps = slot < slots - 1
        results = chain_step(
            slot, section_count - 1, at["section"], weights, fixed, given, stores, keeps
        )
        if not keeps:
            last_out, last_pre, last_in = results
            break
        passed, *stores = results
        route = [
            (s, s - 1)
            for s in range(1, section_count)
            if 0 <= slot - 2 * (section_count - 1 - s) < MICRO
        ]
        arrived.append(lax.ppermute(passed, "section", route) if route else None)

    out_rows, pre_rows = (
        jnp.concatenate([own, last, other, move(last, core=1)])
        for own, last, other in zip(early, (last_out, last_pre), crossed)
    )

    def term(second, distance, part=slice(None)):
        left, right = (hidden_columns, out_rows) if second else (normed_columns, pre_rows)
        return term_of(left, right, at, distance, part)

    def far(second):
        low, high = term(second, 2, LOW).astype(bf16), term(second, 2, HIGH).astype(bf16)
        return move(low, col=1), move(high, col=-1)

    def near_free(second):
        ahead, back = term(second, 1, HIGH).astype(bf16), term(second, 3, LOW).astype(bf16)
        return move(ahead, col=1), move(back, col=-1)

    def near_summed(second, low, high):
        ahead = (term(second, 1, LOW) + low.astype(f32)).astype(bf16)
        back = (term(second, 3, HIGH) + high.astype(f32)).astype(bf16)
        return move(ahead, col=1), move(back, col=-1)

    low2, high2 = far(True)
    ahead_high2, back_low2 = near_free(True)
    low1, high1 = far(False)
    ahead_low2, back_high2 = near_summed(True, low2, high2)
    ahead_high1, back_low1 = near_free(False)
    ahead_low1, back_high1 = near_summed(False, low1, high1)
    second_total = scatter_total(
        term(True, 0), (ahead_low2, ahead_high2), (back_low2, back_high2)
    )
    second_got = scatter_planes(second_total, at)
    *second_got, ahead_low1, ahead_high1, back_low1, back_high1 = together(
        *second_got, ahead_low1, ahead_high1, back_low1, back_high1
    )
    first_total = scatter_total(
        term(False, 0), (ahead_low1, ahead_high1), (back_low1, back_high1)
    )
    first_got = scatter_planes(first_total, at)
    second_sum = scatter_end(second_total, second_got, at)
    first_sum = scatter_end(first_total, first_got, at)
    in_grads = jnp.concatenate([early[2], last_in])
    return (in_grads[None], first_sum[None], second_sum[None])


def solution(mesh):
    return jax.shard_map(
        local,
        mesh=mesh,
        in_specs=(
            P("section", "replica", None),
            P("section", "replica", None),
            P("section", "replica", None),
            P(),
            P("replica", None),
            P("replica", None),
            P(),
        ),
        out_specs=(
            P("section", "replica", None),
            P("section", "replica", None),
            P("section", "replica", None),
        ),
        check_vma=False,
    )
```

```python
import functools

import jax
import jax.numpy as jnp
from jax import lax
from jax.experimental import pallas as pl
from jax.experimental.pallas import tpu as pltpu
from jax.sharding import PartitionSpec as P

MICRO = 4
FRAMES = 44

HI = 4
COL = 4
CORE = 2

MIB = 2**20
LAST_DIMS = (((1,), (1,)), ((), ()))
EXACT = lax.Precision.HIGHEST

eps_norm = 1e-05
eps_unit = 1e-06
inv_temp = 1.0 / 0.07
grad_scale = 256.0
sqrt_half = 0.7071067811865476
inv_sqrt_two_pi = 0.3989422804014327

bf16 = jnp.bfloat16
f32 = jnp.float32


def replica_of(hi, col, core):
    return ((hi % HI) * COL + col % COL) * CORE + core % CORE


def move(block, hi=0, col=0, core=0):
    route = [
        (replica_of(h, c, k), replica_of(h + hi, c + col, k + core))
        for h in range(HI)
        for c in range(COL)
        for k in range(CORE)
    ]
    return lax.ppermute(block, "replica", route)


def place():
    replica = lax.axis_index("replica")
    return replica >> 3, (replica >> 1) & (COL - 1), replica & (CORE - 1)


def together(*values):
    return lax.optimization_barrier(values)


def move_across(block, mask):
    count = HI * COL * CORE
    return lax.ppermute(block, "replica", [(r, r ^ mask) for r in range(count)])


def slice_at(values, start, size, axis):
    return lax.dynamic_slice_in_dim(values, start, size, axis, allow_negative_indices=False)


def item_at(values, index, axis=0):
    return lax.dynamic_index_in_dim(
        values, index, axis, keepdims=False, allow_negative_indices=False
    )


def in_vmem(value):
    return pltpu.with_memory_space_constraint(value, pltpu.VMEM)


VMEM_SPEC = pl.BlockSpec(memory_space=pltpu.VMEM)
ANY_SPEC = pl.BlockSpec(memory_space=pl.ANY)
SMEM_SPEC = pl.BlockSpec(memory_space=pltpu.SMEM)


def place_kernel(plan, by_columns, info, *refs):
    pieces, whole = refs[: len(plan)], refs[-1]
    hi, col, core = info[0], info[1], info[2]
    for (distance, other, blocks), piece in zip(plan, pieces):
        rows, width = piece.shape[1:]
        at_col = (col + distance) & (COL - 1)
        side = 1 - core if other else core
        for k, back in blocks:
            chip = ((hi + HI - back) & (HI - 1)) * COL + at_col
            if by_columns:
                row = chip * rows
                column = pl.ds(pl.multiple_of(side * width, width), width)
            else:
                row = (chip * CORE + side) * rows
                column = slice(None)
            whole[pl.ds(pl.multiple_of(row, 16), rows), column] = piece[k]


def place_blocks(info, plan, pieces, shape, by_columns, whole=None):
    return pl.pallas_call(
        functools.partial(place_kernel, plan, by_columns),
        in_specs=[SMEM_SPEC]
        + [VMEM_SPEC] * len(pieces)
        + ([] if whole is None else [VMEM_SPEC]),
        out_specs=VMEM_SPEC,
        out_shape=pltpu.VMEM(shape, bf16),
        input_output_aliases={} if whole is None else {1 + len(pieces): 0},
        compiler_params=pltpu.CompilerParams(vmem_limit_bytes=12 * MIB),
        cost_estimate=pl.CostEstimate(
            flops=0, bytes_accessed=2 * sum(p.size for p in pieces), transcendentals=0
        ),
        name="place_blocks",
    )(info, *pieces, *([] if whole is None else [in_vmem(whole)]))


def front_kernel(
    inputs_ref, first_ref, waits_ref, normed_ref, inv_ref, normed_t_ref, hidden_ref, hidden_t_ref, slope_ref
):
    micro, rows = normed_ref.shape[:2]
    values = inputs_ref[...].astype(f32)
    centred = values - jnp.mean(values, axis=-1, keepdims=True)
    inv_std = lax.rsqrt(jnp.mean(centred * centred, axis=-1, keepdims=True) + eps_norm)
    scaled = centred * inv_std
    normed = scaled.astype(bf16)
    for m in range(micro):
        normed_ref[m] = normed[m * rows : (m + 1) * rows]
        inv_ref[m] = inv_std[m * rows : (m + 1) * rows]
    normed_t_ref[...] = scaled.T.astype(bf16)
    step = 256

    @pl.loop(0, first_ref.shape[1] // step)
    def _(j):
        part = pl.ds(pl.multiple_of(j * step, step), step)
        preact = jnp.dot(normed, first_ref[:, part], preferred_element_type=f32)
        cdf = 0.5 * (1.0 + lax.erf(preact * sqrt_half))
        hidden = preact * cdf
        hidden_ref[:, part] = hidden.astype(bf16)
        hidden_t_ref[part, :] = hidden.T.astype(bf16)
        slope = cdf + preact * jnp.exp(-0.5 * preact * preact) * inv_sqrt_two_pi
        for m in range(micro):
            slope_ref[m, :, part] = slope[m * rows : (m + 1) * rows]


def front(inputs, first_weight, waits):
    rows, width = inputs.shape
    wide = first_weight.shape[1]
    per_micro = rows // MICRO
    return pl.pallas_call(
        front_kernel,
        in_specs=[VMEM_SPEC] * 3,
        out_specs=[VMEM_SPEC] * 6,
        out_shape=[
            pltpu.VMEM((MICRO, per_micro, width), bf16),
            pltpu.VMEM((MICRO, per_micro, 1), f32),
            jax.ShapeDtypeStruct((width, rows), bf16),
            jax.ShapeDtypeStruct((rows, wide), bf16),
            jax.ShapeDtypeStruct((wide, rows), bf16),
            pltpu.VMEM((MICRO, per_micro, wide), f32),
        ],
        compiler_params=pltpu.CompilerParams(vmem_limit_bytes=24 * MIB),
        cost_estimate=pl.CostEstimate(
            flops=2 * rows * width * wide, bytes_accessed=4 * MIB, transcendentals=0
        ),
        name="front",
    )(inputs, in_vmem(first_weight), in_vmem(waits))


def clip_rows(rows, clips):
    first = lax.broadcasted_iota(jnp.int32, (clips, rows), 0) * (rows // clips)
    row = lax.broadcasted_iota(jnp.int32, (clips, rows), 1)
    return jnp.where((row >= first) & (row < first + rows // clips), 1.0, 0.0).astype(f32)


def embed_kernel(
    info,
    inputs_ref,
    hidden_ref,
    second_ref,
    projection_ref,
    text_ref,
    group_ref,
    normed_ref,
    inv_ref,
    unit_ref,
    inv_norm_ref,
    weighted_ref,
    sums_ref,
    unit_text_ref,
):
    rows = inputs_ref.shape[0]
    clips = unit_ref.shape[0]
    block_out = inputs_ref[...].astype(f32) + jnp.dot(
        hidden_ref[...], second_ref[...], preferred_element_type=f32
    )
    centred = block_out - jnp.mean(block_out, axis=-1, keepdims=True)
    inv_std = lax.rsqrt(jnp.mean(centred * centred, axis=-1, keepdims=True) + eps_norm)
    normed = centred * inv_std
    normed_ref[...] = normed
    inv_ref[...] = inv_std
    sums = jnp.dot(
        clip_rows(rows, clips), normed, precision=EXACT, preferred_element_type=f32
    )
    pooled = (sums * (1.0 / (rows // clips))).astype(bf16)
    embedded = jnp.dot(pooled, projection_ref[...], preferred_element_type=f32)
    inv_norm = lax.rsqrt(jnp.sum(embedded * embedded, axis=-1, keepdims=True) + eps_unit)
    unit = embedded * inv_norm
    unit_ref[...] = unit
    inv_norm_ref[...] = inv_norm
    text = text_ref[...].astype(f32)
    unit_text = text * lax.rsqrt(jnp.sum(text * text, axis=-1, keepdims=True) + eps_unit)
    unit_text = unit_text.astype(bf16)
    unit_text_ref[...] = unit_text
    scores = (
        lax.dot_general(
            unit.astype(bf16), unit_text, LAST_DIMS, preferred_element_type=f32
        )
        * inv_temp
    )
    group = group_ref[...]
    column = lax.broadcasted_iota(jnp.int32, group.shape, 1)
    own_group = jnp.sum(
        jnp.where(column == info[3] * clips, group, 0.0), axis=1, keepdims=True
    )
    weighted = jnp.where(group == own_group, jnp.exp(scores), 0.0)
    weighted_ref[...] = weighted
    sums_ref[...] = jnp.sum(weighted, axis=0, keepdims=True)


def embed(info, inputs, hidden, second_weight, projection, text, groups):
    rows, width = inputs.shape
    clips = rows // FRAMES
    joint = projection.shape[1]
    total = text.shape[0]
    return pl.pallas_call(
        embed_kernel,
        in_specs=[SMEM_SPEC] + [VMEM_SPEC] * 6,
        out_specs=[VMEM_SPEC] * 7,
        out_shape=[
            pltpu.VMEM((rows, width), f32),
            pltpu.VMEM((rows, 1), f32),
            pltpu.VMEM((clips, joint), f32),
            pltpu.VMEM((clips, 1), f32),
            pltpu.VMEM((clips, total), f32),
            jax.ShapeDtypeStruct((1, total), f32),
            pltpu.VMEM((total, joint), bf16),
        ],
        compiler_params=pltpu.CompilerParams(vmem_limit_bytes=24 * MIB),
        cost_estimate=pl.CostEstimate(
            flops=2 * rows * width * hidden.shape[1], bytes_accessed=4 * MIB, transcendentals=0
        ),
        name="embed",
    )(info, inputs, hidden, in_vmem(second_weight), projection, text, groups)


MASKS = (1, 8, 16, 2, 4)


def gather_step(held, mask, later):
    moved = move_across(held, mask)
    return jnp.where(
        later, jnp.concatenate([moved, held]), jnp.concatenate([held, moved])
    )


def sum_over_replicas(values):
    for mask in MASKS:
        values = values + move_across(values, mask)
    return values


def loss_kernel(
    info,
    sums_ref,
    text_ref,
    projection_ref,
    normed_ref,
    inv_ref,
    unit_ref,
    inv_norm_ref,
    weighted_ref,
    out_ref,
):
    clips = unit_ref.shape[0]
    rows = normed_ref.shape[0]
    text = text_ref[...]
    weighted = weighted_ref[...]
    by_cols = weighted / sums_ref[...]
    by_rows = weighted / jnp.sum(weighted, axis=1, keepdims=True)
    shape = by_rows.shape
    own = (
        lax.broadcasted_iota(jnp.int32, shape, 0) + info[3] * clips
        == lax.broadcasted_iota(jnp.int32, shape, 1)
    )
    coeffs = grad_scale * (by_rows + by_cols - jnp.where(own, 2.0, 0.0))
    audio_grad = (
        jnp.dot(coeffs, text.astype(f32), precision=EXACT, preferred_element_type=f32) * inv_temp
    )
    unit = unit_ref[...]
    emb_grad = (
        audio_grad - unit * jnp.sum(unit * audio_grad, axis=-1, keepdims=True)
    ) * inv_norm_ref[...]
    pooled_grad = lax.dot_general(
        emb_grad,
        projection_ref[...].astype(f32),
        LAST_DIMS,
        precision=EXACT,
        preferred_element_type=f32,
    ) * (1.0 / (rows // clips))
    upstream = lax.dot_general(
        clip_rows(rows, clips),
        pooled_grad,
        (((0,), (0,)), ((), ())),
        precision=EXACT,
        preferred_element_type=f32,
    )
    normed = normed_ref[...]
    mean = jnp.mean(upstream, axis=-1, keepdims=True)
    along = jnp.mean(upstream * normed, axis=-1, keepdims=True)
    grad = (inv_ref[...] * (upstream - mean - normed * along)).astype(bf16)
    per_micro = out_ref.shape[1]
    for m in range(out_ref.shape[0]):
        out_ref[m] = grad[m * per_micro : (m + 1) * per_micro]


def loss_grad(info, sums, text, projection, normed, inv_std, unit, inv_norm, weighted):
    rows, width = normed.shape
    return pl.pallas_call(
        loss_kernel,
        in_specs=[SMEM_SPEC] + [VMEM_SPEC] * 8,
        out_specs=VMEM_SPEC,
        out_shape=pltpu.VMEM((MICRO, rows // MICRO, width), bf16),
        compiler_params=pltpu.CompilerParams(vmem_limit_bytes=24 * MIB),
        name="loss_grad",
    )(
        info,
        sums,
        in_vmem(text),
        projection,
        *[in_vmem(a) for a in (normed, inv_std, unit, inv_norm, weighted)],
    )


def step_kernel(inputs_given, keeps, slot, last_section, section_ref, second_ref, first_ref, slope_ref, normed_ref, inv_ref, *rest):
    count = len(inputs_given)
    given, stores = rest[:count], rest[count : count + 3]
    if keeps:
        passed_ref, out_ref, pre_ref, in_ref = rest[count + 3 :]
    else:
        out_ref, pre_ref, in_ref = rest[count + 3 :]
    section = section_ref[0]
    micro_id = slot - 2 * (last_section - section)
    active = (micro_id >= 0) & (micro_id < MICRO)
    micro = jnp.clip(micro_id, 0, MICRO - 1)

    @pl.when(active)
    def _():
        if count == 2:
            upstream = jnp.where(section == last_section, given[0][micro], given[1][...])
        elif inputs_given[0] == "last":
            upstream = given[0][micro]
        else:
            upstream = given[0][...]
        act_grad = lax.dot_general(
            upstream, second_ref[...], LAST_DIMS, preferred_element_type=f32
        )
        pre_grad = (act_grad * slope_ref[micro]).astype(bf16)
        normed_grad = lax.dot_general(
            pre_grad, first_ref[...], LAST_DIMS, preferred_element_type=f32
        )
        normed = normed_ref[micro].astype(f32)
        mean = jnp.mean(normed_grad, axis=-1, keepdims=True)
        along = jnp.mean(normed_grad * normed, axis=-1, keepdims=True)
        in_grad = upstream.astype(f32) + inv_ref[micro] * (normed_grad - mean - normed * along)
        in_grad = in_grad.astype(bf16)
        if keeps:
            passed_ref[...] = in_grad
            pre_ref[micro] = pre_grad
            out_ref[micro] = upstream
            in_ref[micro] = in_grad
        else:
            pre_ref[...] = pre_grad
            out_ref[...] = upstream
            in_ref[...] = in_grad

    if not keeps:

        @pl.when(jnp.logical_not(active))
        def _():
            for store, last in zip(stores, (out_ref, pre_ref, in_ref)):
                last[...] = store[MICRO - 1]


def chain_step(slot, last_section, section, weights, fixed, given, stores, keeps):
    rows, width = fixed[1].shape[1:]
    wide = fixed[0].shape[2]
    names = tuple(given)
    values = [in_vmem(given[n]) if n == "last" else given[n] for n in names]
    first_store = 1 + 5 + len(names)
    if keeps:
        shapes = [jax.ShapeDtypeStruct((rows, width), bf16)]
        shapes += [pltpu.VMEM(a.shape, a.dtype) for a in stores]
        aliases = {first_store + i: 1 + i for i in range(3)}
    else:
        shapes = [jax.ShapeDtypeStruct((rows, n), bf16) for n in (width, wide, width)]
        aliases = {}
    return pl.pallas_call(
        functools.partial(step_kernel, names, keeps, slot, last_section),
        in_specs=[SMEM_SPEC] + [VMEM_SPEC] * (5 + len(names) + 3),
        out_specs=[VMEM_SPEC] * len(shapes),
        out_shape=shapes,
        input_output_aliases=aliases,
        compiler_params=pltpu.CompilerParams(vmem_limit_bytes=16 * MIB),
        cost_estimate=pl.CostEstimate(
            flops=4 * rows * width * wide, bytes_accessed=8 * MIB, transcendentals=0
        ),
        name="chain_step",
    )(
        section,
        *[in_vmem(w) for w in weights],
        *[in_vmem(a) for a in fixed],
        *values,
        *[in_vmem(a) for a in stores],
    )


def empty_stores(shapes):
    return pl.pallas_call(
        lambda *refs: None,
        out_specs=[VMEM_SPEC] * len(shapes),
        out_shape=[pltpu.VMEM(s, bf16) for s in shapes],
        compiler_params=pltpu.CompilerParams(vmem_limit_bytes=MIB),
        name="empty_stores",
    )()


def column_halves(turned, at):
    width, rows = turned.shape
    blocks = turned.reshape(HI, COL, CORE, width // (HI * COL * CORE), rows)
    return item_at(blocks, at["core"], 2), item_at(blocks, at["other"], 2)


LOW, HIGH = slice(0, HI // 2), slice(HI // 2, HI)


def term_of(left, right, at, distance, part=slice(None)):
    chosen = item_at(left[part], at["columns"][distance], 1)
    height, rows = chosen.shape[1:]
    product = jnp.dot(chosen.reshape(-1, rows), right, preferred_element_type=f32)
    return product.reshape(-1, height, right.shape[1])


def scatter_total(own, ahead, back):
    return jnp.concatenate(
        [
            own[part] + a.astype(f32) + b.astype(f32)
            for part, a, b in zip((LOW, HIGH), ahead, back)
        ]
    )


def scatter_planes(total, at):
    rounded = total.astype(bf16)
    return [move(item_at(rounded, at["hi"][d]), hi=d) for d in (1, 2, 3)]


def scatter_end(total, got, at):
    result = item_at(total, at["hi"][0])
    for block in got:
        result = result + block.astype(f32)
    return result / (HI * COL * CORE)


def pick_kernel(label_ref, text_ref, out_ref):
    text = text_ref[...].astype(f32)
    row = lax.broadcasted_iota(jnp.int32, text.shape, 0)
    label = jnp.zeros(text.shape, jnp.int32)
    for i in range(text.shape[0]):
        label = jnp.where(row == i, label_ref[i // 2, i % 2], label)
    below = jnp.concatenate([text[1:], text[:1]])
    above = jnp.concatenate([text[-1:], text[:-1]])
    slot = row & 1
    other = jnp.where(slot == 0, below, above)
    out_ref[...] = jnp.where(label == slot, text, other).astype(bf16)


def paired_texts(text_embed, pair_label):
    return pl.pallas_call(
        pick_kernel,
        in_specs=[SMEM_SPEC, VMEM_SPEC],
        out_specs=VMEM_SPEC,
        out_shape=jax.ShapeDtypeStruct(text_embed.shape, bf16),
        compiler_params=pltpu.CompilerParams(vmem_limit_bytes=MIB),
        name="paired_texts",
    )(pair_label, text_embed)


def local(section_inputs, in_weight, out_weight, projection, text_embed, pair_label, pool_group):
    inputs = section_inputs[0]
    row_count, width = inputs.shape
    per_micro = row_count // MICRO
    clips = row_count // FRAMES
    wide = in_weight.shape[2]
    half = wide // CORE
    section_count = lax.axis_size("section")
    hi, col, core = place()
    at = dict(
        hi=[(hi + d) & (HI - 1) for d in range(HI)],
        core=core,
        other=1 - core,
        chip=jnp.stack([hi, col, core, (col * HI + hi) * CORE + core]).astype(jnp.int32),
        later=[lax.axis_index("replica") & mask != 0 for mask in MASKS],
        section=jnp.full((1,), lax.axis_index("section"), jnp.int32),
        columns=[(col + d) & (COL - 1) for d in range(COL)],
        kept=core * half,
        given=(1 - core) * half,
    )
    at = lax.optimization_barrier(at)

    shard = in_weight[0]
    kept = slice_at(shard, at["kept"], half, 1)
    got = move(slice_at(shard, at["given"], half, 1), core=1)
    first_shard = jnp.where(
        at["core"] == 0, jnp.concatenate([kept, got]), jnp.concatenate([got, kept])
    )
    second_shard = out_weight[0]

    def gathered(texts, step):
        return gather_step(texts, MASKS[step], at["later"][step])

    own = jnp.stack([first_shard, second_shard])
    moved = [move(own, hi=d) for d in (1, 2, 3)]
    own_left, own_right = move(own, col=1), move(own, col=-1)
    own, text_embed, pair_label, pool_group = together(
        own, text_embed, pair_label, pool_group
    )
    texts = paired_texts(text_embed, pair_label)
    groups = pool_group.reshape(HI, COL, CORE).transpose(1, 0, 2).reshape(-1, 1)
    groups = jnp.broadcast_to(groups, (groups.shape[0], clips))
    groups = groups.reshape(1, -1).astype(f32)
    texts = gathered(texts, 0)
    *moved, texts, groups, own_left, own_right = together(
        *moved, texts, groups, own_left, own_right
    )
    first_stack = jnp.stack([m[0] for m in moved])
    second_stack = jnp.stack([m[1] for m in moved])
    first_left, first_right = move(first_stack, col=1), move(first_stack, col=-1)
    second_left, second_right = move(second_stack, col=1), move(second_stack, col=-1)
    first_own_far = move(own_left[:1], col=1)
    second_own_far = move(own_right[1:], col=-1)
    texts = gathered(texts, 1)
    first_left, second_right, texts = together(first_left, second_right, texts)
    first_far = move(first_left, col=1)
    second_far = move(second_right, col=-1)
    texts = gathered(texts, 2)
    first_far, texts = together(first_far, texts)
    texts = gathered(gathered(texts, 3), 4)

    planes = ((0, 1), (1, 2), (2, 3))

    def both(*parts):
        pieces, plan = [], []
        for piece, distance, blocks in parts:
            pieces += [piece, move(piece, core=1)]
            plan += [(distance, other, blocks) for other in (False, True)]
        return plan, pieces

    own_plan, own_pieces = both(
        (own, 0, ()), (own_left, COL - 1, ()), (own_right, 1, ())
    )
    first_plan, first_pieces = both(
        (first_own_far, 2, ((0, 0),)),
        (first_stack, 0, planes),
        (first_left, COL - 1, planes),
        (first_right, 1, planes),
    )
    second_plan, second_pieces = both(
        (second_own_far, 2, ((0, 0),)),
        (second_stack, 0, planes),
        (second_right, 1, planes),
    )
    first_weight = place_blocks(
        at["chip"],
        [(d, o, ((0, 0),)) for d, o, _ in own_plan] + first_plan,
        own_pieces + first_pieces,
        (width, wide),
        True,
    )
    first_weight = place_blocks(
        at["chip"], *both((first_far, 2, planes)), (width, wide), True, first_weight
    )
    second_weight = place_blocks(
        at["chip"],
        [(d, o, ((1, 0),)) for d, o, _ in own_plan] + second_plan,
        own_pieces + second_pieces,
        (wide, width),
        False,
    )
    normed, inv_in, normed_t, hidden, hidden_t, slope = front(
        inputs, first_weight, second_weight
    )
    normed_halves = column_halves(normed_t, at)
    hidden_halves = column_halves(hidden_t, at)
    second_weight = place_blocks(
        at["chip"],
        *both((second_left, COL - 1, planes), (second_far, 2, planes)),
        (wide, width),
        False,
        second_weight,
    )

    out_normed, out_inv, unit, inv_norm, weighted, sums, unit_text = embed(
        at["chip"], inputs, hidden, second_weight, projection, texts, groups
    )
    sums = sum_over_replicas(sums)
    last_micro = loss_grad(
        at["chip"], sums, unit_text, projection, out_normed, out_inv, unit, inv_norm, weighted
    )

    normed_columns, hidden_columns = (
        jnp.concatenate([own, move(other, core=1)], axis=-1)
        for own, other in (normed_halves, hidden_halves)
    )
    fixed = (slope, normed, inv_in)
    weights = (second_weight, first_weight)
    stores = empty_stores([(MICRO, per_micro, n) for n in (width, wide, width)])
    arrived = [None, None]
    slots = 2 * (section_count - 1) + MICRO
    for slot in range(slots):
        given = {}
        if slot == slots - 6:
            arrived[slot], normed_columns, hidden_columns = together(
                arrived[slot], normed_columns, hidden_columns
            )
        if slot == slots - 1:
            early = [a[: MICRO - 1].reshape(-1, a.shape[2]) for a in stores]
            arrived[slot], *early = together(arrived[slot], *early)
            crossed = [move(a, core=1) for a in early[:2]]
        if slot < MICRO:
            given["last"] = last_micro
        if arrived[slot] is not None:
            given["next"] = arrived[slot]
        keeps = slot < slots - 1
        results = chain_step(
            slot, section_count - 1, at["section"], weights, fixed, given, stores, keeps
        )
        if not keeps:
            last_out, last_pre, last_in = results
            break
        passed, *stores = results
        route = [
            (s, s - 1)
            for s in range(1, section_count)
            if 0 <= slot - 2 * (section_count - 1 - s) < MICRO
        ]
        arrived.append(lax.ppermute(passed, "section", route) if route else None)

    out_rows, pre_rows = (
        jnp.concatenate([own, last, other, move(last, core=1)])
        for own, last, other in zip(early, (last_out, last_pre), crossed)
    )

    def term(second, distance, part=slice(None)):
        left, right = (hidden_columns, out_rows) if second else (normed_columns, pre_rows)
        return term_of(left, right, at, distance, part)

    def far(second):
        low, high = term(second, 2, LOW).astype(bf16), term(second, 2, HIGH).astype(bf16)
        return move(low, col=1), move(high, col=-1)

    def near_free(second):
        ahead, back = term(second, 1, HIGH).astype(bf16), term(second, 3, LOW).astype(bf16)
        return move(ahead, col=1), move(back, col=-1)

    def near_summed(second, low, high):
        ahead = (term(second, 1, LOW) + low.astype(f32)).astype(bf16)
        back = (term(second, 3, HIGH) + high.astype(f32)).astype(bf16)
        return move(ahead, col=1), move(back, col=-1)

    low2, high2 = far(True)
    ahead_high2, back_low2 = near_free(True)
    low1, high1 = far(False)
    ahead_low2, back_high2 = near_summed(True, low2, high2)
    ahead_high1, back_low1 = near_free(False)
    ahead_low1, back_high1 = near_summed(False, low1, high1)
    second_total = scatter_total(
        term(True, 0), (ahead_low2, ahead_high2), (back_low2, back_high2)
    )
    second_got = scatter_planes(second_total, at)
    *second_got, ahead_low1, ahead_high1, back_low1, back_high1 = together(
        *second_got, ahead_low1, ahead_high1, back_low1, back_high1
    )
    first_total = scatter_total(
        term(False, 0), (ahead_low1, ahead_high1), (back_low1, back_high1)
    )
    first_got = scatter_planes(first_total, at)
    second_sum = scatter_end(second_total, second_got, at)
    first_sum = scatter_end(first_total, first_got, at)
    in_grads = jnp.concatenate([early[2], last_in])
    return (in_grads[None], first_sum[None], second_sum[None])


def solution(mesh):
    return jax.shard_map(
        local,
        mesh=mesh,
        in_specs=(
            P("section", "replica", None),
            P("section", "replica", None),
            P("section", "replica", None),
            P(),
            P("replica", None),
            P("replica", None),
            P(),
        ),
        out_specs=(
            P("section", "replica", None),
            P("section", "replica", None),
            P("section", "replica", None),
        ),
        check_vma=False,
    )
```

```python
import functools

import jax
import jax.numpy as jnp
from jax import lax
from jax.experimental import pallas as pl
from jax.experimental.pallas import tpu as pltpu
from jax.sharding import PartitionSpec as P

MICRO = 4
FRAMES = 44

HI = 4
COL = 4
CORE = 2

MIB = 2**20
LAST_DIMS = (((1,), (1,)), ((), ()))
EXACT = lax.Precision.HIGHEST

eps_norm = 1e-05
eps_unit = 1e-06
inv_temp = 1.0 / 0.07
grad_scale = 256.0
sqrt_half = 0.7071067811865476
inv_sqrt_two_pi = 0.3989422804014327

bf16 = jnp.bfloat16
f32 = jnp.float32


def replica_of(hi, col, core):
    return ((hi % HI) * COL + col % COL) * CORE + core % CORE


def move(block, hi=0, col=0, core=0):
    route = [
        (replica_of(h, c, k), replica_of(h + hi, c + col, k + core))
        for h in range(HI)
        for c in range(COL)
        for k in range(CORE)
    ]
    return lax.ppermute(block, "replica", route)


def place():
    replica = lax.axis_index("replica")
    return replica >> 3, (replica >> 1) & (COL - 1), replica & (CORE - 1)


def together(*values):
    return lax.optimization_barrier(values)


def move_across(block, mask):
    count = HI * COL * CORE
    return lax.ppermute(block, "replica", [(r, r ^ mask) for r in range(count)])


def slice_at(values, start, size, axis):
    return lax.dynamic_slice_in_dim(values, start, size, axis, allow_negative_indices=False)


def item_at(values, index, axis=0):
    return lax.dynamic_index_in_dim(
        values, index, axis, keepdims=False, allow_negative_indices=False
    )


def in_vmem(value):
    return pltpu.with_memory_space_constraint(value, pltpu.VMEM)


VMEM_SPEC = pl.BlockSpec(memory_space=pltpu.VMEM)
ANY_SPEC = pl.BlockSpec(memory_space=pl.ANY)
SMEM_SPEC = pl.BlockSpec(memory_space=pltpu.SMEM)


def place_kernel(plan, by_columns, info, *refs):
    pieces, whole = refs[: len(plan)], refs[-1]
    hi, col, core = info[0], info[1], info[2]
    for (distance, other, blocks), piece in zip(plan, pieces):
        rows, width = piece.shape[-2:]
        at_col = (col + distance) & (COL - 1)
        side = 1 - core if other else core
        for k, back in blocks:
            chip = ((hi + HI - back) & (HI - 1)) * COL + at_col
            if by_columns:
                row = chip * rows
                column = pl.ds(pl.multiple_of(side * width, width), width)
            else:
                row = (chip * CORE + side) * rows
                column = slice(None)
            whole[pl.ds(pl.multiple_of(row, 16), rows), column] = piece[k]


def place_blocks(info, plan, pieces, shape, by_columns, whole=None):
    return pl.pallas_call(
        functools.partial(place_kernel, plan, by_columns),
        in_specs=[SMEM_SPEC]
        + [VMEM_SPEC] * len(pieces)
        + ([] if whole is None else [VMEM_SPEC]),
        out_specs=VMEM_SPEC,
        out_shape=pltpu.VMEM(shape, bf16),
        input_output_aliases={} if whole is None else {1 + len(pieces): 0},
        compiler_params=pltpu.CompilerParams(vmem_limit_bytes=12 * MIB),
        cost_estimate=pl.CostEstimate(
            flops=0, bytes_accessed=2 * sum(p.size for p in pieces), transcendentals=0
        ),
        name="place_blocks",
    )(info, *pieces, *([] if whole is None else [in_vmem(whole)]))


def front_kernel(
    inputs_ref, first_ref, waits_ref, normed_ref, inv_ref, normed_t_ref, hidden_ref, hidden_t_ref, slope_ref
):
    micro, rows = normed_ref.shape[:2]
    values = inputs_ref[...].astype(f32)
    centred = values - jnp.mean(values, axis=-1, keepdims=True)
    inv_std = lax.rsqrt(jnp.mean(centred * centred, axis=-1, keepdims=True) + eps_norm)
    scaled = centred * inv_std
    normed = scaled.astype(bf16)
    for m in range(micro):
        normed_ref[m] = normed[m * rows : (m + 1) * rows]
        inv_ref[m] = inv_std[m * rows : (m + 1) * rows]
    normed_t_ref[...] = scaled.T.astype(bf16)
    step = 256

    @pl.loop(0, first_ref.shape[1] // step)
    def _(j):
        part = pl.ds(pl.multiple_of(j * step, step), step)
        preact = jnp.dot(normed, first_ref[:, part], preferred_element_type=f32)
        cdf = 0.5 * (1.0 + lax.erf(preact * sqrt_half))
        hidden = preact * cdf
        hidden_ref[:, part] = hidden.astype(bf16)
        hidden_t_ref[part, :] = hidden.T.astype(bf16)
        slope = cdf + preact * jnp.exp(-0.5 * preact * preact) * inv_sqrt_two_pi
        for m in range(micro):
            slope_ref[m, :, part] = slope[m * rows : (m + 1) * rows]


def front(inputs, first_weight, waits):
    rows, width = inputs.shape
    wide = first_weight.shape[1]
    per_micro = rows // MICRO
    return pl.pallas_call(
        front_kernel,
        in_specs=[VMEM_SPEC] * 3,
        out_specs=[VMEM_SPEC] * 6,
        out_shape=[
            pltpu.VMEM((MICRO, per_micro, width), bf16),
            pltpu.VMEM((MICRO, per_micro, 1), f32),
            jax.ShapeDtypeStruct((width, rows), bf16),
            jax.ShapeDtypeStruct((rows, wide), bf16),
            jax.ShapeDtypeStruct((wide, rows), bf16),
            pltpu.VMEM((MICRO, per_micro, wide), f32),
        ],
        compiler_params=pltpu.CompilerParams(vmem_limit_bytes=24 * MIB),
        cost_estimate=pl.CostEstimate(
            flops=2 * rows * width * wide, bytes_accessed=4 * MIB, transcendentals=0
        ),
        name="front",
    )(inputs, in_vmem(first_weight), in_vmem(waits))


def clip_rows(rows, clips):
    first = lax.broadcasted_iota(jnp.int32, (clips, rows), 0) * (rows // clips)
    row = lax.broadcasted_iota(jnp.int32, (clips, rows), 1)
    return jnp.where((row >= first) & (row < first + rows // clips), 1.0, 0.0).astype(f32)


def embed_kernel(
    info,
    inputs_ref,
    hidden_ref,
    second_ref,
    projection_ref,
    text_ref,
    group_ref,
    normed_ref,
    inv_ref,
    unit_ref,
    inv_norm_ref,
    weighted_ref,
    sums_ref,
    unit_text_ref,
):
    rows = inputs_ref.shape[0]
    clips = unit_ref.shape[0]
    block_out = inputs_ref[...].astype(f32) + jnp.dot(
        hidden_ref[...], second_ref[...], preferred_element_type=f32
    )
    centred = block_out - jnp.mean(block_out, axis=-1, keepdims=True)
    inv_std = lax.rsqrt(jnp.mean(centred * centred, axis=-1, keepdims=True) + eps_norm)
    normed = centred * inv_std
    normed_ref[...] = normed
    inv_ref[...] = inv_std
    sums = jnp.dot(
        clip_rows(rows, clips), normed, precision=EXACT, preferred_element_type=f32
    )
    pooled = (sums * (1.0 / (rows // clips))).astype(bf16)
    embedded = jnp.dot(pooled, projection_ref[...], preferred_element_type=f32)
    inv_norm = lax.rsqrt(jnp.sum(embedded * embedded, axis=-1, keepdims=True) + eps_unit)
    unit = embedded * inv_norm
    unit_ref[...] = unit
    inv_norm_ref[...] = inv_norm
    text = text_ref[...].astype(f32)
    unit_text = text * lax.rsqrt(jnp.sum(text * text, axis=-1, keepdims=True) + eps_unit)
    unit_text = unit_text.astype(bf16)
    unit_text_ref[...] = unit_text
    scores = (
        lax.dot_general(
            unit.astype(bf16), unit_text, LAST_DIMS, preferred_element_type=f32
        )
        * inv_temp
    )
    group = group_ref[...]
    column = lax.broadcasted_iota(jnp.int32, group.shape, 1)
    own_group = jnp.sum(
        jnp.where(column == info[3] * clips, group, 0.0), axis=1, keepdims=True
    )
    weighted = jnp.where(group == own_group, jnp.exp(scores), 0.0)
    weighted_ref[...] = weighted
    sums_ref[...] = jnp.sum(weighted, axis=0, keepdims=True)


def embed(info, inputs, hidden, second_weight, projection, text, groups):
    rows, width = inputs.shape
    clips = rows // FRAMES
    joint = projection.shape[1]
    total = text.shape[0]
    return pl.pallas_call(
        embed_kernel,
        in_specs=[SMEM_SPEC] + [VMEM_SPEC] * 6,
        out_specs=[VMEM_SPEC] * 7,
        out_shape=[
            pltpu.VMEM((rows, width), f32),
            pltpu.VMEM((rows, 1), f32),
            pltpu.VMEM((clips, joint), f32),
            pltpu.VMEM((clips, 1), f32),
            pltpu.VMEM((clips, total), f32),
            jax.ShapeDtypeStruct((1, total), f32),
            pltpu.VMEM((total, joint), bf16),
        ],
        compiler_params=pltpu.CompilerParams(vmem_limit_bytes=24 * MIB),
        cost_estimate=pl.CostEstimate(
            flops=2 * rows * width * hidden.shape[1], bytes_accessed=4 * MIB, transcendentals=0
        ),
        name="embed",
    )(info, inputs, hidden, in_vmem(second_weight), projection, text, groups)


MASKS = (1, 8, 16, 2, 4)


def gather_step(held, mask, later):
    moved = move_across(held, mask)
    return jnp.where(
        later, jnp.concatenate([moved, held]), jnp.concatenate([held, moved])
    )


def sum_over_replicas(values, masks):
    for mask in masks:
        values = values + move_across(values, mask)
    return values


def loss_kernel(
    info,
    sums_ref,
    text_ref,
    projection_ref,
    normed_ref,
    inv_ref,
    unit_ref,
    inv_norm_ref,
    weighted_ref,
    out_ref,
):
    clips = unit_ref.shape[0]
    rows = normed_ref.shape[0]
    text = text_ref[...]
    weighted = weighted_ref[...]
    by_cols = weighted / sums_ref[...]
    by_rows = weighted / jnp.sum(weighted, axis=1, keepdims=True)
    shape = by_rows.shape
    own = (
        lax.broadcasted_iota(jnp.int32, shape, 0) + info[3] * clips
        == lax.broadcasted_iota(jnp.int32, shape, 1)
    )
    coeffs = grad_scale * (by_rows + by_cols - jnp.where(own, 2.0, 0.0))
    audio_grad = (
        jnp.dot(coeffs, text.astype(f32), precision=EXACT, preferred_element_type=f32) * inv_temp
    )
    unit = unit_ref[...]
    emb_grad = (
        audio_grad - unit * jnp.sum(unit * audio_grad, axis=-1, keepdims=True)
    ) * inv_norm_ref[...]
    pooled_grad = lax.dot_general(
        emb_grad,
        projection_ref[...].astype(f32),
        LAST_DIMS,
        precision=EXACT,
        preferred_element_type=f32,
    ) * (1.0 / (rows // clips))
    upstream = lax.dot_general(
        clip_rows(rows, clips),
        pooled_grad,
        (((0,), (0,)), ((), ())),
        precision=EXACT,
        preferred_element_type=f32,
    )
    normed = normed_ref[...]
    mean = jnp.mean(upstream, axis=-1, keepdims=True)
    along = jnp.mean(upstream * normed, axis=-1, keepdims=True)
    grad = (inv_ref[...] * (upstream - mean - normed * along)).astype(bf16)
    per_micro = out_ref.shape[1]
    for m in range(out_ref.shape[0]):
        out_ref[m] = grad[m * per_micro : (m + 1) * per_micro]


def loss_grad(info, sums, text, projection, normed, inv_std, unit, inv_norm, weighted):
    rows, width = normed.shape
    return pl.pallas_call(
        loss_kernel,
        in_specs=[SMEM_SPEC] + [VMEM_SPEC] * 8,
        out_specs=VMEM_SPEC,
        out_shape=pltpu.VMEM((MICRO, rows // MICRO, width), bf16),
        compiler_params=pltpu.CompilerParams(vmem_limit_bytes=24 * MIB),
        name="loss_grad",
    )(
        info,
        sums,
        in_vmem(text),
        projection,
        *[in_vmem(a) for a in (normed, inv_std, unit, inv_norm, weighted)],
    )


def step_kernel(inputs_given, keeps, slot, last_section, section_ref, second_ref, first_ref, slope_ref, normed_ref, inv_ref, *rest):
    count = len(inputs_given)
    given, stores = rest[:count], rest[count : count + 3]
    if keeps:
        passed_ref, out_ref, pre_ref, in_ref = rest[count + 3 :]
    else:
        out_ref, pre_ref, in_ref = rest[count + 3 :]
    section = section_ref[0]
    micro_id = slot - 2 * (last_section - section)
    active = (micro_id >= 0) & (micro_id < MICRO)
    micro = jnp.clip(micro_id, 0, MICRO - 1)

    @pl.when(active)
    def _():
        if count == 2:
            upstream = jnp.where(section == last_section, given[0][micro], given[1][...])
        elif inputs_given[0] == "last":
            upstream = given[0][micro]
        else:
            upstream = given[0][...]
        act_grad = lax.dot_general(
            upstream, second_ref[...], LAST_DIMS, preferred_element_type=f32
        )
        pre_grad = (act_grad * slope_ref[micro]).astype(bf16)
        normed_grad = lax.dot_general(
            pre_grad, first_ref[...], LAST_DIMS, preferred_element_type=f32
        )
        normed = normed_ref[micro].astype(f32)
        mean = jnp.mean(normed_grad, axis=-1, keepdims=True)
        along = jnp.mean(normed_grad * normed, axis=-1, keepdims=True)
        in_grad = upstream.astype(f32) + inv_ref[micro] * (normed_grad - mean - normed * along)
        in_grad = in_grad.astype(bf16)
        if keeps:
            passed_ref[...] = in_grad
            pre_ref[micro] = pre_grad
            out_ref[micro] = upstream
            in_ref[micro] = in_grad
        else:
            pre_ref[...] = pre_grad
            out_ref[...] = upstream
            in_ref[...] = in_grad

    if not keeps:

        @pl.when(jnp.logical_not(active))
        def _():
            for store, last in zip(stores, (out_ref, pre_ref, in_ref)):
                last[...] = store[MICRO - 1]


def chain_step(slot, last_section, section, weights, fixed, given, stores, keeps):
    rows, width = fixed[1].shape[1:]
    wide = fixed[0].shape[2]
    names = tuple(given)
    values = [in_vmem(given[n]) if n == "last" else given[n] for n in names]
    first_store = 1 + 5 + len(names)
    if keeps:
        shapes = [jax.ShapeDtypeStruct((rows, width), bf16)]
        shapes += [pltpu.VMEM(a.shape, a.dtype) for a in stores]
        aliases = {first_store + i: 1 + i for i in range(3)}
    else:
        shapes = [jax.ShapeDtypeStruct((rows, n), bf16) for n in (width, wide, width)]
        aliases = {}
    return pl.pallas_call(
        functools.partial(step_kernel, names, keeps, slot, last_section),
        in_specs=[SMEM_SPEC] + [VMEM_SPEC] * (5 + len(names) + 3),
        out_specs=[VMEM_SPEC] * len(shapes),
        out_shape=shapes,
        input_output_aliases=aliases,
        compiler_params=pltpu.CompilerParams(vmem_limit_bytes=16 * MIB),
        cost_estimate=pl.CostEstimate(
            flops=4 * rows * width * wide, bytes_accessed=8 * MIB, transcendentals=0
        ),
        name="chain_step",
    )(
        section,
        *[in_vmem(w) for w in weights],
        *[in_vmem(a) for a in fixed],
        *values,
        *[in_vmem(a) for a in stores],
    )


def empty_stores(shapes):
    return pl.pallas_call(
        lambda *refs: None,
        out_specs=[VMEM_SPEC] * len(shapes),
        out_shape=[pltpu.VMEM(s, bf16) for s in shapes],
        compiler_params=pltpu.CompilerParams(vmem_limit_bytes=MIB),
        name="empty_stores",
    )()


def column_halves(turned, at):
    width, rows = turned.shape
    blocks = turned.reshape(HI, COL, CORE, width // (HI * COL * CORE), rows)
    return item_at(blocks, at["core"], 2), item_at(blocks, at["other"], 2)


LOW, HIGH = slice(0, HI // 2), slice(HI // 2, HI)


def term_of(left, right, at, distance, part=slice(None)):
    chosen = item_at(left[part], at["columns"][distance], 1)
    height, rows = chosen.shape[1:]
    product = jnp.dot(chosen.reshape(-1, rows), right, preferred_element_type=f32)
    return product.reshape(-1, height, right.shape[1])


def scatter_total(own, ahead, back):
    return jnp.concatenate(
        [
            own[part] + a.astype(f32) + b.astype(f32)
            for part, a, b in zip((LOW, HIGH), ahead, back)
        ]
    )


def scatter_planes(total, at):
    rounded = total.astype(bf16)
    return [move(item_at(rounded, at["hi"][d]), hi=d) for d in (1, 2, 3)]


def scatter_end(total, got, at):
    result = item_at(total, at["hi"][0])
    for block in got:
        result = result + block.astype(f32)
    return result / (HI * COL * CORE)


def pick_kernel(label_ref, text_ref, out_ref):
    text = text_ref[...].astype(f32)
    row = lax.broadcasted_iota(jnp.int32, text.shape, 0)
    label = jnp.zeros(text.shape, jnp.int32)
    for i in range(text.shape[0]):
        label = jnp.where(row == i, label_ref[i // 2, i % 2], label)
    below = jnp.concatenate([text[1:], text[:1]])
    above = jnp.concatenate([text[-1:], text[:-1]])
    slot = row & 1
    other = jnp.where(slot == 0, below, above)
    out_ref[...] = jnp.where(label == slot, text, other).astype(bf16)


def paired_texts(text_embed, pair_label):
    return pl.pallas_call(
        pick_kernel,
        in_specs=[SMEM_SPEC, VMEM_SPEC],
        out_specs=VMEM_SPEC,
        out_shape=jax.ShapeDtypeStruct(text_embed.shape, bf16),
        compiler_params=pltpu.CompilerParams(vmem_limit_bytes=MIB),
        name="paired_texts",
    )(pair_label, text_embed)


def local(section_inputs, in_weight, out_weight, projection, text_embed, pair_label, pool_group):
    inputs = section_inputs[0]
    row_count, width = inputs.shape
    per_micro = row_count // MICRO
    clips = row_count // FRAMES
    wide = in_weight.shape[2]
    half = wide // CORE
    section_count = lax.axis_size("section")
    hi, col, core = place()
    at = dict(
        hi=[(hi + d) & (HI - 1) for d in range(HI)],
        core=core,
        other=1 - core,
        chip=jnp.stack([hi, col, core, (col * HI + hi) * CORE + core]).astype(jnp.int32),
        later=[lax.axis_index("replica") & mask != 0 for mask in MASKS],
        section=jnp.full((1,), lax.axis_index("section"), jnp.int32),
        columns=[(col + d) & (COL - 1) for d in range(COL)],
        kept=core * half,
        given=(1 - core) * half,
    )
    at = lax.optimization_barrier(at)

    shard = in_weight[0]
    kept = slice_at(shard, at["kept"], half, 1)
    got = move(slice_at(shard, at["given"], half, 1), core=1)
    first_shard = jnp.where(
        at["core"] == 0, jnp.concatenate([kept, got]), jnp.concatenate([got, kept])
    )
    second_shard = out_weight[0]

    def gathered(texts, step):
        return gather_step(texts, MASKS[step], at["later"][step])

    own = jnp.stack([first_shard, second_shard])
    moved = [move(own, hi=d) for d in (1, 2, 3)]
    own_left, own_right = move(own, col=1), move(own, col=-1)
    own, text_embed, pair_label, pool_group = together(
        own, text_embed, pair_label, pool_group
    )
    texts = paired_texts(text_embed, pair_label)
    groups = pool_group.reshape(HI, COL, CORE).transpose(1, 0, 2).reshape(-1, 1)
    groups = jnp.broadcast_to(groups, (groups.shape[0], clips))
    groups = groups.reshape(1, -1).astype(f32)
    texts = gathered(texts, 0)
    first_own_far = move(own_left[:1], col=1)
    second_own_far = move(own_right[1:], col=-1)
    *moved, texts, groups, first_own_far, second_own_far = together(
        *moved, texts, groups, first_own_far, second_own_far
    )
    stack = jnp.stack(moved, axis=1)
    left, right = move(stack, col=1), move(stack, col=-1)
    texts = gathered(gathered(texts, 1), 2)
    held = [own, own_left, own_right, stack, first_own_far, second_own_far]
    others = [move(a, core=1) for a in held]
    left, right, texts, *others = together(left, right, texts, *others)
    first_far = move(left[0], col=1)
    second_far = move(right[1], col=-1)
    texts = gathered(gathered(texts, 3), 4)

    def both(*parts):
        pieces, plan = [], []
        for piece, other, distance, index in parts:
            pieces += [piece, move(piece, core=1) if other is None else other]
            plan += [(distance, side, index) for side in (False, True)]
        return plan, pieces

    near_plan, near_pieces = both(
        (own, others[0], 0, "own"),
        (own_left, others[1], COL - 1, "own"),
        (own_right, others[2], 1, "own"),
        (stack, others[3], 0, "planes"),
        (left, None, COL - 1, "planes"),
        (right, None, 1, "planes"),
    )

    def placed(weight, shape, own_far, other_own_far, far):
        places = dict(
            own=(((weight,), 0),),
            planes=tuple(((weight, d), d + 1) for d in range(HI - 1)),
            far=tuple(((d,), d + 1) for d in range(HI - 1)),
            own_far=(((0,), 0),),
        )

        def run(plan, pieces, whole):
            plan = [(distance, other, places[index]) for distance, other, index in plan]
            return place_blocks(at["chip"], plan, pieces, shape, weight == 0, whole)

        far_plan, far_pieces = both((own_far, other_own_far, 2, "own_far"))
        whole = run(near_plan + far_plan, near_pieces + far_pieces, None)
        return whole, run(*both((far, None, 2, "far")), whole)

    _, first_weight = placed(0, (width, wide), first_own_far, others[4], first_far)
    early, second_weight = placed(1, (wide, width), second_own_far, others[5], second_far)
    normed, inv_in, normed_t, hidden, hidden_t, slope = front(
        inputs, first_weight, early
    )
    normed_halves = column_halves(normed_t, at)
    hidden_halves = column_halves(hidden_t, at)
    out_normed, out_inv, unit, inv_norm, weighted, sums, unit_text = embed(
        at["chip"], inputs, hidden, second_weight, projection, texts, groups
    )
    normed_columns, hidden_columns = (
        jnp.concatenate([own, move(other, core=1)], axis=-1)
        for own, other in (normed_halves, hidden_halves)
    )
    sums = sum_over_replicas(sums, MASKS[:-1])
    sums, normed_columns, hidden_columns = together(sums, normed_columns, hidden_columns)
    sums = sum_over_replicas(sums, MASKS[-1:])
    last_micro = loss_grad(
        at["chip"], sums, unit_text, projection, out_normed, out_inv, unit, inv_norm, weighted
    )

    fixed = (slope, normed, inv_in)
    weights = (second_weight, first_weight)
    stores = empty_stores([(MICRO, per_micro, n) for n in (width, wide, width)])
    arrived = [None, None]
    slots = 2 * (section_count - 1) + MICRO
    for slot in range(slots):
        given = {}
        if slot == slots - 1:
            early = [a[: MICRO - 1].reshape(-1, a.shape[2]) for a in stores]
            arrived[slot], *early = together(arrived[slot], *early)
            crossed = [move(a, core=1) for a in early[:2]]
        if slot < MICRO:
            given["last"] = last_micro
        if arrived[slot] is not None:
            given["next"] = arrived[slot]
        keeps = slot < slots - 1
        results = chain_step(
            slot, section_count - 1, at["section"], weights, fixed, given, stores, keeps
        )
        if not keeps:
            last_out, last_pre, last_in = results
            break
        passed, *stores = results
        route = [
            (s, s - 1)
            for s in range(1, section_count)
            if 0 <= slot - 2 * (section_count - 1 - s) < MICRO
        ]
        arrived.append(lax.ppermute(passed, "section", route) if route else None)

    out_rows, pre_rows = (
        jnp.concatenate([own, last, other, move(last, core=1)])
        for own, last, other in zip(early, (last_out, last_pre), crossed)
    )

    def term(second, distance, part=slice(None)):
        left, right = (hidden_columns, out_rows) if second else (normed_columns, pre_rows)
        return term_of(left, right, at, distance, part)

    def far(second):
        low, high = term(second, 2, LOW).astype(bf16), term(second, 2, HIGH).astype(bf16)
        return move(low, col=1), move(high, col=-1)

    def near_free(second):
        ahead, back = term(second, 1, HIGH).astype(bf16), term(second, 3, LOW).astype(bf16)
        return move(ahead, col=1), move(back, col=-1)

    def near_summed(second, low, high):
        ahead = (term(second, 1, LOW) + low.astype(f32)).astype(bf16)
        back = (term(second, 3, HIGH) + high.astype(f32)).astype(bf16)
        return move(ahead, col=1), move(back, col=-1)

    low2, high2 = far(True)
    ahead_high2, back_low2 = near_free(True)
    low1, high1 = far(False)
    ahead_low2, back_high2 = near_summed(True, low2, high2)
    ahead_high1, back_low1 = near_free(False)
    ahead_low1, back_high1 = near_summed(False, low1, high1)
    second_total = scatter_total(
        term(True, 0), (ahead_low2, ahead_high2), (back_low2, back_high2)
    )
    second_got = scatter_planes(second_total, at)
    *second_got, ahead_low1, ahead_high1, back_low1, back_high1 = together(
        *second_got, ahead_low1, ahead_high1, back_low1, back_high1
    )
    first_total = scatter_total(
        term(False, 0), (ahead_low1, ahead_high1), (back_low1, back_high1)
    )
    first_got = scatter_planes(first_total, at)
    second_sum = scatter_end(second_total, second_got, at)
    first_sum = scatter_end(first_total, first_got, at)
    in_grads = jnp.concatenate([early[2], last_in])
    return (in_grads[None], first_sum[None], second_sum[None])


def solution(mesh):
    return jax.shard_map(
        local,
        mesh=mesh,
        in_specs=(
            P("section", "replica", None),
            P("section", "replica", None),
            P("section", "replica", None),
            P(),
            P("replica", None),
            P("replica", None),
            P(),
        ),
        out_specs=(
            P("section", "replica", None),
            P("section", "replica", None),
            P("section", "replica", None),
        ),
        check_vma=False,
    )
```

```python
import functools

import jax
import jax.numpy as jnp
from jax import lax
from jax.experimental import pallas as pl
from jax.experimental.pallas import tpu as pltpu
from jax.sharding import PartitionSpec as P

MICRO = 4
FRAMES = 44

HI = 4
COL = 4
CORE = 2

MIB = 2**20
LAST_DIMS = (((1,), (1,)), ((), ()))
EXACT = lax.Precision.HIGHEST

eps_norm = 1e-05
eps_unit = 1e-06
inv_temp = 1.0 / 0.07
grad_scale = 256.0
sqrt_half = 0.7071067811865476
inv_sqrt_two_pi = 0.3989422804014327

bf16 = jnp.bfloat16
f32 = jnp.float32


def replica_of(hi, col, core):
    return ((hi % HI) * COL + col % COL) * CORE + core % CORE


def move(block, hi=0, col=0, core=0):
    route = [
        (replica_of(h, c, k), replica_of(h + hi, c + col, k + core))
        for h in range(HI)
        for c in range(COL)
        for k in range(CORE)
    ]
    return lax.ppermute(block, "replica", route)


def place():
    replica = lax.axis_index("replica")
    return replica >> 3, (replica >> 1) & (COL - 1), replica & (CORE - 1)


def together(*values):
    return lax.optimization_barrier(values)


def move_across(block, mask):
    count = HI * COL * CORE
    return lax.ppermute(block, "replica", [(r, r ^ mask) for r in range(count)])


def slice_at(values, start, size, axis):
    return lax.dynamic_slice_in_dim(values, start, size, axis, allow_negative_indices=False)


def item_at(values, index, axis=0):
    return lax.dynamic_index_in_dim(
        values, index, axis, keepdims=False, allow_negative_indices=False
    )


def in_vmem(value):
    return pltpu.with_memory_space_constraint(value, pltpu.VMEM)


VMEM_SPEC = pl.BlockSpec(memory_space=pltpu.VMEM)
ANY_SPEC = pl.BlockSpec(memory_space=pl.ANY)
SMEM_SPEC = pl.BlockSpec(memory_space=pltpu.SMEM)


def place_kernel(plan, by_columns, info, *refs):
    pieces, whole = refs[: len(plan)], refs[-1]
    hi, col, core = info[0], info[1], info[2]
    for (distance, other, blocks), piece in zip(plan, pieces):
        rows, width = piece.shape[-2:]
        at_col = (col + distance) & (COL - 1)
        side = 1 - core if other else core
        for k, back in blocks:
            chip = ((hi + HI - back) & (HI - 1)) * COL + at_col
            if by_columns:
                row = chip * rows
                column = pl.ds(pl.multiple_of(side * width, width), width)
            else:
                row = (chip * CORE + side) * rows
                column = slice(None)
            whole[pl.ds(pl.multiple_of(row, 16), rows), column] = piece[k]


def place_blocks(info, plan, pieces, shape, by_columns, whole=None):
    return pl.pallas_call(
        functools.partial(place_kernel, plan, by_columns),
        in_specs=[SMEM_SPEC]
        + [VMEM_SPEC] * len(pieces)
        + ([] if whole is None else [VMEM_SPEC]),
        out_specs=VMEM_SPEC,
        out_shape=pltpu.VMEM(shape, bf16),
        input_output_aliases={} if whole is None else {1 + len(pieces): 0},
        compiler_params=pltpu.CompilerParams(vmem_limit_bytes=12 * MIB),
        cost_estimate=pl.CostEstimate(
            flops=0, bytes_accessed=2 * sum(p.size for p in pieces), transcendentals=0
        ),
        name="place_blocks",
    )(info, *pieces, *([] if whole is None else [in_vmem(whole)]))


def front_kernel(
    inputs_ref, first_ref, waits_ref, normed_ref, inv_ref, normed_t_ref, hidden_ref, hidden_t_ref, slope_ref
):
    micro, rows = normed_ref.shape[:2]
    values = inputs_ref[...].astype(f32)
    centred = values - jnp.mean(values, axis=-1, keepdims=True)
    inv_std = lax.rsqrt(jnp.mean(centred * centred, axis=-1, keepdims=True) + eps_norm)
    scaled = centred * inv_std
    normed = scaled.astype(bf16)
    for m in range(micro):
        normed_ref[m] = normed[m * rows : (m + 1) * rows]
        inv_ref[m] = inv_std[m * rows : (m + 1) * rows]
    normed_t_ref[...] = scaled.T.astype(bf16)
    step = 256

    @pl.loop(0, first_ref.shape[1] // step)
    def _(j):
        part = pl.ds(pl.multiple_of(j * step, step), step)
        preact = jnp.dot(normed, first_ref[:, part], preferred_element_type=f32)
        cdf = 0.5 * (1.0 + lax.erf(preact * sqrt_half))
        hidden = preact * cdf
        hidden_ref[:, part] = hidden.astype(bf16)
        hidden_t_ref[part, :] = hidden.T.astype(bf16)
        slope = cdf + preact * jnp.exp(-0.5 * preact * preact) * inv_sqrt_two_pi
        for m in range(micro):
            slope_ref[m, :, part] = slope[m * rows : (m + 1) * rows]


def front(inputs, first_weight, waits):
    rows, width = inputs.shape
    wide = first_weight.shape[1]
    per_micro = rows // MICRO
    return pl.pallas_call(
        front_kernel,
        in_specs=[VMEM_SPEC] * 3,
        out_specs=[VMEM_SPEC] * 6,
        out_shape=[
            pltpu.VMEM((MICRO, per_micro, width), bf16),
            pltpu.VMEM((MICRO, per_micro, 1), f32),
            jax.ShapeDtypeStruct((width, rows), bf16),
            jax.ShapeDtypeStruct((rows, wide), bf16),
            jax.ShapeDtypeStruct((wide, rows), bf16),
            pltpu.VMEM((MICRO, per_micro, wide), f32),
        ],
        compiler_params=pltpu.CompilerParams(vmem_limit_bytes=24 * MIB),
        cost_estimate=pl.CostEstimate(
            flops=2 * rows * width * wide, bytes_accessed=4 * MIB, transcendentals=0
        ),
        name="front",
    )(inputs, in_vmem(first_weight), in_vmem(waits))


def clip_rows(rows, clips):
    first = lax.broadcasted_iota(jnp.int32, (clips, rows), 0) * (rows // clips)
    row = lax.broadcasted_iota(jnp.int32, (clips, rows), 1)
    return jnp.where((row >= first) & (row < first + rows // clips), 1.0, 0.0).astype(f32)


def embed_kernel(
    info,
    inputs_ref,
    hidden_ref,
    second_ref,
    projection_ref,
    text_ref,
    group_ref,
    normed_ref,
    inv_ref,
    unit_ref,
    inv_norm_ref,
    weighted_ref,
    sums_ref,
    unit_text_ref,
):
    rows = inputs_ref.shape[0]
    clips = unit_ref.shape[0]
    block_out = inputs_ref[...].astype(f32) + jnp.dot(
        hidden_ref[...], second_ref[...], preferred_element_type=f32
    )
    centred = block_out - jnp.mean(block_out, axis=-1, keepdims=True)
    inv_std = lax.rsqrt(jnp.mean(centred * centred, axis=-1, keepdims=True) + eps_norm)
    normed = centred * inv_std
    normed_ref[...] = normed
    inv_ref[...] = inv_std
    sums = jnp.dot(
        clip_rows(rows, clips), normed, precision=EXACT, preferred_element_type=f32
    )
    pooled = (sums * (1.0 / (rows // clips))).astype(bf16)
    embedded = jnp.dot(pooled, projection_ref[...], preferred_element_type=f32)
    inv_norm = lax.rsqrt(jnp.sum(embedded * embedded, axis=-1, keepdims=True) + eps_unit)
    unit = embedded * inv_norm
    unit_ref[...] = unit
    inv_norm_ref[...] = inv_norm
    text = text_ref[...].astype(f32)
    unit_text = text * lax.rsqrt(jnp.sum(text * text, axis=-1, keepdims=True) + eps_unit)
    unit_text = unit_text.astype(bf16)
    unit_text_ref[...] = unit_text
    scores = (
        lax.dot_general(
            unit.astype(bf16), unit_text, LAST_DIMS, preferred_element_type=f32
        )
        * inv_temp
    )
    group = group_ref[...]
    column = lax.broadcasted_iota(jnp.int32, group.shape, 1)
    own_group = jnp.sum(
        jnp.where(column == info[3] * clips, group, 0.0), axis=1, keepdims=True
    )
    weighted = jnp.where(group == own_group, jnp.exp(scores), 0.0)
    weighted_ref[...] = weighted
    sums_ref[...] = jnp.sum(weighted, axis=0, keepdims=True)


def embed(info, inputs, hidden, second_weight, projection, text, groups):
    rows, width = inputs.shape
    clips = rows // FRAMES
    joint = projection.shape[1]
    total = text.shape[0]
    return pl.pallas_call(
        embed_kernel,
        in_specs=[SMEM_SPEC] + [VMEM_SPEC] * 6,
        out_specs=[VMEM_SPEC] * 7,
        out_shape=[
            pltpu.VMEM((rows, width), f32),
            pltpu.VMEM((rows, 1), f32),
            pltpu.VMEM((clips, joint), f32),
            pltpu.VMEM((clips, 1), f32),
            pltpu.VMEM((clips, total), f32),
            jax.ShapeDtypeStruct((1, total), f32),
            pltpu.VMEM((total, joint), bf16),
        ],
        compiler_params=pltpu.CompilerParams(vmem_limit_bytes=24 * MIB),
        cost_estimate=pl.CostEstimate(
            flops=2 * rows * width * hidden.shape[1], bytes_accessed=4 * MIB, transcendentals=0
        ),
        name="embed",
    )(info, inputs, hidden, in_vmem(second_weight), projection, text, groups)


MASKS = (1, 8, 16, 2, 4)


def gather_step(held, mask, later):
    moved = move_across(held, mask)
    return jnp.where(
        later, jnp.concatenate([moved, held]), jnp.concatenate([held, moved])
    )


def sum_over_replicas(values, masks):
    for mask in masks:
        values = values + move_across(values, mask)
    return values


def loss_kernel(
    info,
    sums_ref,
    text_ref,
    projection_ref,
    normed_ref,
    inv_ref,
    unit_ref,
    inv_norm_ref,
    weighted_ref,
    out_ref,
):
    clips = unit_ref.shape[0]
    rows = normed_ref.shape[0]
    text = text_ref[...]
    weighted = weighted_ref[...]
    by_cols = weighted / sums_ref[...]
    by_rows = weighted / jnp.sum(weighted, axis=1, keepdims=True)
    shape = by_rows.shape
    own = (
        lax.broadcasted_iota(jnp.int32, shape, 0) + info[3] * clips
        == lax.broadcasted_iota(jnp.int32, shape, 1)
    )
    coeffs = grad_scale * (by_rows + by_cols - jnp.where(own, 2.0, 0.0))
    audio_grad = (
        jnp.dot(coeffs, text.astype(f32), precision=EXACT, preferred_element_type=f32) * inv_temp
    )
    unit = unit_ref[...]
    emb_grad = (
        audio_grad - unit * jnp.sum(unit * audio_grad, axis=-1, keepdims=True)
    ) * inv_norm_ref[...]
    pooled_grad = lax.dot_general(
        emb_grad,
        projection_ref[...].astype(f32),
        LAST_DIMS,
        precision=EXACT,
        preferred_element_type=f32,
    ) * (1.0 / (rows // clips))
    upstream = lax.dot_general(
        clip_rows(rows, clips),
        pooled_grad,
        (((0,), (0,)), ((), ())),
        precision=EXACT,
        preferred_element_type=f32,
    )
    normed = normed_ref[...]
    mean = jnp.mean(upstream, axis=-1, keepdims=True)
    along = jnp.mean(upstream * normed, axis=-1, keepdims=True)
    grad = (inv_ref[...] * (upstream - mean - normed * along)).astype(bf16)
    per_micro = out_ref.shape[1]
    for m in range(out_ref.shape[0]):
        out_ref[m] = grad[m * per_micro : (m + 1) * per_micro]


def loss_grad(info, sums, text, projection, normed, inv_std, unit, inv_norm, weighted):
    rows, width = normed.shape
    return pl.pallas_call(
        loss_kernel,
        in_specs=[SMEM_SPEC] + [VMEM_SPEC] * 8,
        out_specs=VMEM_SPEC,
        out_shape=pltpu.VMEM((MICRO, rows // MICRO, width), bf16),
        compiler_params=pltpu.CompilerParams(vmem_limit_bytes=24 * MIB),
        name="loss_grad",
    )(
        info,
        sums,
        in_vmem(text),
        projection,
        *[in_vmem(a) for a in (normed, inv_std, unit, inv_norm, weighted)],
    )


def step_kernel(inputs_given, keeps, slot, last_section, section_ref, second_ref, first_ref, slope_ref, normed_ref, inv_ref, *rest):
    count = len(inputs_given)
    given, stores = rest[:count], rest[count : count + 3]
    if keeps:
        passed_ref, out_ref, pre_ref, in_ref = rest[count + 3 :]
    else:
        out_ref, pre_ref, in_ref = rest[count + 3 :]
    section = section_ref[0]
    micro_id = slot - 2 * (last_section - section)
    active = (micro_id >= 0) & (micro_id < MICRO)
    micro = jnp.clip(micro_id, 0, MICRO - 1)

    @pl.when(active)
    def _():
        if count == 2:
            upstream = jnp.where(section == last_section, given[0][micro], given[1][...])
        elif inputs_given[0] == "last":
            upstream = given[0][micro]
        else:
            upstream = given[0][...]
        act_grad = lax.dot_general(
            upstream, second_ref[...], LAST_DIMS, preferred_element_type=f32
        )
        pre_grad = (act_grad * slope_ref[micro]).astype(bf16)
        normed_grad = lax.dot_general(
            pre_grad, first_ref[...], LAST_DIMS, preferred_element_type=f32
        )
        normed = normed_ref[micro].astype(f32)
        mean = jnp.mean(normed_grad, axis=-1, keepdims=True)
        along = jnp.mean(normed_grad * normed, axis=-1, keepdims=True)
        in_grad = upstream.astype(f32) + inv_ref[micro] * (normed_grad - mean - normed * along)
        in_grad = in_grad.astype(bf16)
        if keeps:
            passed_ref[...] = in_grad
            pre_ref[micro] = pre_grad
            out_ref[micro] = upstream
            in_ref[micro] = in_grad
        else:
            pre_ref[...] = pre_grad
            out_ref[...] = upstream
            in_ref[...] = in_grad

    if not keeps:

        @pl.when(jnp.logical_not(active))
        def _():
            for store, last in zip(stores, (out_ref, pre_ref, in_ref)):
                last[...] = store[MICRO - 1]


def chain_step(slot, last_section, section, weights, fixed, given, stores, keeps):
    rows, width = fixed[1].shape[1:]
    wide = fixed[0].shape[2]
    names = tuple(given)
    values = [in_vmem(given[n]) if n == "last" else given[n] for n in names]
    first_store = 1 + 5 + len(names)
    if keeps:
        shapes = [jax.ShapeDtypeStruct((rows, width), bf16)]
        shapes += [pltpu.VMEM(a.shape, a.dtype) for a in stores]
        aliases = {first_store + i: 1 + i for i in range(3)}
    else:
        shapes = [jax.ShapeDtypeStruct((rows, n), bf16) for n in (width, wide, width)]
        aliases = {}
    return pl.pallas_call(
        functools.partial(step_kernel, names, keeps, slot, last_section),
        in_specs=[SMEM_SPEC] + [VMEM_SPEC] * (5 + len(names) + 3),
        out_specs=[VMEM_SPEC] * len(shapes),
        out_shape=shapes,
        input_output_aliases=aliases,
        compiler_params=pltpu.CompilerParams(vmem_limit_bytes=16 * MIB),
        cost_estimate=pl.CostEstimate(flops=3 * 10**9, bytes_accessed=MIB, transcendentals=0),
        name="chain_step",
    )(
        section,
        *[in_vmem(w) for w in weights],
        *[in_vmem(a) for a in fixed],
        *values,
        *[in_vmem(a) for a in stores],
    )


def empty_stores(shapes):
    return pl.pallas_call(
        lambda *refs: None,
        out_specs=[VMEM_SPEC] * len(shapes),
        out_shape=[pltpu.VMEM(s, bf16) for s in shapes],
        compiler_params=pltpu.CompilerParams(vmem_limit_bytes=MIB),
        name="empty_stores",
    )()


def column_halves(turned, at):
    width, rows = turned.shape
    blocks = turned.reshape(HI, COL, CORE, width // (HI * COL * CORE), rows)
    return item_at(blocks, at["core"], 2), item_at(blocks, at["other"], 2)


LOW, HIGH = slice(0, HI // 2), slice(HI // 2, HI)


def term_of(left, right, at, distance, part=slice(None)):
    chosen = item_at(left[part], at["columns"][distance], 1)
    height, rows = chosen.shape[1:]
    product = jnp.dot(chosen.reshape(-1, rows), right, preferred_element_type=f32)
    return product.reshape(-1, height, right.shape[1])


def scatter_total(own, ahead, back):
    return own + ahead.astype(f32) + back.astype(f32)


def scatter_planes(total, at):
    rounded = total.astype(bf16)
    return [move(item_at(rounded, at["hi"][d]), hi=d) for d in (1, 2, 3)]


def scatter_end(total, got, at):
    result = item_at(total, at["hi"][0])
    for block in got:
        result = result + block.astype(f32)
    return result / (HI * COL * CORE)


def pick_kernel(label_ref, text_ref, out_ref):
    text = text_ref[...].astype(f32)
    row = lax.broadcasted_iota(jnp.int32, text.shape, 0)
    label = jnp.zeros(text.shape, jnp.int32)
    for i in range(text.shape[0]):
        label = jnp.where(row == i, label_ref[i // 2, i % 2], label)
    below = jnp.concatenate([text[1:], text[:1]])
    above = jnp.concatenate([text[-1:], text[:-1]])
    slot = row & 1
    other = jnp.where(slot == 0, below, above)
    out_ref[...] = jnp.where(label == slot, text, other).astype(bf16)


def paired_texts(text_embed, pair_label):
    return pl.pallas_call(
        pick_kernel,
        in_specs=[SMEM_SPEC, VMEM_SPEC],
        out_specs=VMEM_SPEC,
        out_shape=jax.ShapeDtypeStruct(text_embed.shape, bf16),
        compiler_params=pltpu.CompilerParams(vmem_limit_bytes=MIB),
        name="paired_texts",
    )(pair_label, text_embed)


def local(section_inputs, in_weight, out_weight, projection, text_embed, pair_label, pool_group):
    inputs = section_inputs[0]
    row_count, width = inputs.shape
    per_micro = row_count // MICRO
    clips = row_count // FRAMES
    wide = in_weight.shape[2]
    half = wide // CORE
    section_count = lax.axis_size("section")
    hi, col, core = place()
    at = dict(
        hi=[(hi + d) & (HI - 1) for d in range(HI)],
        core=core,
        other=1 - core,
        chip=jnp.stack([hi, col, core, (col * HI + hi) * CORE + core]).astype(jnp.int32),
        later=[lax.axis_index("replica") & mask != 0 for mask in MASKS],
        section=jnp.full((1,), lax.axis_index("section"), jnp.int32),
        columns=[(col + d) & (COL - 1) for d in range(COL)],
        kept=core * half,
        given=(1 - core) * half,
    )
    at = lax.optimization_barrier(at)

    shard = in_weight[0]
    kept = slice_at(shard, at["kept"], half, 1)
    got = move(slice_at(shard, at["given"], half, 1), core=1)
    first_shard = jnp.where(
        at["core"] == 0, jnp.concatenate([kept, got]), jnp.concatenate([got, kept])
    )
    second_shard = out_weight[0]

    def gathered(texts, step):
        return gather_step(texts, MASKS[step], at["later"][step])

    own = jnp.stack([first_shard, second_shard])
    moved = [move(own, hi=d) for d in (1, 2, 3)]
    own_left, own_right = move(own, col=1), move(own, col=-1)
    own, text_embed, pair_label, pool_group = together(
        own, text_embed, pair_label, pool_group
    )
    texts = paired_texts(text_embed, pair_label)
    groups = pool_group.reshape(HI, COL, CORE).transpose(1, 0, 2).reshape(-1, 1)
    groups = jnp.broadcast_to(groups, (groups.shape[0], clips))
    groups = groups.reshape(1, -1).astype(f32)
    texts = gathered(texts, 0)
    first_own_far = move(own_left[:1], col=1)
    second_own_far = move(own_right[1:], col=-1)
    *moved, texts, groups, first_own_far, second_own_far = together(
        *moved, texts, groups, first_own_far, second_own_far
    )
    stack = jnp.stack(moved, axis=1)
    left, right = move(stack, col=1), move(stack, col=-1)
    for step in (1, 2, 3):
        texts = gathered(texts, step)
    held = [own, own_left, own_right, stack, first_own_far, second_own_far]
    others = [move(a, core=1) for a in held]
    left, right, texts, *others = together(left, right, texts, *others)
    first_far = move(left[0], col=1)
    second_far = move(right[1], col=-1)
    texts = gathered(texts, 4)
    first_far, texts = together(first_far, texts)

    def both(*parts):
        pieces, plan = [], []
        for piece, other, distance, index in parts:
            pieces += [piece, move(piece, core=1) if other is None else other]
            plan += [(distance, side, index) for side in (False, True)]
        return plan, pieces

    near_plan, near_pieces = both(
        (own, others[0], 0, "own"),
        (own_left, others[1], COL - 1, "own"),
        (own_right, others[2], 1, "own"),
        (stack, others[3], 0, "planes"),
        (left, None, COL - 1, "planes"),
        (right, None, 1, "planes"),
    )

    def placed(weight, shape, own_far, other_own_far, far):
        places = dict(
            own=(((weight,), 0),),
            planes=tuple(((weight, d), d + 1) for d in range(HI - 1)),
            far=tuple(((d,), d + 1) for d in range(HI - 1)),
            own_far=(((0,), 0),),
        )

        def run(plan, pieces, whole):
            plan = [(distance, other, places[index]) for distance, other, index in plan]
            return place_blocks(at["chip"], plan, pieces, shape, weight == 0, whole)

        far_plan, far_pieces = both((own_far, other_own_far, 2, "own_far"))
        whole = run(near_plan + far_plan, near_pieces + far_pieces, None)
        return whole, run(*both((far, None, 2, "far")), whole)

    _, first_weight = placed(0, (width, wide), first_own_far, others[4], first_far)
    early, second_weight = placed(1, (wide, width), second_own_far, others[5], second_far)
    normed, inv_in, normed_t, hidden, hidden_t, slope = front(
        inputs, first_weight, early
    )
    normed_halves = column_halves(normed_t, at)
    hidden_halves = column_halves(hidden_t, at)
    out_normed, out_inv, unit, inv_norm, weighted, sums, unit_text = embed(
        at["chip"], inputs, hidden, second_weight, projection, texts, groups
    )
    normed_columns, hidden_columns = (
        jnp.concatenate([own, move(other, core=1)], axis=-1)
        for own, other in (normed_halves, hidden_halves)
    )
    sums = sum_over_replicas(sums, MASKS[:-1])
    sums, normed_columns, hidden_columns = together(sums, normed_columns, hidden_columns)
    sums = sum_over_replicas(sums, MASKS[-1:])
    last_micro = loss_grad(
        at["chip"], sums, unit_text, projection, out_normed, out_inv, unit, inv_norm, weighted
    )

    fixed = (slope, normed, inv_in)
    weights = (second_weight, first_weight)
    stores = empty_stores([(MICRO, per_micro, n) for n in (width, wide, width)])
    arrived = [None, None]
    slots = 2 * (section_count - 1) + MICRO
    for slot in range(slots):
        given = {}
        if slot == slots - 1:
            early = [a[: MICRO - 1].reshape(-1, a.shape[2]) for a in stores]
            arrived[slot], *early = together(arrived[slot], *early)
            crossed = [move(a, core=1) for a in early[:2]]
        if slot < MICRO:
            given["last"] = last_micro
        if arrived[slot] is not None:
            given["next"] = arrived[slot]
        keeps = slot < slots - 1
        results = chain_step(
            slot, section_count - 1, at["section"], weights, fixed, given, stores, keeps
        )
        if not keeps:
            last_out, last_pre, last_in = results
            break
        passed, *stores = results
        route = [
            (s, s - 1)
            for s in range(1, section_count)
            if 0 <= slot - 2 * (section_count - 1 - s) < MICRO
        ]
        arrived.append(lax.ppermute(passed, "section", route) if route else None)

    out_rows, pre_rows = (
        jnp.concatenate([own, last, other, move(last, core=1)])
        for own, last, other in zip(early, (last_out, last_pre), crossed)
    )

    def term(second, distance, part=slice(None)):
        left, right = (hidden_columns, out_rows) if second else (normed_columns, pre_rows)
        return term_of(left, right, at, distance, part)

    def far(second):
        low, high = term(second, 2, LOW).astype(bf16), term(second, 2, HIGH).astype(bf16)
        return move(low, col=1), move(high, col=-1)

    def near(second, low, high):
        ahead, back = term(second, 1), term(second, 3)
        ahead = jnp.concatenate([ahead[LOW] + low.astype(f32), ahead[HIGH]])
        back = jnp.concatenate([back[LOW], back[HIGH] + high.astype(f32)])
        return move(ahead.astype(bf16), col=1), move(back.astype(bf16), col=-1)

    low2, high2, low1, high1 = together(*far(True), *far(False))
    ahead2, back2 = near(True, low2, high2)
    ahead2, back2, low1, high1 = together(ahead2, back2, low1, high1)
    ahead1, back1 = near(False, low1, high1)
    second_total = scatter_total(term(True, 0), ahead2, back2)
    second_got = scatter_planes(second_total, at)
    *second_got, ahead1, back1 = together(*second_got, ahead1, back1)
    first_total = scatter_total(term(False, 0), ahead1, back1)
    first_got = scatter_planes(first_total, at)
    second_sum = scatter_end(second_total, second_got, at)
    first_sum = scatter_end(first_total, first_got, at)
    in_grads = jnp.concatenate([early[2], last_in])
    return (in_grads[None], first_sum[None], second_sum[None])


def solution(mesh):
    return jax.shard_map(
        local,
        mesh=mesh,
        in_specs=(
            P("section", "replica", None),
            P("section", "replica", None),
            P("section", "replica", None),
            P(),
            P("replica", None),
            P("replica", None),
            P(),
        ),
        out_specs=(
            P("section", "replica", None),
            P("section", "replica", None),
            P("section", "replica", None),
        ),
        check_vma=False,
    )
```

```python
import functools

import jax
import jax.numpy as jnp
from jax import lax
from jax.experimental import pallas as pl
from jax.experimental.pallas import tpu as pltpu
from jax.sharding import PartitionSpec as P

MICRO = 4
FRAMES = 44

HI = 4
COL = 4
CORE = 2

MIB = 2**20
LAST_DIMS = (((1,), (1,)), ((), ()))
EXACT = lax.Precision.HIGHEST

eps_norm = 1e-05
eps_unit = 1e-06
inv_temp = 1.0 / 0.07
grad_scale = 256.0
sqrt_half = 0.7071067811865476
inv_sqrt_two_pi = 0.3989422804014327

bf16 = jnp.bfloat16
f32 = jnp.float32


def replica_of(hi, col, core):
    return ((hi % HI) * COL + col % COL) * CORE + core % CORE


def move(block, hi=0, col=0, core=0):
    route = [
        (replica_of(h, c, k), replica_of(h + hi, c + col, k + core))
        for h in range(HI)
        for c in range(COL)
        for k in range(CORE)
    ]
    return lax.ppermute(block, "replica", route)


def place():
    replica = lax.axis_index("replica")
    return replica >> 3, (replica >> 1) & (COL - 1), replica & (CORE - 1)


def together(*values):
    return lax.optimization_barrier(values)


def move_across(block, mask):
    count = HI * COL * CORE
    first = (lax.axis_size("section") - 1) * count
    route = [(first + r, first + (r ^ mask)) for r in range(count)]
    return lax.ppermute(block, ("section", "replica"), route)


def slice_at(values, start, size, axis):
    return lax.dynamic_slice_in_dim(values, start, size, axis, allow_negative_indices=False)


def item_at(values, index, axis=0):
    return lax.dynamic_index_in_dim(
        values, index, axis, keepdims=False, allow_negative_indices=False
    )


def in_vmem(value):
    return pltpu.with_memory_space_constraint(value, pltpu.VMEM)


VMEM_SPEC = pl.BlockSpec(memory_space=pltpu.VMEM)
ANY_SPEC = pl.BlockSpec(memory_space=pl.ANY)
SMEM_SPEC = pl.BlockSpec(memory_space=pltpu.SMEM)


def place_kernel(plan, by_columns, info, *refs):
    pieces, whole = refs[: len(plan)], refs[-1]
    hi, col, core = info[0], info[1], info[2]
    for (distance, other, blocks), piece in zip(plan, pieces):
        rows, width = piece.shape[-2:]
        at_col = (col + distance) & (COL - 1)
        side = 1 - core if other else core
        for k, back in blocks:
            chip = ((hi + HI - back) & (HI - 1)) * COL + at_col
            if by_columns:
                row = chip * rows
                column = pl.ds(pl.multiple_of(side * width, width), width)
            else:
                row = (chip * CORE + side) * rows
                column = slice(None)
            whole[pl.ds(pl.multiple_of(row, 16), rows), column] = piece[k]


def place_blocks(info, plan, pieces, shape, by_columns, whole=None):
    return pl.pallas_call(
        functools.partial(place_kernel, plan, by_columns),
        in_specs=[SMEM_SPEC]
        + [VMEM_SPEC] * len(pieces)
        + ([] if whole is None else [VMEM_SPEC]),
        out_specs=VMEM_SPEC,
        out_shape=pltpu.VMEM(shape, bf16),
        input_output_aliases={} if whole is None else {1 + len(pieces): 0},
        compiler_params=pltpu.CompilerParams(vmem_limit_bytes=12 * MIB),
        cost_estimate=pl.CostEstimate(
            flops=0, bytes_accessed=2 * sum(p.size for p in pieces), transcendentals=0
        ),
        name="place_blocks",
    )(info, *pieces, *([] if whole is None else [in_vmem(whole)]))


def front_kernel(
    inputs_ref, first_ref, waits_ref, normed_ref, inv_ref, normed_t_ref, hidden_ref, hidden_t_ref, slope_ref
):
    micro, rows = normed_ref.shape[:2]
    values = inputs_ref[...].astype(f32)
    centred = values - jnp.mean(values, axis=-1, keepdims=True)
    inv_std = lax.rsqrt(jnp.mean(centred * centred, axis=-1, keepdims=True) + eps_norm)
    scaled = centred * inv_std
    normed = scaled.astype(bf16)
    for m in range(micro):
        normed_ref[m] = normed[m * rows : (m + 1) * rows]
        inv_ref[m] = inv_std[m * rows : (m + 1) * rows]
    normed_t_ref[...] = scaled.T.astype(bf16)
    step = 256

    @pl.loop(0, first_ref.shape[1] // step)
    def _(j):
        part = pl.ds(pl.multiple_of(j * step, step), step)
        preact = jnp.dot(normed, first_ref[:, part], preferred_element_type=f32)
        cdf = 0.5 * (1.0 + lax.erf(preact * sqrt_half))
        hidden = preact * cdf
        hidden_ref[:, part] = hidden.astype(bf16)
        hidden_t_ref[part, :] = hidden.T.astype(bf16)
        slope = cdf + preact * jnp.exp(-0.5 * preact * preact) * inv_sqrt_two_pi
        for m in range(micro):
            slope_ref[m, :, part] = slope[m * rows : (m + 1) * rows]


def front(inputs, first_weight, waits):
    rows, width = inputs.shape
    wide = first_weight.shape[1]
    per_micro = rows // MICRO
    return pl.pallas_call(
        front_kernel,
        in_specs=[VMEM_SPEC] * 3,
        out_specs=[VMEM_SPEC] * 6,
        out_shape=[
            pltpu.VMEM((MICRO, per_micro, width), bf16),
            pltpu.VMEM((MICRO, per_micro, 1), f32),
            jax.ShapeDtypeStruct((width, rows), bf16),
            jax.ShapeDtypeStruct((rows, wide), bf16),
            jax.ShapeDtypeStruct((wide, rows), bf16),
            pltpu.VMEM((MICRO, per_micro, wide), f32),
        ],
        compiler_params=pltpu.CompilerParams(vmem_limit_bytes=24 * MIB),
        cost_estimate=pl.CostEstimate(
            flops=2 * rows * width * wide, bytes_accessed=4 * MIB, transcendentals=0
        ),
        name="front",
    )(inputs, in_vmem(first_weight), in_vmem(waits))


def clip_rows(rows, clips):
    first = lax.broadcasted_iota(jnp.int32, (clips, rows), 0) * (rows // clips)
    row = lax.broadcasted_iota(jnp.int32, (clips, rows), 1)
    return jnp.where((row >= first) & (row < first + rows // clips), 1.0, 0.0).astype(f32)


def embed_kernel(
    info,
    inputs_ref,
    hidden_ref,
    second_ref,
    projection_ref,
    text_ref,
    group_ref,
    normed_ref,
    inv_ref,
    unit_ref,
    inv_norm_ref,
    weighted_ref,
    sums_ref,
    unit_text_ref,
):
    @pl.when(info[4] == 1)
    def _():
        rows = inputs_ref.shape[0]
        clips = unit_ref.shape[0]
        block_out = inputs_ref[...].astype(f32) + jnp.dot(
            hidden_ref[...], second_ref[...], preferred_element_type=f32
        )
        centred = block_out - jnp.mean(block_out, axis=-1, keepdims=True)
        inv_std = lax.rsqrt(jnp.mean(centred * centred, axis=-1, keepdims=True) + eps_norm)
        normed = centred * inv_std
        normed_ref[...] = normed
        inv_ref[...] = inv_std
        sums = jnp.dot(
            clip_rows(rows, clips), normed, precision=EXACT, preferred_element_type=f32
        )
        pooled = (sums * (1.0 / (rows // clips))).astype(bf16)
        embedded = jnp.dot(pooled, projection_ref[...], preferred_element_type=f32)
        inv_norm = lax.rsqrt(jnp.sum(embedded * embedded, axis=-1, keepdims=True) + eps_unit)
        unit = embedded * inv_norm
        unit_ref[...] = unit
        inv_norm_ref[...] = inv_norm
        text = text_ref[...].astype(f32)
        unit_text = text * lax.rsqrt(jnp.sum(text * text, axis=-1, keepdims=True) + eps_unit)
        unit_text = unit_text.astype(bf16)
        unit_text_ref[...] = unit_text
        scores = (
            lax.dot_general(
                unit.astype(bf16), unit_text, LAST_DIMS, preferred_element_type=f32
            )
            * inv_temp
        )
        group = group_ref[...]
        column = lax.broadcasted_iota(jnp.int32, group.shape, 1)
        own_group = jnp.sum(
            jnp.where(column == info[3] * clips, group, 0.0), axis=1, keepdims=True
        )
        weighted = jnp.where(group == own_group, jnp.exp(scores), 0.0)
        weighted_ref[...] = weighted
        sums_ref[...] = jnp.sum(weighted, axis=0, keepdims=True)


def embed(info, inputs, hidden, second_weight, projection, text, groups):
    rows, width = inputs.shape
    clips = rows // FRAMES
    joint = projection.shape[1]
    total = text.shape[0]
    return pl.pallas_call(
        embed_kernel,
        in_specs=[SMEM_SPEC] + [VMEM_SPEC] * 6,
        out_specs=[VMEM_SPEC] * 7,
        out_shape=[
            pltpu.VMEM((rows, width), f32),
            pltpu.VMEM((rows, 1), f32),
            pltpu.VMEM((clips, joint), f32),
            pltpu.VMEM((clips, 1), f32),
            pltpu.VMEM((clips, total), f32),
            jax.ShapeDtypeStruct((1, total), f32),
            pltpu.VMEM((total, joint), bf16),
        ],
        compiler_params=pltpu.CompilerParams(vmem_limit_bytes=24 * MIB),
        cost_estimate=pl.CostEstimate(
            flops=2 * rows * width * hidden.shape[1], bytes_accessed=4 * MIB, transcendentals=0
        ),
        name="embed",
    )(info, inputs, hidden, in_vmem(second_weight), projection, text, groups)


MASKS = (1, 8, 16, 2, 4)


def gather_step(held, mask, later):
    moved = move_across(held, mask)
    return jnp.where(
        later, jnp.concatenate([moved, held]), jnp.concatenate([held, moved])
    )


def sum_over_replicas(values, masks):
    for mask in masks:
        values = values + move_across(values, mask)
    return values


def loss_kernel(
    info,
    sums_ref,
    text_ref,
    projection_ref,
    normed_ref,
    inv_ref,
    unit_ref,
    inv_norm_ref,
    weighted_ref,
    out_ref,
):
    @pl.when(info[4] == 1)
    def _():
        clips = unit_ref.shape[0]
        rows = normed_ref.shape[0]
        text = text_ref[...]
        weighted = weighted_ref[...]
        by_cols = weighted / sums_ref[...]
        by_rows = weighted / jnp.sum(weighted, axis=1, keepdims=True)
        shape = by_rows.shape
        own = (
            lax.broadcasted_iota(jnp.int32, shape, 0) + info[3] * clips
            == lax.broadcasted_iota(jnp.int32, shape, 1)
        )
        coeffs = grad_scale * (by_rows + by_cols - jnp.where(own, 2.0, 0.0))
        audio_grad = (
            jnp.dot(coeffs, text.astype(f32), precision=EXACT, preferred_element_type=f32) * inv_temp
        )
        unit = unit_ref[...]
        emb_grad = (
            audio_grad - unit * jnp.sum(unit * audio_grad, axis=-1, keepdims=True)
        ) * inv_norm_ref[...]
        pooled_grad = lax.dot_general(
            emb_grad,
            projection_ref[...].astype(f32),
            LAST_DIMS,
            precision=EXACT,
            preferred_element_type=f32,
        ) * (1.0 / (rows // clips))
        upstream = lax.dot_general(
            clip_rows(rows, clips),
            pooled_grad,
            (((0,), (0,)), ((), ())),
            precision=EXACT,
            preferred_element_type=f32,
        )
        normed = normed_ref[...]
        mean = jnp.mean(upstream, axis=-1, keepdims=True)
        along = jnp.mean(upstream * normed, axis=-1, keepdims=True)
        grad = (inv_ref[...] * (upstream - mean - normed * along)).astype(bf16)
        per_micro = out_ref.shape[1]
        for m in range(out_ref.shape[0]):
            out_ref[m] = grad[m * per_micro : (m + 1) * per_micro]


def loss_grad(info, sums, text, projection, normed, inv_std, unit, inv_norm, weighted):
    rows, width = normed.shape
    return pl.pallas_call(
        loss_kernel,
        in_specs=[SMEM_SPEC] + [VMEM_SPEC] * 8,
        out_specs=VMEM_SPEC,
        out_shape=pltpu.VMEM((MICRO, rows // MICRO, width), bf16),
        compiler_params=pltpu.CompilerParams(vmem_limit_bytes=24 * MIB),
        name="loss_grad",
    )(
        info,
        sums,
        in_vmem(text),
        projection,
        *[in_vmem(a) for a in (normed, inv_std, unit, inv_norm, weighted)],
    )


def step_kernel(inputs_given, keeps, slot, last_section, section_ref, second_ref, first_ref, slope_ref, normed_ref, inv_ref, *rest):
    count = len(inputs_given)
    given, stores = rest[:count], rest[count : count + 3]
    if keeps:
        passed_ref, out_ref, pre_ref, in_ref = rest[count + 3 :]
    else:
        out_ref, pre_ref, in_ref = rest[count + 3 :]
    section = section_ref[0]
    micro_id = slot - 2 * (last_section - section)
    active = (micro_id >= 0) & (micro_id < MICRO)
    micro = jnp.clip(micro_id, 0, MICRO - 1)

    @pl.when(active)
    def _():
        if count == 2:
            upstream = jnp.where(section == last_section, given[0][micro], given[1][...])
        elif inputs_given[0] == "last":
            upstream = given[0][micro]
        else:
            upstream = given[0][...]
        act_grad = lax.dot_general(
            upstream, second_ref[...], LAST_DIMS, preferred_element_type=f32
        )
        pre_grad = (act_grad * slope_ref[micro]).astype(bf16)
        normed_grad = lax.dot_general(
            pre_grad, first_ref[...], LAST_DIMS, preferred_element_type=f32
        )
        normed = normed_ref[micro].astype(f32)
        mean = jnp.mean(normed_grad, axis=-1, keepdims=True)
        along = jnp.mean(normed_grad * normed, axis=-1, keepdims=True)
        in_grad = upstream.astype(f32) + inv_ref[micro] * (normed_grad - mean - normed * along)
        in_grad = in_grad.astype(bf16)
        if keeps:
            passed_ref[...] = in_grad
            pre_ref[micro] = pre_grad
            out_ref[micro] = upstream
            in_ref[micro] = in_grad
        else:
            pre_ref[...] = pre_grad
            out_ref[...] = upstream
            in_ref[...] = in_grad

    if not keeps:

        @pl.when(jnp.logical_not(active))
        def _():
            for store, last in zip(stores, (out_ref, pre_ref, in_ref)):
                last[...] = store[MICRO - 1]


def chain_step(slot, last_section, section, weights, fixed, given, stores, keeps):
    rows, width = fixed[1].shape[1:]
    wide = fixed[0].shape[2]
    names = tuple(given)
    values = [in_vmem(given[n]) if n == "last" else given[n] for n in names]
    first_store = 1 + 5 + len(names)
    if keeps:
        shapes = [jax.ShapeDtypeStruct((rows, width), bf16)]
        shapes += [pltpu.VMEM(a.shape, a.dtype) for a in stores]
        aliases = {first_store + i: 1 + i for i in range(3)}
    else:
        shapes = [jax.ShapeDtypeStruct((rows, n), bf16) for n in (width, wide, width)]
        aliases = {}
    return pl.pallas_call(
        functools.partial(step_kernel, names, keeps, slot, last_section),
        in_specs=[SMEM_SPEC] + [VMEM_SPEC] * (5 + len(names) + 3),
        out_specs=[VMEM_SPEC] * len(shapes),
        out_shape=shapes,
        input_output_aliases=aliases,
        compiler_params=pltpu.CompilerParams(vmem_limit_bytes=16 * MIB),
        cost_estimate=pl.CostEstimate(flops=3 * 10**9, bytes_accessed=MIB, transcendentals=0),
        name="chain_step",
    )(
        section,
        *[in_vmem(w) for w in weights],
        *[in_vmem(a) for a in fixed],
        *values,
        *[in_vmem(a) for a in stores],
    )


def empty_stores(shapes):
    return pl.pallas_call(
        lambda *refs: None,
        out_specs=[VMEM_SPEC] * len(shapes),
        out_shape=[pltpu.VMEM(s, bf16) for s in shapes],
        compiler_params=pltpu.CompilerParams(vmem_limit_bytes=MIB),
        name="empty_stores",
    )()


def column_halves(turned, at):
    width, rows = turned.shape
    blocks = turned.reshape(HI, COL, CORE, width // (HI * COL * CORE), rows)
    return item_at(blocks, at["core"], 2), item_at(blocks, at["other"], 2)


LOW, HIGH = slice(0, HI // 2), slice(HI // 2, HI)


def term_of(left, right, at, distance, part=slice(None)):
    chosen = item_at(left[part], at["columns"][distance], 1)
    height, rows = chosen.shape[1:]
    product = jnp.dot(chosen.reshape(-1, rows), right, preferred_element_type=f32)
    return product.reshape(-1, height, right.shape[1])


def scatter_total(own, ahead, back):
    return own + ahead.astype(f32) + back.astype(f32)


def scatter_planes(total, at):
    rounded = total.astype(bf16)
    return [move(item_at(rounded, at["hi"][d]), hi=d) for d in (1, 2, 3)]


def scatter_end(total, got, at):
    result = item_at(total, at["hi"][0])
    for block in got:
        result = result + block.astype(f32)
    return result / (HI * COL * CORE)


def pick_kernel(label_ref, text_ref, out_ref):
    text = text_ref[...].astype(f32)
    row = lax.broadcasted_iota(jnp.int32, text.shape, 0)
    label = jnp.zeros(text.shape, jnp.int32)
    for i in range(text.shape[0]):
        label = jnp.where(row == i, label_ref[i // 2, i % 2], label)
    below = jnp.concatenate([text[1:], text[:1]])
    above = jnp.concatenate([text[-1:], text[:-1]])
    slot = row & 1
    other = jnp.where(slot == 0, below, above)
    out_ref[...] = jnp.where(label == slot, text, other).astype(bf16)


def paired_texts(text_embed, pair_label):
    return pl.pallas_call(
        pick_kernel,
        in_specs=[SMEM_SPEC, VMEM_SPEC],
        out_specs=VMEM_SPEC,
        out_shape=jax.ShapeDtypeStruct(text_embed.shape, bf16),
        compiler_params=pltpu.CompilerParams(vmem_limit_bytes=MIB),
        name="paired_texts",
    )(pair_label, text_embed)


def local(section_inputs, in_weight, out_weight, projection, text_embed, pair_label, pool_group):
    inputs = section_inputs[0]
    row_count, width = inputs.shape
    per_micro = row_count // MICRO
    clips = row_count // FRAMES
    wide = in_weight.shape[2]
    half = wide // CORE
    section_count = lax.axis_size("section")
    hi, col, core = place()
    at = dict(
        hi=[(hi + d) & (HI - 1) for d in range(HI)],
        core=core,
        other=1 - core,
        chip=jnp.stack(
            [
                hi,
                col,
                core,
                (col * HI + hi) * CORE + core,
                lax.axis_index("section") == section_count - 1,
            ]
        ).astype(jnp.int32),
        later=[lax.axis_index("replica") & mask != 0 for mask in MASKS],
        section=jnp.full((1,), lax.axis_index("section"), jnp.int32),
        columns=[(col + d) & (COL - 1) for d in range(COL)],
        kept=core * half,
        given=(1 - core) * half,
    )
    at = lax.optimization_barrier(at)

    shard = in_weight[0]
    kept = slice_at(shard, at["kept"], half, 1)
    got = move(slice_at(shard, at["given"], half, 1), core=1)
    first_shard = jnp.where(
        at["core"] == 0, jnp.concatenate([kept, got]), jnp.concatenate([got, kept])
    )
    second_shard = out_weight[0]

    def gathered(texts, step):
        return gather_step(texts, MASKS[step], at["later"][step])

    own = jnp.stack([first_shard, second_shard])
    moved = [move(own, hi=d) for d in (1, 2, 3)]
    own_left, own_right = move(own, col=1), move(own, col=-1)
    own, text_embed, pair_label, pool_group = together(
        own, text_embed, pair_label, pool_group
    )
    texts = paired_texts(text_embed, pair_label)
    groups = pool_group.reshape(HI, COL, CORE).transpose(1, 0, 2).reshape(-1, 1)
    groups = jnp.broadcast_to(groups, (groups.shape[0], clips))
    groups = groups.reshape(1, -1).astype(f32)
    texts = gathered(texts, 0)
    first_own_far = move(own_left[:1], col=1)
    second_own_far = move(own_right[1:], col=-1)
    *moved, texts, groups, first_own_far, second_own_far = together(
        *moved, texts, groups, first_own_far, second_own_far
    )
    stack = jnp.stack(moved, axis=1)
    left, right = move(stack, col=1), move(stack, col=-1)
    for step in (1, 2, 3):
        texts = gathered(texts, step)
    held = [own, own_left, own_right, stack, first_own_far, second_own_far]
    others = [move(a, core=1) for a in held]
    left, right, texts, *others = together(left, right, texts, *others)
    first_far = move(left[0], col=1)
    second_far = move(right[1], col=-1)
    texts = gathered(texts, 4)
    first_far, texts = together(first_far, texts)

    def both(*parts):
        pieces, plan = [], []
        for piece, other, distance, index in parts:
            pieces += [piece, move(piece, core=1) if other is None else other]
            plan += [(distance, side, index) for side in (False, True)]
        return plan, pieces

    near_plan, near_pieces = both(
        (own, others[0], 0, "own"),
        (own_left, others[1], COL - 1, "own"),
        (own_right, others[2], 1, "own"),
        (stack, others[3], 0, "planes"),
        (left, None, COL - 1, "planes"),
        (right, None, 1, "planes"),
    )

    def placed(weight, shape, own_far, other_own_far, far):
        places = dict(
            own=(((weight,), 0),),
            planes=tuple(((weight, d), d + 1) for d in range(HI - 1)),
            far=tuple(((d,), d + 1) for d in range(HI - 1)),
            own_far=(((0,), 0),),
        )

        def run(plan, pieces, whole):
            plan = [(distance, other, places[index]) for distance, other, index in plan]
            return place_blocks(at["chip"], plan, pieces, shape, weight == 0, whole)

        far_plan, far_pieces = both((own_far, other_own_far, 2, "own_far"))
        whole = run(near_plan + far_plan, near_pieces + far_pieces, None)
        return whole, run(*both((far, None, 2, "far")), whole)

    _, first_weight = placed(0, (width, wide), first_own_far, others[4], first_far)
    early, second_weight = placed(1, (wide, width), second_own_far, others[5], second_far)
    normed, inv_in, normed_t, hidden, hidden_t, slope = front(
        inputs, first_weight, early
    )
    normed_halves = column_halves(normed_t, at)
    hidden_halves = column_halves(hidden_t, at)
    out_normed, out_inv, unit, inv_norm, weighted, sums, unit_text = embed(
        at["chip"], inputs, hidden, second_weight, projection, texts, groups
    )
    normed_columns, hidden_columns = (
        jnp.concatenate([own, move(other, core=1)], axis=-1)
        for own, other in (normed_halves, hidden_halves)
    )
    sums = sum_over_replicas(sums, MASKS[:-1])
    sums, normed_columns, hidden_columns = together(sums, normed_columns, hidden_columns)
    sums = sum_over_replicas(sums, MASKS[-1:])
    last_micro = loss_grad(
        at["chip"], sums, unit_text, projection, out_normed, out_inv, unit, inv_norm, weighted
    )

    fixed = (slope, normed, inv_in)
    weights = (second_weight, first_weight)
    stores = empty_stores([(MICRO, per_micro, n) for n in (width, wide, width)])
    arrived = [None, None]
    slots = 2 * (section_count - 1) + MICRO
    for slot in range(slots):
        given = {}
        if slot == slots - 1:
            early = [a[: MICRO - 1].reshape(-1, a.shape[2]) for a in stores]
            arrived[slot], *early = together(arrived[slot], *early)
            crossed = [move(a, core=1) for a in early[:2]]
        if slot < MICRO:
            given["last"] = last_micro
        if arrived[slot] is not None:
            given["next"] = arrived[slot]
        keeps = slot < slots - 1
        results = chain_step(
            slot, section_count - 1, at["section"], weights, fixed, given, stores, keeps
        )
        if not keeps:
            last_out, last_pre, last_in = results
            break
        passed, *stores = results
        route = [
            (s, s - 1)
            for s in range(1, section_count)
            if 0 <= slot - 2 * (section_count - 1 - s) < MICRO
        ]
        arrived.append(lax.ppermute(passed, "section", route) if route else None)

    out_rows, pre_rows = (
        jnp.concatenate([own, last, other, move(last, core=1)])
        for own, last, other in zip(early, (last_out, last_pre), crossed)
    )

    def term(second, distance, part=slice(None)):
        left, right = (hidden_columns, out_rows) if second else (normed_columns, pre_rows)
        return term_of(left, right, at, distance, part)

    def far(second):
        low, high = term(second, 2, LOW).astype(bf16), term(second, 2, HIGH).astype(bf16)
        return move(low, col=1), move(high, col=-1)

    def near(second, low, high):
        ahead, back = term(second, 1), term(second, 3)
        ahead = jnp.concatenate([ahead[LOW] + low.astype(f32), ahead[HIGH]])
        back = jnp.concatenate([back[LOW], back[HIGH] + high.astype(f32)])
        return ahead.astype(bf16), back.astype(bf16)

    low2, high2, low1, high1 = together(*far(True), *far(False))
    ahead2, back2, low1, high1 = together(*near(True, low2, high2), low1, high1)
    ahead2, back2 = move(ahead2, col=1), move(back2, col=-1)
    ahead1, back1 = near(False, low1, high1)
    ahead1, back1 = move(ahead1, col=1), move(back1, col=-1)
    second_total = scatter_total(term(True, 0), ahead2, back2)
    second_got = scatter_planes(second_total, at)
    *second_got, ahead1, back1 = together(*second_got, ahead1, back1)
    first_total = scatter_total(term(False, 0), ahead1, back1)
    first_got = scatter_planes(first_total, at)
    second_sum = scatter_end(second_total, second_got, at)
    first_sum = scatter_end(first_total, first_got, at)
    in_grads = jnp.concatenate([early[2], last_in])
    return (in_grads[None], first_sum[None], second_sum[None])


def solution(mesh):
    return jax.shard_map(
        local,
        mesh=mesh,
        in_specs=(
            P("section", "replica", None),
            P("section", "replica", None),
            P("section", "replica", None),
            P(),
            P("replica", None),
            P("replica", None),
            P(),
        ),
        out_specs=(
            P("section", "replica", None),
            P("section", "replica", None),
            P("section", "replica", None),
        ),
        check_vma=False,
    )
```

```python
import functools

import jax
import jax.numpy as jnp
from jax import lax
from jax.experimental import pallas as pl
from jax.experimental.pallas import tpu as pltpu
from jax.sharding import PartitionSpec as P

MICRO = 4
FRAMES = 44

HI = 4
COL = 4
CORE = 2

MIB = 2**20
LAST_DIMS = (((1,), (1,)), ((), ()))
EXACT = lax.Precision.HIGHEST

eps_norm = 1e-05
eps_unit = 1e-06
inv_temp = 1.0 / 0.07
grad_scale = 256.0
sqrt_half = 0.7071067811865476
inv_sqrt_two_pi = 0.3989422804014327

bf16 = jnp.bfloat16
f32 = jnp.float32


def replica_of(hi, col, core):
    return ((hi % HI) * COL + col % COL) * CORE + core % CORE


def move(block, hi=0, col=0, core=0):
    route = [
        (replica_of(h, c, k), replica_of(h + hi, c + col, k + core))
        for h in range(HI)
        for c in range(COL)
        for k in range(CORE)
    ]
    return lax.ppermute(block, "replica", route)


def place():
    replica = lax.axis_index("replica")
    return replica >> 3, (replica >> 1) & (COL - 1), replica & (CORE - 1)


def together(*values):
    return lax.optimization_barrier(values)


def move_across(block, mask):
    count = HI * COL * CORE
    return lax.ppermute(block, "replica", [(r, r ^ mask) for r in range(count)])


def slice_at(values, start, size, axis):
    return lax.dynamic_slice_in_dim(values, start, size, axis, allow_negative_indices=False)


def item_at(values, index, axis=0):
    return lax.dynamic_index_in_dim(
        values, index, axis, keepdims=False, allow_negative_indices=False
    )


def in_vmem(value):
    return pltpu.with_memory_space_constraint(value, pltpu.VMEM)


VMEM_SPEC = pl.BlockSpec(memory_space=pltpu.VMEM)
ANY_SPEC = pl.BlockSpec(memory_space=pl.ANY)
SMEM_SPEC = pl.BlockSpec(memory_space=pltpu.SMEM)


def place_kernel(plan, by_columns, info, *refs):
    pieces, whole = refs[: len(plan)], refs[-1]
    hi, col, core = info[0], info[1], info[2]
    for (distance, other, blocks), piece in zip(plan, pieces):
        rows, width = piece.shape[-2:]
        at_col = (col + distance) & (COL - 1)
        side = 1 - core if other else core
        for k, back in blocks:
            chip = ((hi + HI - back) & (HI - 1)) * COL + at_col
            if by_columns:
                row = chip * rows
                column = pl.ds(pl.multiple_of(side * width, width), width)
            else:
                row = (chip * CORE + side) * rows
                column = slice(None)
            whole[pl.ds(pl.multiple_of(row, 16), rows), column] = piece[k]


def place_blocks(info, plan, pieces, shape, by_columns, whole=None):
    return pl.pallas_call(
        functools.partial(place_kernel, plan, by_columns),
        in_specs=[SMEM_SPEC]
        + [VMEM_SPEC] * len(pieces)
        + ([] if whole is None else [VMEM_SPEC]),
        out_specs=VMEM_SPEC,
        out_shape=pltpu.VMEM(shape, bf16),
        input_output_aliases={} if whole is None else {1 + len(pieces): 0},
        compiler_params=pltpu.CompilerParams(vmem_limit_bytes=12 * MIB),
        cost_estimate=pl.CostEstimate(
            flops=0, bytes_accessed=2 * sum(p.size for p in pieces), transcendentals=0
        ),
        name="place_blocks",
    )(info, *pieces, *([] if whole is None else [in_vmem(whole)]))


def front_kernel(
    inputs_ref, first_ref, waits_ref, normed_ref, inv_ref, normed_t_ref, hidden_ref, hidden_t_ref, slope_ref
):
    micro, rows = normed_ref.shape[:2]
    values = inputs_ref[...].astype(f32)
    centred = values - jnp.mean(values, axis=-1, keepdims=True)
    inv_std = lax.rsqrt(jnp.mean(centred * centred, axis=-1, keepdims=True) + eps_norm)
    scaled = centred * inv_std
    normed = scaled.astype(bf16)
    for m in range(micro):
        normed_ref[m] = normed[m * rows : (m + 1) * rows]
        inv_ref[m] = inv_std[m * rows : (m + 1) * rows]
    normed_t_ref[...] = scaled.T.astype(bf16)
    step = 256

    @pl.loop(0, first_ref.shape[1] // step)
    def _(j):
        part = pl.ds(pl.multiple_of(j * step, step), step)
        preact = jnp.dot(normed, first_ref[:, part], preferred_element_type=f32)
        cdf = 0.5 * (1.0 + lax.erf(preact * sqrt_half))
        hidden = preact * cdf
        hidden_ref[:, part] = hidden.astype(bf16)
        hidden_t_ref[part, :] = hidden.T.astype(bf16)
        slope = cdf + preact * jnp.exp(-0.5 * preact * preact) * inv_sqrt_two_pi
        for m in range(micro):
            slope_ref[m, :, part] = slope[m * rows : (m + 1) * rows]


def front(inputs, first_weight, waits):
    rows, width = inputs.shape
    wide = first_weight.shape[1]
    per_micro = rows // MICRO
    return pl.pallas_call(
        front_kernel,
        in_specs=[VMEM_SPEC] * 3,
        out_specs=[VMEM_SPEC] * 6,
        out_shape=[
            pltpu.VMEM((MICRO, per_micro, width), bf16),
            pltpu.VMEM((MICRO, per_micro, 1), f32),
            jax.ShapeDtypeStruct((width, rows), bf16),
            jax.ShapeDtypeStruct((rows, wide), bf16),
            jax.ShapeDtypeStruct((wide, rows), bf16),
            pltpu.VMEM((MICRO, per_micro, wide), f32),
        ],
        compiler_params=pltpu.CompilerParams(vmem_limit_bytes=24 * MIB),
        cost_estimate=pl.CostEstimate(
            flops=2 * rows * width * wide, bytes_accessed=4 * MIB, transcendentals=0
        ),
        name="front",
    )(inputs, in_vmem(first_weight), in_vmem(waits))


def clip_rows(rows, clips):
    first = lax.broadcasted_iota(jnp.int32, (clips, rows), 0) * (rows // clips)
    row = lax.broadcasted_iota(jnp.int32, (clips, rows), 1)
    return jnp.where((row >= first) & (row < first + rows // clips), 1.0, 0.0).astype(f32)


def embed_kernel(
    info,
    inputs_ref,
    hidden_ref,
    second_ref,
    projection_ref,
    text_ref,
    group_ref,
    normed_ref,
    inv_ref,
    unit_ref,
    inv_norm_ref,
    weighted_ref,
    sums_ref,
    unit_text_ref,
):
    @pl.when(info[4] == 1)
    def _():
        rows = inputs_ref.shape[0]
        clips = unit_ref.shape[0]
        block_out = inputs_ref[...].astype(f32) + jnp.dot(
            hidden_ref[...], second_ref[...], preferred_element_type=f32
        )
        centred = block_out - jnp.mean(block_out, axis=-1, keepdims=True)
        inv_std = lax.rsqrt(jnp.mean(centred * centred, axis=-1, keepdims=True) + eps_norm)
        normed = centred * inv_std
        normed_ref[...] = normed
        inv_ref[...] = inv_std
        sums = jnp.dot(
            clip_rows(rows, clips), normed, precision=EXACT, preferred_element_type=f32
        )
        pooled = (sums * (1.0 / (rows // clips))).astype(bf16)
        embedded = jnp.dot(pooled, projection_ref[...], preferred_element_type=f32)
        inv_norm = lax.rsqrt(jnp.sum(embedded * embedded, axis=-1, keepdims=True) + eps_unit)
        unit = embedded * inv_norm
        unit_ref[...] = unit
        inv_norm_ref[...] = inv_norm
        text = text_ref[...].astype(f32)
        unit_text = text * lax.rsqrt(jnp.sum(text * text, axis=-1, keepdims=True) + eps_unit)
        unit_text = unit_text.astype(bf16)
        unit_text_ref[...] = unit_text
        scores = (
            lax.dot_general(
                unit.astype(bf16), unit_text, LAST_DIMS, preferred_element_type=f32
            )
            * inv_temp
        )
        group = group_ref[...]
        column = lax.broadcasted_iota(jnp.int32, group.shape, 1)
        own_group = jnp.sum(
            jnp.where(column == info[3] * clips, group, 0.0), axis=1, keepdims=True
        )
        weighted = jnp.where(group == own_group, jnp.exp(scores), 0.0)
        weighted_ref[...] = weighted
        sums_ref[...] = jnp.sum(weighted, axis=0, keepdims=True)


def embed(info, inputs, hidden, second_weight, projection, text, groups):
    rows, width = inputs.shape
    clips = rows // FRAMES
    joint = projection.shape[1]
    total = text.shape[0]
    return pl.pallas_call(
        embed_kernel,
        in_specs=[SMEM_SPEC] + [VMEM_SPEC] * 6,
        out_specs=[VMEM_SPEC] * 7,
        out_shape=[
            pltpu.VMEM((rows, width), f32),
            pltpu.VMEM((rows, 1), f32),
            pltpu.VMEM((clips, joint), f32),
            pltpu.VMEM((clips, 1), f32),
            pltpu.VMEM((clips, total), f32),
            jax.ShapeDtypeStruct((1, total), f32),
            pltpu.VMEM((total, joint), bf16),
        ],
        compiler_params=pltpu.CompilerParams(vmem_limit_bytes=24 * MIB),
        cost_estimate=pl.CostEstimate(
            flops=2 * rows * width * hidden.shape[1], bytes_accessed=4 * MIB, transcendentals=0
        ),
        name="embed",
    )(info, inputs, hidden, in_vmem(second_weight), projection, text, groups)


MASKS = (1, 2, 4, 8, 16)


def gather_step(held, mask, later):
    moved = move_across(held, mask)
    return jnp.where(
        later, jnp.concatenate([moved, held]), jnp.concatenate([held, moved])
    )


def sum_over_replicas(values, masks):
    for mask in masks:
        values = values + move_across(values, mask)
    return values


def loss_kernel(
    info,
    sums_ref,
    text_ref,
    projection_ref,
    normed_ref,
    inv_ref,
    unit_ref,
    inv_norm_ref,
    weighted_ref,
    out_ref,
):
    @pl.when(info[4] == 1)
    def _():
        clips = unit_ref.shape[0]
        rows = normed_ref.shape[0]
        text = text_ref[...]
        weighted = weighted_ref[...]
        by_cols = weighted / sums_ref[...]
        by_rows = weighted / jnp.sum(weighted, axis=1, keepdims=True)
        shape = by_rows.shape
        own = (
            lax.broadcasted_iota(jnp.int32, shape, 0) + info[3] * clips
            == lax.broadcasted_iota(jnp.int32, shape, 1)
        )
        coeffs = grad_scale * (by_rows + by_cols - jnp.where(own, 2.0, 0.0))
        audio_grad = (
            jnp.dot(coeffs, text.astype(f32), precision=EXACT, preferred_element_type=f32) * inv_temp
        )
        unit = unit_ref[...]
        emb_grad = (
            audio_grad - unit * jnp.sum(unit * audio_grad, axis=-1, keepdims=True)
        ) * inv_norm_ref[...]
        pooled_grad = lax.dot_general(
            emb_grad,
            projection_ref[...].astype(f32),
            LAST_DIMS,
            precision=EXACT,
            preferred_element_type=f32,
        ) * (1.0 / (rows // clips))
        upstream = lax.dot_general(
            clip_rows(rows, clips),
            pooled_grad,
            (((0,), (0,)), ((), ())),
            precision=EXACT,
            preferred_element_type=f32,
        )
        normed = normed_ref[...]
        mean = jnp.mean(upstream, axis=-1, keepdims=True)
        along = jnp.mean(upstream * normed, axis=-1, keepdims=True)
        grad = (inv_ref[...] * (upstream - mean - normed * along)).astype(bf16)
        per_micro = out_ref.shape[1]
        for m in range(out_ref.shape[0]):
            out_ref[m] = grad[m * per_micro : (m + 1) * per_micro]


def loss_grad(info, sums, text, projection, normed, inv_std, unit, inv_norm, weighted):
    rows, width = normed.shape
    return pl.pallas_call(
        loss_kernel,
        in_specs=[SMEM_SPEC] + [VMEM_SPEC] * 8,
        out_specs=VMEM_SPEC,
        out_shape=pltpu.VMEM((MICRO, rows // MICRO, width), bf16),
        compiler_params=pltpu.CompilerParams(vmem_limit_bytes=24 * MIB),
        name="loss_grad",
    )(
        info,
        sums,
        in_vmem(text),
        projection,
        *[in_vmem(a) for a in (normed, inv_std, unit, inv_norm, weighted)],
    )


def step_kernel(inputs_given, keeps, slot, last_section, section_ref, second_ref, first_ref, slope_ref, normed_ref, inv_ref, *rest):
    count = len(inputs_given)
    given, stores = rest[:count], rest[count : count + 3]
    if keeps:
        passed_ref, out_ref, pre_ref, in_ref = rest[count + 3 :]
    else:
        out_ref, pre_ref, in_ref = rest[count + 3 :]
    section = section_ref[0]
    micro_id = slot - 2 * (last_section - section)
    active = (micro_id >= 0) & (micro_id < MICRO)
    micro = jnp.clip(micro_id, 0, MICRO - 1)

    @pl.when(active)
    def _():
        if count == 2:
            upstream = jnp.where(section == last_section, given[0][micro], given[1][...])
        elif inputs_given[0] == "last":
            upstream = given[0][micro]
        else:
            upstream = given[0][...]
        act_grad = lax.dot_general(
            upstream, second_ref[...], LAST_DIMS, preferred_element_type=f32
        )
        pre_grad = (act_grad * slope_ref[micro]).astype(bf16)
        normed_grad = lax.dot_general(
            pre_grad, first_ref[...], LAST_DIMS, preferred_element_type=f32
        )
        normed = normed_ref[micro].astype(f32)
        mean = jnp.mean(normed_grad, axis=-1, keepdims=True)
        along = jnp.mean(normed_grad * normed, axis=-1, keepdims=True)
        in_grad = upstream.astype(f32) + inv_ref[micro] * (normed_grad - mean - normed * along)
        in_grad = in_grad.astype(bf16)
        if keeps:
            passed_ref[...] = in_grad
            pre_ref[micro] = pre_grad
            out_ref[micro] = upstream
            in_ref[micro] = in_grad
        else:
            pre_ref[...] = pre_grad
            out_ref[...] = upstream
            in_ref[...] = in_grad

    if not keeps:

        @pl.when(jnp.logical_not(active))
        def _():
            for store, last in zip(stores, (out_ref, pre_ref, in_ref)):
                last[...] = store[MICRO - 1]


def chain_step(slot, last_section, section, weights, fixed, given, stores, keeps):
    rows, width = fixed[1].shape[1:]
    wide = fixed[0].shape[2]
    names = tuple(given)
    values = [in_vmem(given[n]) if n == "last" else given[n] for n in names]
    first_store = 1 + 5 + len(names)
    if keeps:
        shapes = [jax.ShapeDtypeStruct((rows, width), bf16)]
        shapes += [pltpu.VMEM(a.shape, a.dtype) for a in stores]
        aliases = {first_store + i: 1 + i for i in range(3)}
    else:
        shapes = [jax.ShapeDtypeStruct((rows, n), bf16) for n in (width, wide, width)]
        aliases = {}
    return pl.pallas_call(
        functools.partial(step_kernel, names, keeps, slot, last_section),
        in_specs=[SMEM_SPEC] + [VMEM_SPEC] * (5 + len(names) + 3),
        out_specs=[VMEM_SPEC] * len(shapes),
        out_shape=shapes,
        input_output_aliases=aliases,
        compiler_params=pltpu.CompilerParams(vmem_limit_bytes=16 * MIB),
        cost_estimate=pl.CostEstimate(flops=3 * 10**9, bytes_accessed=MIB, transcendentals=0),
        name="chain_step",
    )(
        section,
        *[in_vmem(w) for w in weights],
        *[in_vmem(a) for a in fixed],
        *values,
        *[in_vmem(a) for a in stores],
    )


def empty_stores(shapes):
    return pl.pallas_call(
        lambda *refs: None,
        out_specs=[VMEM_SPEC] * len(shapes),
        out_shape=[pltpu.VMEM(s, bf16) for s in shapes],
        compiler_params=pltpu.CompilerParams(vmem_limit_bytes=MIB),
        name="empty_stores",
    )()


def column_halves(turned, at):
    width, rows = turned.shape
    blocks = turned.reshape(HI, COL, CORE, width // (HI * COL * CORE), rows)
    return item_at(blocks, at["core"], 2), item_at(blocks, at["other"], 2)


LOW, HIGH = slice(0, HI // 2), slice(HI // 2, HI)


def term_of(left, right, at, distance, part=slice(None)):
    chosen = item_at(left[part], at["columns"][distance], 1)
    height, rows = chosen.shape[1:]
    product = jnp.dot(chosen.reshape(-1, rows), right, preferred_element_type=f32)
    return product.reshape(-1, height, right.shape[1])


def scatter_total(own, ahead, back):
    return own + ahead.astype(f32) + back.astype(f32)


def scatter_planes(total, at):
    rounded = total.astype(bf16)
    return [move(item_at(rounded, at["hi"][d]), hi=d) for d in (1, 2, 3)]


def scatter_end(total, got, at):
    result = item_at(total, at["hi"][0])
    for block in got:
        result = result + block.astype(f32)
    return result / (HI * COL * CORE)


def pick_kernel(label_ref, text_ref, out_ref):
    text = text_ref[...].astype(f32)
    row = lax.broadcasted_iota(jnp.int32, text.shape, 0)
    label = jnp.zeros(text.shape, jnp.int32)
    for i in range(text.shape[0]):
        label = jnp.where(row == i, label_ref[i // 2, i % 2], label)
    below = jnp.concatenate([text[1:], text[:1]])
    above = jnp.concatenate([text[-1:], text[:-1]])
    slot = row & 1
    other = jnp.where(slot == 0, below, above)
    out_ref[...] = jnp.where(label == slot, text, other).astype(bf16)


def paired_texts(text_embed, pair_label):
    return pl.pallas_call(
        pick_kernel,
        in_specs=[SMEM_SPEC, VMEM_SPEC],
        out_specs=VMEM_SPEC,
        out_shape=jax.ShapeDtypeStruct(text_embed.shape, bf16),
        compiler_params=pltpu.CompilerParams(vmem_limit_bytes=MIB),
        name="paired_texts",
    )(pair_label, text_embed)


def local(section_inputs, in_weight, out_weight, projection, text_embed, pair_label, pool_group):
    inputs = section_inputs[0]
    row_count, width = inputs.shape
    per_micro = row_count // MICRO
    clips = row_count // FRAMES
    wide = in_weight.shape[2]
    half = wide // CORE
    section_count = lax.axis_size("section")
    hi, col, core = place()
    at = dict(
        hi=[(hi + d) & (HI - 1) for d in range(HI)],
        core=core,
        other=1 - core,
        chip=jnp.stack(
            [
                hi,
                col,
                core,
                lax.axis_index("replica"),
                lax.axis_index("section") == section_count - 1,
            ]
        ).astype(jnp.int32),
        later=[lax.axis_index("replica") & mask != 0 for mask in MASKS],
        section=jnp.full((1,), lax.axis_index("section"), jnp.int32),
        columns=[(col + d) & (COL - 1) for d in range(COL)],
        kept=core * half,
        given=(1 - core) * half,
    )
    at = lax.optimization_barrier(at)

    shard = in_weight[0]
    kept = slice_at(shard, at["kept"], half, 1)
    got = move(slice_at(shard, at["given"], half, 1), core=1)
    first_shard = jnp.where(
        at["core"] == 0, jnp.concatenate([kept, got]), jnp.concatenate([got, kept])
    )
    second_shard = out_weight[0]

    def gathered(texts, step):
        return gather_step(texts, MASKS[step], at["later"][step])

    own = jnp.stack([first_shard, second_shard])
    moved = [move(own, hi=d) for d in (1, 2, 3)]
    own_left, own_right = move(own, col=1), move(own, col=-1)
    own, text_embed, pair_label, pool_group = together(
        own, text_embed, pair_label, pool_group
    )
    texts = paired_texts(text_embed, pair_label)
    groups = jnp.broadcast_to(pool_group[:, None], (pool_group.shape[0], clips))
    groups = groups.reshape(1, -1).astype(f32)
    texts = gathered(texts, 0)
    first_own_far = move(own_left[:1], col=1)
    second_own_far = move(own_right[1:], col=-1)
    *moved, texts, groups, first_own_far, second_own_far = together(
        *moved, texts, groups, first_own_far, second_own_far
    )
    stack = jnp.stack(moved, axis=1)
    left, right = move(stack, col=1), move(stack, col=-1)
    for step in (1, 2, 3):
        texts = gathered(texts, step)
    held = [own, own_left, own_right, stack, first_own_far, second_own_far]
    others = [move(a, core=1) for a in held]
    left, right, texts, *others = together(left, right, texts, *others)
    first_far = move(left[0], col=1)
    second_far = move(right[1], col=-1)
    texts = gathered(texts, 4)
    first_far, texts = together(first_far, texts)

    def both(*parts):
        pieces, plan = [], []
        for piece, other, distance, index in parts:
            pieces += [piece, move(piece, core=1) if other is None else other]
            plan += [(distance, side, index) for side in (False, True)]
        return plan, pieces

    near_plan, near_pieces = both(
        (own, others[0], 0, "own"),
        (own_left, others[1], COL - 1, "own"),
        (own_right, others[2], 1, "own"),
        (stack, others[3], 0, "planes"),
        (left, None, COL - 1, "planes"),
        (right, None, 1, "planes"),
    )

    def placed(weight, shape, own_far, other_own_far, far):
        places = dict(
            own=(((weight,), 0),),
            planes=tuple(((weight, d), d + 1) for d in range(HI - 1)),
            far=tuple(((d,), d + 1) for d in range(HI - 1)),
            own_far=(((0,), 0),),
        )

        def run(plan, pieces, whole):
            plan = [(distance, other, places[index]) for distance, other, index in plan]
            return place_blocks(at["chip"], plan, pieces, shape, weight == 0, whole)

        far_plan, far_pieces = both((own_far, other_own_far, 2, "own_far"))
        whole = run(near_plan + far_plan, near_pieces + far_pieces, None)
        return whole, run(*both((far, None, 2, "far")), whole)

    _, first_weight = placed(0, (width, wide), first_own_far, others[4], first_far)
    early, second_weight = placed(1, (wide, width), second_own_far, others[5], second_far)
    normed, inv_in, normed_t, hidden, hidden_t, slope = front(
        inputs, first_weight, early
    )
    normed_halves = column_halves(normed_t, at)
    hidden_halves = column_halves(hidden_t, at)
    out_normed, out_inv, unit, inv_norm, weighted, sums, unit_text = embed(
        at["chip"], inputs, hidden, second_weight, projection, texts, groups
    )
    normed_columns, hidden_columns = (
        jnp.concatenate([own, move(other, core=1)], axis=-1)
        for own, other in (normed_halves, hidden_halves)
    )
    sums = sum_over_replicas(sums, MASKS[:-1])
    sums, normed_columns, hidden_columns = together(sums, normed_columns, hidden_columns)
    sums = sum_over_replicas(sums, MASKS[-1:])
    last_micro = loss_grad(
        at["chip"], sums, unit_text, projection, out_normed, out_inv, unit, inv_norm, weighted
    )

    fixed = (slope, normed, inv_in)
    weights = (second_weight, first_weight)
    stores = empty_stores([(MICRO, per_micro, n) for n in (width, wide, width)])
    arrived = [None, None]
    slots = 2 * (section_count - 1) + MICRO
    for slot in range(slots):
        given = {}
        if slot == slots - 1:
            early = [a[: MICRO - 1].reshape(-1, a.shape[2]) for a in stores]
            arrived[slot], *early = together(arrived[slot], *early)
            crossed = [move(a, core=1) for a in early[:2]]
        if slot < MICRO:
            given["last"] = last_micro
        if arrived[slot] is not None:
            given["next"] = arrived[slot]
        keeps = slot < slots - 1
        results = chain_step(
            slot, section_count - 1, at["section"], weights, fixed, given, stores, keeps
        )
        if not keeps:
            last_out, last_pre, last_in = results
            break
        passed, *stores = results
        route = [
            (s, s - 1)
            for s in range(1, section_count)
            if 0 <= slot - 2 * (section_count - 1 - s) < MICRO
        ]
        arrived.append(lax.ppermute(passed, "section", route) if route else None)

    out_rows, pre_rows = (
        jnp.concatenate([own, last, other, move(last, core=1)])
        for own, last, other in zip(early, (last_out, last_pre), crossed)
    )

    def term(second, distance, part=slice(None)):
        left, right = (hidden_columns, out_rows) if second else (normed_columns, pre_rows)
        return term_of(left, right, at, distance, part)

    def far(second):
        low, high = term(second, 2, LOW).astype(bf16), term(second, 2, HIGH).astype(bf16)
        return move(low, col=1), move(high, col=-1)

    def near(second, low, high):
        ahead, back = term(second, 1), term(second, 3)
        ahead = jnp.concatenate([ahead[LOW] + low.astype(f32), ahead[HIGH]])
        back = jnp.concatenate([back[LOW], back[HIGH] + high.astype(f32)])
        return move(ahead.astype(bf16), col=1), move(back.astype(bf16), col=-1)

    low2, high2, low1, high1 = together(*far(True), *far(False))
    ahead2, back2 = near(True, low2, high2)
    ahead2, back2, low1, high1 = together(ahead2, back2, low1, high1)
    ahead1, back1 = near(False, low1, high1)
    second_total = scatter_total(term(True, 0), ahead2, back2)
    second_got = scatter_planes(second_total, at)
    *second_got, ahead1, back1 = together(*second_got, ahead1, back1)
    first_total = scatter_total(term(False, 0), ahead1, back1)
    first_got = scatter_planes(first_total, at)
    second_sum = scatter_end(second_total, second_got, at)
    first_sum = scatter_end(first_total, first_got, at)
    in_grads = jnp.concatenate([early[2], last_in])
    return (in_grads[None], first_sum[None], second_sum[None])


def solution(mesh):
    return jax.shard_map(
        local,
        mesh=mesh,
        in_specs=(
            P("section", "replica", None),
            P("section", "replica", None),
            P("section", "replica", None),
            P(),
            P("replica", None),
            P("replica", None),
            P(),
        ),
        out_specs=(
            P("section", "replica", None),
            P("section", "replica", None),
            P("section", "replica", None),
        ),
        check_vma=False,
    )
```

```python
import functools

import jax
import jax.numpy as jnp
from jax import lax
from jax.experimental import pallas as pl
from jax.experimental.pallas import tpu as pltpu
from jax.sharding import PartitionSpec as P

MICRO = 4
FRAMES = 44

HI = 4
COL = 4
CORE = 2

MIB = 2**20
LAST_DIMS = (((1,), (1,)), ((), ()))
EXACT = lax.Precision.HIGHEST

eps_norm = 1e-05
eps_unit = 1e-06
inv_temp = 1.0 / 0.07
grad_scale = 256.0
sqrt_half = 0.7071067811865476
inv_sqrt_two_pi = 0.3989422804014327

bf16 = jnp.bfloat16
f32 = jnp.float32


def replica_of(hi, col, core):
    return ((hi % HI) * COL + col % COL) * CORE + core % CORE


def move(block, hi=0, col=0, core=0):
    route = [
        (replica_of(h, c, k), replica_of(h + hi, c + col, k + core))
        for h in range(HI)
        for c in range(COL)
        for k in range(CORE)
    ]
    return lax.ppermute(block, "replica", route)


def place():
    replica = lax.axis_index("replica")
    return replica >> 3, (replica >> 1) & (COL - 1), replica & (CORE - 1)


def together(*values):
    return lax.optimization_barrier(values)


def move_across(block, mask):
    count = HI * COL * CORE
    return lax.ppermute(block, "replica", [(r, r ^ mask) for r in range(count)])


def slice_at(values, start, size, axis):
    return lax.dynamic_slice_in_dim(values, start, size, axis, allow_negative_indices=False)


def item_at(values, index, axis=0):
    return lax.dynamic_index_in_dim(
        values, index, axis, keepdims=False, allow_negative_indices=False
    )


def in_vmem(value):
    return pltpu.with_memory_space_constraint(value, pltpu.VMEM)


VMEM_SPEC = pl.BlockSpec(memory_space=pltpu.VMEM)
ANY_SPEC = pl.BlockSpec(memory_space=pl.ANY)
SMEM_SPEC = pl.BlockSpec(memory_space=pltpu.SMEM)


def place_kernel(plan, by_columns, info, *refs):
    pieces, whole = refs[: len(plan)], refs[-1]
    hi, col, core = info[0], info[1], info[2]
    for (distance, other, blocks), piece in zip(plan, pieces):
        rows, width = piece.shape[-2:]
        at_col = (col + distance) & (COL - 1)
        side = 1 - core if other else core
        for k, back in blocks:
            chip = ((hi + HI - back) & (HI - 1)) * COL + at_col
            if by_columns:
                row = chip * rows
                column = pl.ds(pl.multiple_of(side * width, width), width)
            else:
                row = (chip * CORE + side) * rows
                column = slice(None)
            whole[pl.ds(pl.multiple_of(row, 16), rows), column] = piece[k]


def place_blocks(info, plan, pieces, shape, by_columns, whole=None):
    return pl.pallas_call(
        functools.partial(place_kernel, plan, by_columns),
        in_specs=[SMEM_SPEC]
        + [VMEM_SPEC] * len(pieces)
        + ([] if whole is None else [VMEM_SPEC]),
        out_specs=VMEM_SPEC,
        out_shape=pltpu.VMEM(shape, bf16),
        input_output_aliases={} if whole is None else {1 + len(pieces): 0},
        compiler_params=pltpu.CompilerParams(vmem_limit_bytes=12 * MIB),
        cost_estimate=pl.CostEstimate(
            flops=0, bytes_accessed=2 * sum(p.size for p in pieces), transcendentals=0
        ),
        name="place_blocks",
    )(info, *pieces, *([] if whole is None else [in_vmem(whole)]))


def front_kernel(
    inputs_ref, first_ref, waits_ref, normed_ref, inv_ref, normed_t_ref, hidden_ref, hidden_t_ref, slope_ref
):
    micro, rows = normed_ref.shape[:2]
    values = inputs_ref[...].astype(f32)
    centred = values - jnp.mean(values, axis=-1, keepdims=True)
    inv_std = lax.rsqrt(jnp.mean(centred * centred, axis=-1, keepdims=True) + eps_norm)
    scaled = centred * inv_std
    normed = scaled.astype(bf16)
    for m in range(micro):
        normed_ref[m] = normed[m * rows : (m + 1) * rows]
        inv_ref[m] = inv_std[m * rows : (m + 1) * rows]
    normed_t_ref[...] = scaled.T.astype(bf16)
    step = 256

    @pl.loop(0, first_ref.shape[1] // step)
    def _(j):
        part = pl.ds(pl.multiple_of(j * step, step), step)
        preact = jnp.dot(normed, first_ref[:, part], preferred_element_type=f32)
        cdf = 0.5 * (1.0 + lax.erf(preact * sqrt_half))
        hidden = preact * cdf
        hidden_ref[:, part] = hidden.astype(bf16)
        hidden_t_ref[part, :] = hidden.T.astype(bf16)
        slope = cdf + preact * jnp.exp(-0.5 * preact * preact) * inv_sqrt_two_pi
        for m in range(micro):
            slope_ref[m, :, part] = slope[m * rows : (m + 1) * rows]


def front(inputs, first_weight, waits):
    rows, width = inputs.shape
    wide = first_weight.shape[1]
    per_micro = rows // MICRO
    return pl.pallas_call(
        front_kernel,
        in_specs=[VMEM_SPEC] * 3,
        out_specs=[VMEM_SPEC] * 6,
        out_shape=[
            pltpu.VMEM((MICRO, per_micro, width), bf16),
            pltpu.VMEM((MICRO, per_micro, 1), f32),
            jax.ShapeDtypeStruct((width, rows), bf16),
            jax.ShapeDtypeStruct((rows, wide), bf16),
            jax.ShapeDtypeStruct((wide, rows), bf16),
            pltpu.VMEM((MICRO, per_micro, wide), f32),
        ],
        compiler_params=pltpu.CompilerParams(vmem_limit_bytes=24 * MIB),
        cost_estimate=pl.CostEstimate(
            flops=2 * rows * width * wide, bytes_accessed=4 * MIB, transcendentals=0
        ),
        name="front",
    )(inputs, in_vmem(first_weight), in_vmem(waits))


def clip_rows(rows, clips):
    first = lax.broadcasted_iota(jnp.int32, (clips, rows), 0) * (rows // clips)
    row = lax.broadcasted_iota(jnp.int32, (clips, rows), 1)
    return jnp.where((row >= first) & (row < first + rows // clips), 1.0, 0.0).astype(f32)


def embed_kernel(
    info,
    inputs_ref,
    hidden_ref,
    second_ref,
    projection_ref,
    text_ref,
    group_ref,
    normed_ref,
    inv_ref,
    unit_ref,
    inv_norm_ref,
    weighted_ref,
    sums_ref,
    unit_text_ref,
):
    @pl.when(info[4] == 1)
    def _():
        rows = inputs_ref.shape[0]
        clips = unit_ref.shape[0]
        block_out = inputs_ref[...].astype(f32) + jnp.dot(
            hidden_ref[...], second_ref[...], preferred_element_type=f32
        )
        centred = block_out - jnp.mean(block_out, axis=-1, keepdims=True)
        inv_std = lax.rsqrt(jnp.mean(centred * centred, axis=-1, keepdims=True) + eps_norm)
        normed = centred * inv_std
        normed_ref[...] = normed
        inv_ref[...] = inv_std
        sums = jnp.dot(
            clip_rows(rows, clips), normed, precision=EXACT, preferred_element_type=f32
        )
        pooled = (sums * (1.0 / (rows // clips))).astype(bf16)
        embedded = jnp.dot(pooled, projection_ref[...], preferred_element_type=f32)
        inv_norm = lax.rsqrt(jnp.sum(embedded * embedded, axis=-1, keepdims=True) + eps_unit)
        unit = embedded * inv_norm
        unit_ref[...] = unit
        inv_norm_ref[...] = inv_norm
        text = text_ref[...].astype(f32)
        unit_text = text * lax.rsqrt(jnp.sum(text * text, axis=-1, keepdims=True) + eps_unit)
        unit_text = unit_text.astype(bf16)
        unit_text_ref[...] = unit_text
        scores = (
            lax.dot_general(
                unit.astype(bf16), unit_text, LAST_DIMS, preferred_element_type=f32
            )
            * inv_temp
        )
        group = group_ref[...]
        column = lax.broadcasted_iota(jnp.int32, group.shape, 1)
        own_group = jnp.sum(
            jnp.where(column == info[3] * clips, group, 0.0), axis=1, keepdims=True
        )
        weighted = jnp.where(group == own_group, jnp.exp(scores), 0.0)
        weighted_ref[...] = weighted
        sums_ref[...] = jnp.sum(weighted, axis=0, keepdims=True)


def embed(info, inputs, hidden, second_weight, projection, text, groups):
    rows, width = inputs.shape
    clips = rows // FRAMES
    joint = projection.shape[1]
    total = text.shape[0]
    return pl.pallas_call(
        embed_kernel,
        in_specs=[SMEM_SPEC] + [VMEM_SPEC] * 6,
        out_specs=[VMEM_SPEC] * 7,
        out_shape=[
            pltpu.VMEM((rows, width), f32),
            pltpu.VMEM((rows, 1), f32),
            pltpu.VMEM((clips, joint), f32),
            pltpu.VMEM((clips, 1), f32),
            pltpu.VMEM((clips, total), f32),
            jax.ShapeDtypeStruct((1, total), f32),
            pltpu.VMEM((total, joint), bf16),
        ],
        compiler_params=pltpu.CompilerParams(vmem_limit_bytes=24 * MIB),
        cost_estimate=pl.CostEstimate(
            flops=2 * rows * width * hidden.shape[1], bytes_accessed=4 * MIB, transcendentals=0
        ),
        name="embed",
    )(info, inputs, hidden, in_vmem(second_weight), projection, text, groups)


MASKS = (1, 8, 16, 2, 4)


def gather_step(held, mask, later):
    moved = move_across(held, mask)
    return jnp.where(
        later, jnp.concatenate([moved, held]), jnp.concatenate([held, moved])
    )


def sum_over_replicas(values, masks):
    for mask in masks:
        values = values + move_across(values, mask)
    return values


def loss_kernel(
    info,
    sums_ref,
    text_ref,
    projection_ref,
    normed_ref,
    inv_ref,
    unit_ref,
    inv_norm_ref,
    weighted_ref,
    out_ref,
):
    @pl.when(info[4] == 1)
    def _():
        clips = unit_ref.shape[0]
        rows = normed_ref.shape[0]
        text = text_ref[...]
        weighted = weighted_ref[...]
        by_cols = weighted / sums_ref[...]
        by_rows = weighted / jnp.sum(weighted, axis=1, keepdims=True)
        shape = by_rows.shape
        own = (
            lax.broadcasted_iota(jnp.int32, shape, 0) + info[3] * clips
            == lax.broadcasted_iota(jnp.int32, shape, 1)
        )
        coeffs = grad_scale * (by_rows + by_cols - jnp.where(own, 2.0, 0.0))
        audio_grad = (
            jnp.dot(coeffs, text.astype(f32), precision=EXACT, preferred_element_type=f32) * inv_temp
        )
        unit = unit_ref[...]
        emb_grad = (
            audio_grad - unit * jnp.sum(unit * audio_grad, axis=-1, keepdims=True)
        ) * inv_norm_ref[...]
        pooled_grad = lax.dot_general(
            emb_grad,
            projection_ref[...].astype(f32),
            LAST_DIMS,
            precision=EXACT,
            preferred_element_type=f32,
        ) * (1.0 / (rows // clips))
        upstream = lax.dot_general(
            clip_rows(rows, clips),
            pooled_grad,
            (((0,), (0,)), ((), ())),
            precision=EXACT,
            preferred_element_type=f32,
        )
        normed = normed_ref[...]
        mean = jnp.mean(upstream, axis=-1, keepdims=True)
        along = jnp.mean(upstream * normed, axis=-1, keepdims=True)
        grad = (inv_ref[...] * (upstream - mean - normed * along)).astype(bf16)
        per_micro = out_ref.shape[1]
        for m in range(out_ref.shape[0]):
            out_ref[m] = grad[m * per_micro : (m + 1) * per_micro]


def loss_grad(info, sums, text, projection, normed, inv_std, unit, inv_norm, weighted):
    rows, width = normed.shape
    return pl.pallas_call(
        loss_kernel,
        in_specs=[SMEM_SPEC] + [VMEM_SPEC] * 8,
        out_specs=VMEM_SPEC,
        out_shape=pltpu.VMEM((MICRO, rows // MICRO, width), bf16),
        compiler_params=pltpu.CompilerParams(vmem_limit_bytes=24 * MIB),
        name="loss_grad",
    )(
        info,
        sums,
        in_vmem(text),
        projection,
        *[in_vmem(a) for a in (normed, inv_std, unit, inv_norm, weighted)],
    )


def step_kernel(inputs_given, keeps, slot, last_section, section_ref, second_ref, first_ref, slope_ref, normed_ref, inv_ref, *rest):
    count = len(inputs_given)
    given, stores = rest[:count], rest[count : count + 3]
    if keeps:
        passed_ref, out_ref, pre_ref, in_ref = rest[count + 3 :]
    else:
        out_ref, pre_ref, in_ref = rest[count + 3 :]
    section = section_ref[0]
    micro_id = slot - 2 * (last_section - section)
    active = (micro_id >= 0) & (micro_id < MICRO)
    micro = jnp.clip(micro_id, 0, MICRO - 1)

    @pl.when(active)
    def _():
        if count == 2:
            upstream = jnp.where(section == last_section, given[0][micro], given[1][...])
        elif inputs_given[0] == "last":
            upstream = given[0][micro]
        else:
            upstream = given[0][...]
        act_grad = lax.dot_general(
            upstream, second_ref[...], LAST_DIMS, preferred_element_type=f32
        )
        pre_grad = (act_grad * slope_ref[micro]).astype(bf16)
        normed_grad = lax.dot_general(
            pre_grad, first_ref[...], LAST_DIMS, preferred_element_type=f32
        )
        normed = normed_ref[micro].astype(f32)
        mean = jnp.mean(normed_grad, axis=-1, keepdims=True)
        along = jnp.mean(normed_grad * normed, axis=-1, keepdims=True)
        in_grad = upstream.astype(f32) + inv_ref[micro] * (normed_grad - mean - normed * along)
        in_grad = in_grad.astype(bf16)
        if keeps:
            passed_ref[...] = in_grad
            pre_ref[micro] = pre_grad
            out_ref[micro] = upstream
            in_ref[micro] = in_grad
        else:
            pre_ref[...] = pre_grad
            out_ref[...] = upstream
            in_ref[...] = in_grad

    if not keeps:

        @pl.when(jnp.logical_not(active))
        def _():
            for store, last in zip(stores, (out_ref, pre_ref, in_ref)):
                last[...] = store[MICRO - 1]


def chain_step(slot, last_section, section, weights, fixed, given, stores, keeps):
    rows, width = fixed[1].shape[1:]
    wide = fixed[0].shape[2]
    names = tuple(given)
    values = [in_vmem(given[n]) if n == "last" else given[n] for n in names]
    first_store = 1 + 5 + len(names)
    if keeps:
        shapes = [jax.ShapeDtypeStruct((rows, width), bf16)]
        shapes += [pltpu.VMEM(a.shape, a.dtype) for a in stores]
        aliases = {first_store + i: 1 + i for i in range(3)}
    else:
        shapes = [jax.ShapeDtypeStruct((rows, n), bf16) for n in (width, wide, width)]
        aliases = {}
    return pl.pallas_call(
        functools.partial(step_kernel, names, keeps, slot, last_section),
        in_specs=[SMEM_SPEC] + [VMEM_SPEC] * (5 + len(names) + 3),
        out_specs=[VMEM_SPEC] * len(shapes),
        out_shape=shapes,
        input_output_aliases=aliases,
        compiler_params=pltpu.CompilerParams(vmem_limit_bytes=16 * MIB),
        cost_estimate=pl.CostEstimate(flops=3 * 10**9, bytes_accessed=MIB, transcendentals=0),
        name="chain_step",
    )(
        section,
        *[in_vmem(w) for w in weights],
        *[in_vmem(a) for a in fixed],
        *values,
        *[in_vmem(a) for a in stores],
    )


def empty_stores(shapes):
    return pl.pallas_call(
        lambda *refs: None,
        out_specs=[VMEM_SPEC] * len(shapes),
        out_shape=[pltpu.VMEM(s, bf16) for s in shapes],
        compiler_params=pltpu.CompilerParams(vmem_limit_bytes=MIB),
        name="empty_stores",
    )()


def column_halves(turned, at):
    width, rows = turned.shape
    blocks = turned.reshape(HI, COL, CORE, width // (HI * COL * CORE), rows)
    return item_at(blocks, at["core"], 2), item_at(blocks, at["other"], 2)


LOW, HIGH = slice(0, HI // 2), slice(HI // 2, HI)


def term_of(left, right, at, distance, part=slice(None)):
    chosen = item_at(left[part], at["columns"][distance], 1)
    height, rows = chosen.shape[1:]
    product = jnp.dot(chosen.reshape(-1, rows), right, preferred_element_type=f32)
    return product.reshape(-1, height, right.shape[1])


def scatter_total(own, ahead, back):
    return own + ahead.astype(f32) + back.astype(f32)


def scatter_planes(total, at):
    rounded = total.astype(bf16)
    return [move(item_at(rounded, at["hi"][d]), hi=d) for d in (1, 2, 3)]


def scatter_end(total, got, at):
    result = item_at(total, at["hi"][0])
    for block in got:
        result = result + block.astype(f32)
    return result / (HI * COL * CORE)


def pick_kernel(label_ref, text_ref, out_ref):
    text = text_ref[...].astype(f32)
    row = lax.broadcasted_iota(jnp.int32, text.shape, 0)
    label = jnp.zeros(text.shape, jnp.int32)
    for i in range(text.shape[0]):
        label = jnp.where(row == i, label_ref[i // 2, i % 2], label)
    below = jnp.concatenate([text[1:], text[:1]])
    above = jnp.concatenate([text[-1:], text[:-1]])
    slot = row & 1
    other = jnp.where(slot == 0, below, above)
    out_ref[...] = jnp.where(label == slot, text, other).astype(bf16)


def paired_texts(text_embed, pair_label):
    return pl.pallas_call(
        pick_kernel,
        in_specs=[SMEM_SPEC, VMEM_SPEC],
        out_specs=VMEM_SPEC,
        out_shape=jax.ShapeDtypeStruct(text_embed.shape, bf16),
        compiler_params=pltpu.CompilerParams(vmem_limit_bytes=MIB),
        name="paired_texts",
    )(pair_label, text_embed)


def local(section_inputs, in_weight, out_weight, projection, text_embed, pair_label, pool_group):
    inputs = section_inputs[0]
    row_count, width = inputs.shape
    per_micro = row_count // MICRO
    clips = row_count // FRAMES
    wide = in_weight.shape[2]
    half = wide // CORE
    section_count = lax.axis_size("section")
    hi, col, core = place()
    at = dict(
        hi=[(hi + d) & (HI - 1) for d in range(HI)],
        core=core,
        other=1 - core,
        chip=jnp.stack(
            [
                hi,
                col,
                core,
                (col * HI + hi) * CORE + core,
                lax.axis_index("section") == section_count - 1,
            ]
        ).astype(jnp.int32),
        later=[lax.axis_index("replica") & mask != 0 for mask in MASKS],
        section=jnp.full((1,), lax.axis_index("section"), jnp.int32),
        columns=[(col + d) & (COL - 1) for d in range(COL)],
        kept=core * half,
        given=(1 - core) * half,
    )
    at = lax.optimization_barrier(at)

    shard = in_weight[0]
    kept = slice_at(shard, at["kept"], half, 1)
    got = move(slice_at(shard, at["given"], half, 1), core=1)
    first_shard = jnp.where(
        at["core"] == 0, jnp.concatenate([kept, got]), jnp.concatenate([got, kept])
    )
    second_shard = out_weight[0]

    def gathered(texts, step):
        return gather_step(texts, MASKS[step], at["later"][step])

    own = jnp.stack([first_shard, second_shard])
    moved = [move(own, hi=d) for d in (1, 2, 3)]
    own_left, own_right = move(own, col=1), move(own, col=-1)
    own, text_embed, pair_label, pool_group = together(
        own, text_embed, pair_label, pool_group
    )
    texts = paired_texts(text_embed, pair_label)
    groups = pool_group.reshape(HI, COL, CORE).transpose(1, 0, 2).reshape(-1, 1)
    groups = jnp.broadcast_to(groups, (groups.shape[0], clips))
    groups = groups.reshape(1, -1).astype(f32)
    texts = gathered(texts, 0)
    first_own_far = move(own_left[:1], col=1)
    second_own_far = move(own_right[1:], col=-1)
    *moved, texts, groups, first_own_far, second_own_far = together(
        *moved, texts, groups, first_own_far, second_own_far
    )
    stack = jnp.stack(moved, axis=1)
    left, right = move(stack, col=1), move(stack, col=-1)
    for step in (1, 2, 3):
        texts = gathered(texts, step)
    held = [own, own_left, own_right, stack, first_own_far, second_own_far]
    others = [move(a, core=1) for a in held]
    left, right, texts, *others = together(left, right, texts, *others)
    first_far = move(left[0], col=1)
    second_far = move(right[1], col=-1)
    texts = gathered(texts, 4)
    first_far, texts = together(first_far, texts)

    def both(*parts):
        pieces, plan = [], []
        for piece, other, distance, index in parts:
            pieces += [piece, move(piece, core=1) if other is None else other]
            plan += [(distance, side, index) for side in (False, True)]
        return plan, pieces

    near_plan, near_pieces = both(
        (own, others[0], 0, "own"),
        (own_left, others[1], COL - 1, "own"),
        (own_right, others[2], 1, "own"),
        (stack, others[3], 0, "planes"),
        (left, None, COL - 1, "planes"),
        (right, None, 1, "planes"),
    )

    def placed(weight, shape, own_far, other_own_far, far):
        places = dict(
            own=(((weight,), 0),),
            planes=tuple(((weight, d), d + 1) for d in range(HI - 1)),
            far=tuple(((d,), d + 1) for d in range(HI - 1)),
            own_far=(((0,), 0),),
        )

        def run(plan, pieces, whole):
            plan = [(distance, other, places[index]) for distance, other, index in plan]
            return place_blocks(at["chip"], plan, pieces, shape, weight == 0, whole)

        far_plan, far_pieces = both((own_far, other_own_far, 2, "own_far"))
        whole = run(near_plan + far_plan, near_pieces + far_pieces, None)
        return whole, run(*both((far, None, 2, "far")), whole)

    _, first_weight = placed(0, (width, wide), first_own_far, others[4], first_far)
    early, second_weight = placed(1, (wide, width), second_own_far, others[5], second_far)
    normed, inv_in, normed_t, hidden, hidden_t, slope = front(
        inputs, first_weight, early
    )
    normed_halves = column_halves(normed_t, at)
    hidden_halves = column_halves(hidden_t, at)
    out_normed, out_inv, unit, inv_norm, weighted, sums, unit_text = embed(
        at["chip"], inputs, hidden, second_weight, projection, texts, groups
    )
    normed_columns, hidden_columns = (
        jnp.concatenate([own, move(other, core=1)], axis=-1)
        for own, other in (normed_halves, hidden_halves)
    )
    sums = sum_over_replicas(sums, MASKS[:-1])
    sums, normed_columns, hidden_columns = together(sums, normed_columns, hidden_columns)
    sums = sum_over_replicas(sums, MASKS[-1:])
    last_micro = loss_grad(
        at["chip"], sums, unit_text, projection, out_normed, out_inv, unit, inv_norm, weighted
    )

    fixed = (slope, normed, inv_in)
    weights = (second_weight, first_weight)
    stores = empty_stores([(MICRO, per_micro, n) for n in (width, wide, width)])
    arrived = [None, None]
    slots = 2 * (section_count - 1) + MICRO
    for slot in range(slots):
        given = {}
        if slot == slots - 1:
            early = [a[: MICRO - 1].reshape(-1, a.shape[2]) for a in stores]
            arrived[slot], *early = together(arrived[slot], *early)
            crossed = [move(a, core=1) for a in early[:2]]
        if slot < MICRO:
            given["last"] = last_micro
        if arrived[slot] is not None:
            given["next"] = arrived[slot]
        keeps = slot < slots - 1
        results = chain_step(
            slot, section_count - 1, at["section"], weights, fixed, given, stores, keeps
        )
        if not keeps:
            last_out, last_pre, last_in = results
            break
        passed, *stores = results
        route = [
            (s, s - 1)
            for s in range(1, section_count)
            if 0 <= slot - 2 * (section_count - 1 - s) < MICRO
        ]
        arrived.append(lax.ppermute(passed, "section", route) if route else None)

    out_rows, pre_rows = (
        jnp.concatenate([own, last, other, move(last, core=1)])
        for own, last, other in zip(early, (last_out, last_pre), crossed)
    )

    def term(second, distance, part=slice(None)):
        left, right = (hidden_columns, out_rows) if second else (normed_columns, pre_rows)
        return term_of(left, right, at, distance, part)

    def far(second):
        low, high = term(second, 2, LOW).astype(bf16), term(second, 2, HIGH).astype(bf16)
        return move(low, col=1), move(high, col=-1)

    def near(second, low, high):
        ahead, back = term(second, 1), term(second, 3)
        ahead = jnp.concatenate([ahead[LOW] + low.astype(f32), ahead[HIGH]])
        back = jnp.concatenate([back[LOW], back[HIGH] + high.astype(f32)])
        return move(ahead.astype(bf16), col=1), move(back.astype(bf16), col=-1)

    low2, high2, low1, high1 = together(*far(True), *far(False))
    ahead2, back2 = near(True, low2, high2)
    ahead2, back2, low1, high1 = together(ahead2, back2, low1, high1)
    ahead1, back1 = near(False, low1, high1)
    second_total = scatter_total(term(True, 0), ahead2, back2)
    second_got = scatter_planes(second_total, at)
    *second_got, ahead1, back1 = together(*second_got, ahead1, back1)
    first_total = scatter_total(term(False, 0), ahead1, back1)
    first_got = scatter_planes(first_total, at)
    second_sum = scatter_end(second_total, second_got, at)
    first_sum = scatter_end(first_total, first_got, at)
    in_grads = jnp.concatenate([early[2], last_in])
    return (in_grads[None], first_sum[None], second_sum[None])


def solution(mesh):
    return jax.shard_map(
        local,
        mesh=mesh,
        in_specs=(
            P("section", "replica", None),
            P("section", "replica", None),
            P("section", "replica", None),
            P(),
            P("replica", None),
            P("replica", None),
            P(),
        ),
        out_specs=(
            P("section", "replica", None),
            P("section", "replica", None),
            P("section", "replica", None),
        ),
        check_vma=False,
    )
```
